128 devices in a mesh: seq: 16 (over x_lo, z, core), fsdp: 8 (over y, x_hi).
Axes of the slice: x: 4 (x_hi: 2, x_lo: 2; x = x_hi * 2 + x_lo), y: 4, z: 4, core: 2. Of those that a mesh axis runs over, the one named last changes fastest.
Arguments:
- img_tokens: bfloat16 [4096, 3072], P('seq'), may hold values from -6 to 6
- txt_tokens: bfloat16 [512, 3072], P('seq'), may hold values from -6 to 6
- img_weight: bfloat16 [3072, 3, 2048], P('fsdp'), may hold values from -0.109375 to 0.109375
- txt_weight: bfloat16 [3072, 3, 2048], P('fsdp'), may hold values from -0.109375 to 0.109375
- img_modulation: bfloat16 [256, 6144], replicated, may hold values from -0.375 to 0.375
- txt_modulation: bfloat16 [256, 6144], replicated, may hold values from -0.375 to 0.375
- qk_gains: float32 [2, 2, 128], replicated, may hold values from 0.5 to 1.5
- timestep: int32 [1], replicated, may hold values from 0 to 999
- valid_text: int32 [1], replicated, may hold values from 256 to 512
- img_cotangent: bfloat16 [4096, 2048], P('seq', 'fsdp'), may hold values from -48 to 48
- txt_cotangent: bfloat16 [512, 2048], P('seq', 'fsdp'), may hold values from -48 to 48
Outputs:
- img_weight_grad: float32 [3072, 3, 2048], P('seq', None, 'fsdp')
- txt_weight_grad: float32 [3072, 3, 2048], P('seq', None, 'fsdp')
- img_input_grad: bfloat16 [4096, 3072], P('seq', 'fsdp')
- txt_input_grad: bfloat16 [512, 3072], P('seq', 'fsdp')
The draws below stay inside these ranges and needn't reach their ends.
All inputs are finite; a program needn't handle non-finite values.
Results may differ from the reference program's by a relative error of at most 0.03.
Values may be sent and summed in bfloat16 or wider, within the bound.
A program may use at most 128 MiB of HBM per device.

```python
import math
import jax
import jax.numpy as jnp
from jax import lax

D = 3072
HD = 128
FREQ = 256
HEADS = 16
TXT = 512
IMG_DEV = 256
IMG = 4096
TXT_DEV = 32
N_SEQ = 16
N_FSDP = 8


def levels(rng, extent, split, smallest, top_value):
    def one(position, parts):
        heights = jax.random.uniform(jax.random.fold_in(jax.random.fold_in(rng, 6), position), (parts,), jnp.float32, smallest / len(split), top_value / len(split))
        return jnp.repeat(jnp.exp(heights), extent[position] // parts).reshape((-1,) + (1,) * (len(extent) - position - 1))

    gain = one(*split[0])
    for cut in split[1:]:
        gain = gain * one(*cut)
    return gain


def bell_draw(stream_key, extent, width, limit, pieces=(), held_as=jnp.bfloat16):
    values = width * jax.random.normal(stream_key, extent, jnp.float32)
    if pieces:
        values = values * levels(stream_key, extent, pieces, -0.22, 0.18)
    return jnp.clip(values, -limit, limit).astype(held_as)


def setup_inputs(seed: int = 0) -> dict:
    key_of = jax.random.split(jax.random.key(seed), 12)
    return {
        "img_tokens": bell_draw(key_of[0], (IMG, D), 1.0, 6.0, ((0, 16),)),
        "txt_tokens": bell_draw(key_of[1], (TXT, D), 1.0, 6.0, ((0, 16),)),
        "img_weight": bell_draw(key_of[2], (D, 3, HEADS * HD), D ** -0.5, 0.109375, ((0, 8),)),
        "txt_weight": bell_draw(key_of[3], (D, 3, HEADS * HD), D ** -0.5, 0.109375, ((0, 8),)),
        "img_modulation": bell_draw(key_of[4], (FREQ, 2 * D), FREQ ** -0.5, 0.375),
        "txt_modulation": bell_draw(key_of[5], (FREQ, 2 * D), FREQ ** -0.5, 0.375),
        "qk_gains": jnp.clip(1.0 + 0.1 * jax.random.normal(key_of[6], (2, 2, HD), jnp.float32), 0.5, 1.5),
        "timestep": jax.random.randint(key_of[7], (1,), 0, 1000).astype(jnp.int32),
        "valid_text": jax.random.randint(key_of[8], (1,), TXT // 2, TXT + 1).astype(jnp.int32),
        "img_cotangent": bell_draw(key_of[9], (IMG, HEADS * HD), 8.0, 48.0, ((0, 16), (1, 8))),
        "txt_cotangent": bell_draw(key_of[10], (TXT, HEADS * HD), 8.0, 48.0, ((0, 16), (1, 8))),
    }


def time_features(timestep, freq_dim):
    half_freq = freq_dim // 2
    frequency = jnp.exp(-math.log(10000.0) * jnp.arange(half_freq, dtype=jnp.float32) / half_freq)
    angles = timestep.astype(jnp.float32)[:, None] * frequency[None, :]
    features = jnp.concatenate([jnp.cos(angles), jnp.sin(angles)], axis=1)
    return jax.nn.silu(features).astype(jnp.bfloat16)

def modulation(features, table, model_width):
    mixed = jnp.dot(features, table, preferred_element_type=jnp.float32)[0]
    return (mixed[:model_width], mixed[model_width:])

def prepare(tokens, shifts, scales):
    values = tokens.astype(jnp.float32)
    centred = values - lax.optimization_barrier(jnp.mean(values, axis=-1, keepdims=True))
    inv_std = lax.rsqrt(lax.optimization_barrier(jnp.mean(centred * centred, axis=-1, keepdims=True)) + 1e-06)
    normed = centred * inv_std
    hidden = (normed * (1.0 + scales) + shifts).astype(jnp.bfloat16)
    return (hidden, normed, inv_std)

def qk_norm(values, gains):
    return values * lax.rsqrt(lax.optimization_barrier(jnp.mean(values * values, axis=-1, keepdims=True)) + 1e-06) * gains

def norm_grads(q_pre, k_pre, gains, grad_q, grad_k):

    def normalize(query_pre, key_pre):
        return (qk_norm(query_pre, gains[0]), qk_norm(key_pre, gains[1]))
    outputs, pullback = jax.vjp(normalize, q_pre, k_pre)
    return pullback((grad_q, grad_k))

def input_grad(grad_hidden, scales, normed, inv_std):
    scaled = grad_hidden * (1.0 + scales)
    mean_grad = lax.optimization_barrier(jnp.mean(scaled, axis=-1, keepdims=True))
    mean_cross = lax.optimization_barrier(jnp.mean(scaled * normed, axis=-1, keepdims=True))
    return (inv_std * (scaled - mean_grad - normed * mean_cross)).astype(jnp.bfloat16)

def rounded(term):
    return lax.optimization_barrier(term.astype(jnp.bfloat16)).astype(jnp.float32)

def weight_grad(hidden, grad_qkv, per_device):
    hidden_groups = hidden.reshape(N_SEQ, per_device, D)
    grad_groups = grad_qkv.reshape(N_SEQ, per_device, 3 * HEADS * HD)

    def add_group(running, operand_pair):
        term = jnp.dot(operand_pair[0].T, operand_pair[1], preferred_element_type=jnp.float32)
        return (running + rounded(term), None)
    running, unused = lax.scan(add_group, jnp.zeros((D, 3 * HEADS * HD), jnp.float32), (hidden_groups, grad_groups))
    return running.reshape(D, 3, HEADS * HD)

def hidden_grad(grad_qkv, weight):
    group_cols = HEADS // N_FSDP * HD
    grad_groups = jnp.transpose(grad_qkv.reshape(-1, 3, N_FSDP, group_cols), (2, 0, 1, 3))
    weight_groups = jnp.transpose(weight.reshape(D, 3, N_FSDP, group_cols), (2, 0, 1, 3))

    def add_group(running, operand_pair):
        term = jnp.einsum('nkw,dkw->nd', operand_pair[0].astype(jnp.float32), operand_pair[1].astype(jnp.float32))
        return (running + rounded(term), None)
    start_value = jnp.zeros((grad_qkv.shape[0], D), jnp.float32)
    running, unused = lax.scan(add_group, start_value, (grad_groups, weight_groups))
    return running

def reference(img_tokens, txt_tokens, img_weight, txt_weight, img_modulation, txt_modulation, qk_gains, timestep, valid_text, img_cotangent, txt_cotangent):
    features = time_features(timestep, FREQ)
    streams = []
    for tokens, weight, table in ((txt_tokens, txt_weight, txt_modulation), (img_tokens, img_weight, img_modulation)):
        shifts, scales = modulation(features, table, D)
        hidden, normed, inv_std = prepare(tokens, shifts, scales)
        qkv = jnp.dot(hidden, weight.reshape(D, 3 * HEADS * HD), preferred_element_type=jnp.float32)
        streams.append((hidden, normed, inv_std, scales, qkv.reshape(-1, 3, HEADS, HD), weight))
    query = jnp.concatenate([qk_norm(streams[which][4][:, 0], qk_gains[which, 0]) for which in range(2)], 0).astype(jnp.bfloat16)
    key_all = jnp.concatenate([qk_norm(streams[which][4][:, 1], qk_gains[which, 1]) for which in range(2)], 0).astype(jnp.bfloat16)
    value_all = jnp.concatenate([streams[which][4][:, 2] for which in range(2)], 0).astype(jnp.bfloat16)
    grad_out = jnp.concatenate([txt_cotangent, img_cotangent], 0).reshape(-1, HEADS, HD)
    key_live = jnp.concatenate([(jnp.arange(TXT, dtype=jnp.int32) < valid_text[0]).astype(jnp.float32), jnp.ones((IMG,), jnp.float32)])
    score_scale = HD ** (-0.5)

    def head_pass(operands):
        query_head, key_head, value_head, grad_head = operands
        scores = jnp.dot(query_head, key_head.T, preferred_element_type=jnp.float32) * score_scale
        expo = jnp.exp(scores) * key_live[None, :]
        totals = lax.optimization_barrier(jnp.sum(expo, axis=-1))
        summed = jnp.dot(expo.astype(jnp.bfloat16), value_head, preferred_element_type=jnp.float32)
        attended = (summed / totals[:, None]).astype(jnp.bfloat16)
        deltas = lax.optimization_barrier(jnp.sum(grad_head.astype(jnp.float32) * attended.astype(jnp.float32), axis=-1))
        probs = expo / totals[:, None]
        grad_v = jnp.dot(probs.astype(jnp.bfloat16).T, grad_head, preferred_element_type=jnp.float32)
        grad_probs = jnp.dot(grad_head, value_head.T, preferred_element_type=jnp.float32)
        grad_scores = (probs * (grad_probs - deltas[:, None])).astype(jnp.bfloat16)
        grad_q = jnp.dot(grad_scores, key_head, preferred_element_type=jnp.float32) * score_scale
        grad_k = jnp.dot(grad_scores.T, query_head, preferred_element_type=jnp.float32) * score_scale
        return (grad_q, grad_k, grad_v)

    def heads_first(array):
        return jnp.transpose(array, (1, 0, 2))
    grad_q, grad_k, grad_v = lax.map(head_pass, (heads_first(query), heads_first(key_all), heads_first(value_all), heads_first(grad_out)))
    grad_q, grad_k, grad_v = (heads_first(grad_q), heads_first(grad_k), heads_first(grad_v))
    bounds = ((0, TXT, TXT_DEV), (TXT, TXT + IMG, IMG_DEV))
    results = []
    for which in range(2):
        hidden, normed, inv_std, scales, qkv, weight = streams[which]
        row_begin, row_end, per_device = bounds[which]
        grad_q_pre, grad_k_pre = norm_grads(qkv[:, 0], qkv[:, 1], qk_gains[which], grad_q[row_begin:row_end], grad_k[row_begin:row_end])
        grad_qkv = jnp.stack([grad_q_pre, grad_k_pre, grad_v[row_begin:row_end]], 1).astype(jnp.bfloat16)
        weight_sum = weight_grad(hidden, grad_qkv.reshape(-1, 3 * HEADS * HD), per_device)
        grad_hidden = hidden_grad(grad_qkv.reshape(-1, 3, HEADS * HD), weight)
        results.append((weight_sum, input_grad(grad_hidden, scales, normed, inv_std)))
    return (results[1][0], results[0][0], results[1][1], results[0][1])
```

```python
import functools
import math

import jax
import jax.numpy as jnp
from jax import lax
from jax.experimental import pallas as pl
from jax.experimental.pallas import tpu as pltpu
from jax.sharding import PartitionSpec as P

HD = 128
BF = jnp.bfloat16
F32 = jnp.float32
MESH = pl.DeviceIdType.MESH
SCALE = HD ** (-0.5)
EXP2 = SCALE / math.log(2.0)
EPS = 1e-06


def time_features(timestep, freq_dim):
    half_freq = freq_dim // 2
    frequency = jnp.exp(-math.log(10000.0) * jnp.arange(half_freq, dtype=jnp.float32) / half_freq)
    angles = timestep.astype(jnp.float32)[:, None] * frequency[None, :]
    features = jnp.concatenate([jnp.cos(angles), jnp.sin(angles)], axis=1)
    return jax.nn.silu(features).astype(jnp.bfloat16)


def dot(a, b):
    return jnp.dot(a, b, preferred_element_type=F32)


def dot_nt(a, b):
    return lax.dot_general(a, b, (((1,), (1,)), ((), ())), preferred_element_type=F32)


def dot_tn(a, b):
    return lax.dot_general(a, b, (((0,), (0,)), ((), ())), preferred_element_type=F32)


def norm_back(x, gain, grad):
    r = lax.rsqrt(jnp.mean(x * x, axis=-1, keepdims=True) + EPS)
    gd = gain * grad
    return r * gd - x * (r * r * r * jnp.mean(x * gd, axis=-1, keepdims=True))


def kernel(
    x_img, x_txt, w_img, w_txt, mod_img, mod_txt, feat, gains, live, cot_img, cot_txt,
    dw_img, dw_txt, dx_img, dx_txt,
    xi, xt, mods, mixed, sc, W, wt, hid, hidt, htg, nimg, ntxt, invi, invt,
    tps, tpr, qkvp, dO, qT, dOT, q2, dO2, kv, kvt, ets, dkvs, dkvr, dkvts, dkvtr,
    oT, tot, gq, gtf, gts, dws, dwr, pxs, pxr, phs, phr, s1v, s2v, sts, str_,
    thx, thr, tsts, tstr, wx, wxr, wxt, wxtr, wsum,
    lsem, wl_sem, wtl_sem, w_ss, w_rs, p_ss, p_rs, t_ss, t_rs, h_ss, h_rs,
    kv_ss, kv_rs, kt_ss, kt_rs, dk_ss, dk_rs, dt_ss, dt_rs, gf_ss, gf_rs, gs_ss, gs_rs,
    dw_ss, dw_rs, ph_ss, ph_rs, st_ss, st_rs, ts_ss, ts_rs,
):
    s = lax.axis_index("seq")
    f = lax.axis_index("fsdp")
    chip, c = s // 2, s % 2
    xlo, z = chip // 4, chip % 4
    y, xhi = f // 2, f % 2
    o = 1 - c

    def f_at(r, sign):
        return ((y + sign * (r % 4) + 4) % 4) * 2 + (xhi + r // 4) % 2

    def chip_at(r, sign):
        return ((xlo + r // 4) % 2) * 4 + (z + sign * (r % 4) + 4) % 4

    def fdev(r, sign):
        return (s, f_at(r, sign))

    def sdev(r, sign):
        return (chip_at(r, sign) * 2 + c, f)

    pdev = (chip * 2 + o, f)

    def remote(src, dst, ss, rs, dev):
        return pltpu.make_async_remote_copy(
            src_ref=src, dst_ref=dst, send_sem=ss, recv_sem=rs, device_id=dev, device_id_type=MESH
        )

    def loop(lo, hi, body):
        def step(i, carry):
            body(i)
            return carry

        lax.fori_loop(lo, hi, step, 0)

    def m128(v):
        return pl.multiple_of(v, 128)

    loc = [
        pltpu.make_async_copy(x_img, xi, lsem.at[0]),
        pltpu.make_async_copy(x_txt, xt, lsem.at[1]),
        pltpu.make_async_copy(mod_img, mods.at[1], lsem.at[2]),
        pltpu.make_async_copy(mod_txt, mods.at[0], lsem.at[3]),
        pltpu.make_async_copy(
            cot_img.at[:, pl.ds(m128(c * 128), 128)],
            dO.at[pl.ds(pl.multiple_of(128 + c * 256, 128), 256)], lsem.at[4]),
        pltpu.make_async_copy(
            cot_txt.at[:, pl.ds(m128(c * 128), 128)],
            dO.at[pl.ds(pl.multiple_of(c * 32, 32), 32)], lsem.at[5]),
    ]
    for cp in loc:
        cp.start()

    barrier = pltpu.get_barrier_semaphore()

    def hello(r):
        pl.semaphore_signal(barrier, inc=1, device_id=fdev(r, 1), device_id_type=MESH)
        pl.semaphore_signal(barrier, inc=1, device_id=sdev(r, 1), device_id_type=MESH)

    loop(1, 8, hello)
    pl.semaphore_signal(barrier, inc=1, device_id=pdev, device_id_type=MESH)

    def w_cols(ref, j, fp):
        return ref.at[j, :, pl.ds(m128((2 * fp + c) * 128), 128)]

    def wl_copy(j):
        return pltpu.make_async_copy(
            w_cols(w_img, j, f), W.at[0, :, pl.ds(j * 128, 128)], wl_sem.at[j])

    def wt_copy(r, j):
        return pltpu.make_async_copy(
            w_cols(w_txt, j, f_at(r, 1)), wt.at[r, :, pl.ds(j * 128, 128)], wtl_sem.at[r, j])

    for j in range(3):
        wl_copy(j).start()

    pl.semaphore_wait(barrier, 15)

    def w_copy(r, j):
        return remote(
            w_cols(w_img, j, f_at(r, 1)), W.at[r, :, pl.ds(j * 128, 128)],
            w_ss.at[r, j], w_rs.at[r, j], fdev(r, 1))

    def send_w(r):
        for j in range(3):
            w_copy(r, j).start()

    loop(1, 8, send_w)

    def start_wt(r):
        for j in range(3):
            wt_copy(r, j).start()

    loop(0, 8, start_wt)

    img_rows = pl.ds(pl.multiple_of(128 + c * 256, 128), 256)
    txt_rows = pl.ds(pl.multiple_of(c * 32, 32), 32)
    half_rows = pl.ds(pl.multiple_of(c * 256, 256), 256)
    cp_coti = remote(cot_img.at[:, pl.ds(m128(o * 128), 128)], dO.at[img_rows],
                     p_ss.at[0], p_rs.at[0], pdev)
    cp_cott = remote(cot_txt.at[:, pl.ds(m128(o * 128), 128)], dO.at[txt_rows],
                     p_ss.at[1], p_rs.at[1], pdev)
    cp_coti.start()
    cp_cott.start()

    for which in (0, 1):
        loc[3 - which].wait()
        mixed[which] = dot(feat[...], mods[which])[:8]
        for b in range(8):
            sc[which, b] = 1.0 + mixed[which, :, 3072 + b * 384:3072 + (b + 1) * 384]

    def prepare(which, src, nrm, inv, put):
        rows = 16

        def body(i):
            at = pl.multiple_of(i * rows, rows)
            v = src[pl.ds(at, rows), :].astype(F32)
            cen = v - jnp.mean(v, axis=-1, keepdims=True)
            iv = lax.rsqrt(jnp.mean(cen * cen, axis=-1, keepdims=True) + EPS)
            n = cen * iv
            inv[pl.ds(at, rows), :] = jnp.broadcast_to(iv, (rows, 128))
            h = (n * (1.0 + mixed[which, 0:1, 3072:]) + mixed[which, 0:1, :3072]).astype(BF)
            for b in range(8):
                nrm[b, pl.ds(at, rows), :] = n[:, b * 384:(b + 1) * 384]
                put(b, at, rows, h[:, b * 384:(b + 1) * 384])

        loop(0, src.shape[0] // rows, body)

    def put_txt(b, at, rows, h):
        hidt[b, pl.ds(pl.multiple_of(c * 32 + at, 16), rows), :] = h

    def put_img(b, at, rows, h):
        hid[b, pl.ds(pl.multiple_of(c * 256 + at, 16), rows), :] = h

    loc[1].wait()
    prepare(0, xt, ntxt, invt, put_txt)
    cp_ht = remote(hidt.at[:, txt_rows], hidt.at[:, txt_rows], p_ss.at[2], p_rs.at[2], pdev)
    cp_ht.start()
    loc[0].wait()
    prepare(1, xi, nimg, invi, put_img)
    cp_hi = remote(hid.at[:, half_rows], hid.at[:, half_rows], p_ss.at[3], p_rs.at[3], pdev)
    cp_hi.start()

    cp_ht.wait_recv()

    def t_copy(r):
        return remote(tps.at[r], tpr.at[r], t_ss.at[r], t_rs.at[r], fdev(r, 1))

    def h_copy(r):
        return remote(hidt.at[chip_at(r, 1)], htg.at[r], h_ss.at[r], h_rs.at[r], sdev(r, 1))

    def txt_partial(i):
        r = (i + 1) % 8
        for j in range(3):
            wt_copy(r, j).wait()
        tps[r] = dot(hidt[f], wt[r]).astype(BF)

        @pl.when(r != 0)
        def _():
            t_copy(r).start()

    loop(0, 8, txt_partial)
    htg[0] = hidt[chip]
    loop(1, 8, lambda r: h_copy(r).start())

    loc[4].wait()
    loc[5].wait()
    cp_coti.wait_recv()
    cp_cott.wait_recv()
    dO[64:128, :] = jnp.zeros((64, 128), BF)
    dOT[...] = dO[...].astype(F32).T.astype(BF)

    cp_hi.wait_recv()
    for j in range(3):
        wl_copy(j).wait()
    qkvp[128:, :] = dot(hid[f], W[0])

    def img_proj(r):
        for j in range(3):
            w_copy(r, j).wait_recv()
        qkvp[128:, :] += dot(hid[f_at(r, -1)], W[r])

    loop(1, 8, img_proj)

    qkvp[0:64, :] = tps[0].astype(F32)
    qkvp[64:128, :] = jnp.zeros((64, 384), F32)

    def txt_add(r):
        t_copy(r).wait_recv()
        qkvp[0:64, :] += tpr[r].astype(F32)

    loop(1, 8, txt_add)

    def normed_heads(lo, hi, g0):
        a = qkvp[lo:hi, 0:128]
        b = qkvp[lo:hi, 128:256]
        qn = a * lax.rsqrt(jnp.mean(a * a, axis=-1, keepdims=True) + EPS) * gains[g0:g0 + 1, :]
        kn = b * lax.rsqrt(jnp.mean(b * b, axis=-1, keepdims=True) + EPS) * gains[g0 + 1:g0 + 2, :]
        qT[:, lo:hi] = qn.T.astype(BF)
        return kn.astype(BF)

    kv[0, :, 0:128] = normed_heads(128, 640, 2)
    kv[0, :, 128:256] = qkvp[128:, 256:384].astype(BF)

    def kv_copy(r):
        return remote(kv.at[0], kv.at[r], kv_ss.at[r], kv_rs.at[r], sdev(r, 1))

    def kt_copy(r):
        return remote(kvt.at[0], kvt.at[r], kt_ss.at[r], kt_rs.at[r], sdev(r, 1))

    loop(1, 8, lambda r: kv_copy(r).start())
    kt = normed_heads(0, 128, 0)
    kvt[0, :, 0:128] = kt[0:64]
    kvt[0, :, 128:256] = qkvp[0:64, 256:384].astype(BF)
    loop(1, 8, lambda r: kt_copy(r).start())

    oT[...] = jnp.zeros_like(oT)
    tot[...] = jnp.zeros_like(tot)

    def forward(r):
        @pl.when(r != 0)
        def _():
            kv_copy(r).wait_recv()

        e = jnp.exp2(dot(kv[r, :, 0:128], qT[...]) * EXP2)
        tot[0:1, :] += jnp.sum(e, axis=0, keepdims=True)
        eb = e.astype(BF)
        ets[r] = eb
        oT[...] += dot_tn(kv[r, :, 128:256], eb)

    loop(0, 8, forward)
    loop(1, 8, lambda r: kt_copy(r).wait_recv())

    def forward_text(r):
        rows = pl.ds(pl.multiple_of(r * 64, 64), 64)
        e = jnp.exp2(dot(kvt[r, :, 0:128], qT[...]) * EXP2)
        e = e * live[pl.ds(pl.multiple_of(chip_at(r, -1) * 64, 64), 64), 0:1]
        tot[0:1, :] += jnp.sum(e, axis=0, keepdims=True)
        ets[8, rows, :] = e.astype(BF)

    loop(0, 8, forward_text)
    vt = kvt[:, :, 128:256].reshape(512, 128)
    kt_all = kvt[:, :, 0:128].reshape(512, 128)
    oT[...] += dot_tn(vt, ets[8])

    rcp = 1.0 / tot[0:1, :]
    att = (oT[...] * rcp).astype(BF).astype(F32)
    dOTf = dOT[...].astype(F32)
    delta = jnp.sum(dOTf * att, axis=0, keepdims=True)
    tot[0:1, :] = rcp
    tot[1:2, :] = delta
    q2[...] = (qT[...].astype(F32) * rcp).T.astype(BF)
    dO2[...] = (dOTf * rcp).T.astype(BF)
    oT[...] = jnp.zeros_like(oT)

    def back(k, v, eb):
        dp = dot(v, dOT[...])
        ds = (eb.astype(F32) * (dp - tot[1:2, :])).astype(BF)
        oT[...] += dot_tn(k, ds)
        return (dot(ds, q2[...]) * SCALE).astype(BF), dot(eb, dO2[...]).astype(BF)

    def dk_copy(r):
        return remote(dkvs.at[r], dkvr.at[r], dk_ss.at[r], dk_rs.at[r], sdev(r, -1))

    def dt_copy(r):
        return remote(dkvts.at[r], dkvtr.at[r], dt_ss.at[r], dt_rs.at[r], sdev(r, -1))

    def backward(i):
        r = (i + 1) % 8
        gk, gv = back(kv[r, :, 0:128], kv[r, :, 128:256], ets[r])
        dkvs[r, :, 0:128] = gk
        dkvs[r, :, 128:256] = gv

        @pl.when(r != 0)
        def _():
            dk_copy(r).start()

    loop(0, 7, backward)
    gk, gv = back(kt_all, vt, ets[8])
    dkvts[:, :, 0:128] = gk.reshape(8, 64, 128)
    dkvts[:, :, 128:256] = gv.reshape(8, 64, 128)
    loop(1, 8, lambda r: dt_copy(r).start())
    backward(7)

    dq = (oT[...] * (tot[0:1, :] * SCALE)).T
    gq[128:, 0:128] = norm_back(qkvp[128:, 0:128], gains[2:3, :], dq[128:]).astype(BF)
    gq[0:64, 0:128] = norm_back(qkvp[0:64, 0:128], gains[0:1, :], dq[0:64]).astype(BF)

    wsum[0:64, 0:256] = dkvts[0].astype(F32)

    def add_t(r):
        dt_copy(r).wait_recv()
        wsum[0:64, 0:256] += dkvtr[r].astype(F32)

    loop(1, 8, add_t)
    gq[0:64, 128:256] = norm_back(
        qkvp[0:64, 128:256], gains[1:2, :], wsum[0:64, 0:128]).astype(BF)
    gq[0:64, 256:384] = wsum[0:64, 128:256].astype(BF)

    def gf_copy(r):
        return remote(gtf.at[0], gtf.at[r], gf_ss.at[r], gf_rs.at[r], fdev(r, 1))

    def gs_copy(r):
        return remote(gts.at[0], gts.at[r], gs_ss.at[r], gs_rs.at[r], sdev(r, 1))

    gtf[0] = gq[0:64, :]
    gts[0] = gq[0:64, :]
    loop(1, 8, lambda r: gf_copy(r).start())
    loop(1, 8, lambda r: gs_copy(r).start())

    wsum[:, 0:256] = dkvs[0].astype(F32)

    def add_k(r):
        dk_copy(r).wait_recv()
        wsum[:, 0:256] += dkvr[r].astype(F32)

    loop(1, 8, add_k)
    gq[128:, 128:256] = norm_back(
        qkvp[128:, 128:256], gains[3:4, :], wsum[:, 0:128]).astype(BF)
    gq[128:, 256:384] = wsum[:, 128:256].astype(BF)

    other_rows = pl.ds(pl.multiple_of(128 + o * 256, 128), 256)

    def px_copy(r):
        return remote(pxs.at[r], pxr.at[r], ph_ss.at[0, r], ph_rs.at[0, r], pdev)

    def partner_part(r):
        pxs[r] = dot_nt(gq[other_rows, :], W[r]).astype(BF)
        px_copy(r).start()

    loop(0, 8, partner_part)

    def dw_copy(r):
        return remote(dws.at[r], dwr.at[r], dw_ss.at[r], dw_rs.at[r], sdev(r, 1))

    def weight_part(i):
        r = (i + 1) % 8
        dws[r] = dot_tn(hid[chip_at(r, 1)], gq[128:, :]).astype(BF)

        @pl.when(r != 0)
        def _():
            dw_copy(r).start()

    def ph_copy(r):
        return remote(phs.at[r], phr.at[r], ph_ss.at[1, r], ph_rs.at[1, r], fdev(r, -1))

    s1v[...] = jnp.zeros_like(s1v)
    s2v[...] = jnp.zeros_like(s2v)

    def hidden_part(i):
        r = (i + 1) % 8
        b = f_at(r, -1)
        px_copy(r).wait_recv()
        p = (dot_nt(gq[img_rows, :], W[r]) + pxr[r].astype(F32)).astype(BF)
        phs[r] = p

        @pl.when(r != 0)
        def _():
            ph_copy(r).start()

        t = p.astype(F32) * sc[1, b, 0:1, :]
        u = t * nimg[b]
        s1v[...] += t[:, 0:128] + t[:, 128:256] + t[:, 256:384]
        s2v[...] += u[:, 0:128] + u[:, 128:256] + u[:, 256:384]

    def both(i):
        weight_part(i)
        hidden_part(i)

    loop(0, 8, both)

    lane = lax.broadcasted_iota(jnp.int32, (256, 128), 1)
    s1 = jnp.sum(s1v[...], axis=-1, keepdims=True)
    s2 = jnp.sum(s2v[...], axis=-1, keepdims=True)
    sts[...] = jnp.where(lane == 0, s1, s2).T[0:8]

    def st_copy(r):
        return remote(sts, str_.at[r], st_ss.at[r], st_rs.at[r], fdev(r, 1))

    loop(1, 8, lambda r: st_copy(r).start())

    thx[...] = jnp.zeros_like(thx)

    def txt_hidden(r):
        @pl.when(r != 0)
        def _():
            gf_copy(r).wait_recv()

        thx[...] += dot_nt(gtf[r], wt[(r // 4) * 4 + (4 - r % 4) % 4])

    loop(0, 8, txt_hidden)
    their = pl.ds(pl.multiple_of(o * 32, 32), 32)
    cp_th = remote(thx.at[their], thr, p_ss.at[4], p_rs.at[4], pdev)
    cp_th.start()

    loop(1, 8, lambda r: gs_copy(r).wait_recv())
    loop(1, 8, lambda r: h_copy(r).wait_recv())
    wxt[...] = dot_tn(htg[...].reshape(512, 384), gts[...].reshape(512, 384))
    mine = pl.ds(pl.multiple_of(c * 192, 64), 192)
    theirs = pl.ds(pl.multiple_of(o * 192, 64), 192)
    cp_wt = remote(wxt.at[theirs], wxtr, p_ss.at[5], p_rs.at[5], pdev)
    cp_wt.start()

    cp_th.wait_recv()
    gh = thx[txt_rows, :] + thr[...]
    tsc = gh * sc[0, f, 0:1, :]
    tn = ntxt[f]
    t1 = jnp.sum(tsc, axis=-1, keepdims=True)
    t2 = jnp.sum(tsc * tn, axis=-1, keepdims=True)
    lane_t = lax.broadcasted_iota(jnp.int32, (32, 128), 1)
    tsts[...] = jnp.where(lane_t == 0, t1, t2)

    def ts_copy(r):
        return remote(tsts, tstr.at[r], ts_ss.at[r], ts_rs.at[r], fdev(r, 1))

    loop(1, 8, lambda r: ts_copy(r).start())
    thr[...] = tsc

    def place(out, part, head):
        for j in range(3):
            out[j, :, pl.ds(m128(head * 128), 128)] = part[:, j * 128:(j + 1) * 128]

    cp_wt.wait_recv()
    place(dw_txt, wxt[mine, :], c)
    place(dw_txt, wxtr[...], o)

    st = sts[...]
    for r in range(1, 8):
        st_copy(r).wait_recv()
        st = st + str_[r]
    stT = jnp.concatenate([st, jnp.zeros((120, 256), F32)], axis=0).T
    acc = phs[0].astype(F32)
    for r in range(1, 8):
        ph_copy(r).wait_recv()
        acc = acc + phr[r].astype(F32)
    scaled = acc * sc[1, f, 0:1, :]
    dx_img[...] = (invi[:, 0:1] * (
        scaled - stT[:, 0:1] * (1.0 / 3072) - nimg[f] * (stT[:, 1:2] * (1.0 / 3072))
    )).astype(BF)

    tt = tsts[...]
    for r in range(1, 8):
        ts_copy(r).wait_recv()
        tt = tt + tstr[r]
    dx_txt[...] = (invt[:, 0:1] * (
        thr[...] - tt[:, 0:1] * (1.0 / 3072) - ntxt[f] * (tt[:, 1:2] * (1.0 / 3072))
    )).astype(BF)

    wx[...] = dws[0].astype(F32)

    def add_w(r):
        dw_copy(r).wait_recv()
        wx[...] += dwr[r].astype(F32)

    loop(1, 8, add_w)
    cp_wi = remote(wx.at[theirs], wxr, p_ss.at[6], p_rs.at[6], pdev)
    cp_wi.start()
    place(dw_img, wx[mine, :], c)
    cp_wi.wait_recv()
    place(dw_img, wxr[...], o)

    def drain(r):
        for j in range(3):
            w_copy(r, j).wait_send()
        for cp in (t_copy, h_copy, kv_copy, kt_copy, dk_copy, dt_copy, gf_copy, gs_copy,
                   dw_copy, ph_copy, st_copy, ts_copy):
            cp(r).wait_send()

    loop(1, 8, drain)
    loop(0, 8, lambda r: px_copy(r).wait_send())
    for cp in (cp_coti, cp_cott, cp_ht, cp_hi, cp_th, cp_wt, cp_wi):
        cp.wait_send()


def scratch():
    V = pltpu.VMEM
    return [
        V((256, 3072), BF), V((32, 3072), BF), V((2, 256, 6144), BF), V((2, 8, 6144), F32),
        V((2, 8, 8, 384), F32), V((8, 384, 384), BF), V((8, 384, 384), BF),
        V((8, 512, 384), BF), V((8, 64, 384), BF), V((8, 64, 384), BF),
        V((8, 256, 384), F32), V((8, 32, 384), F32), V((256, 128), F32), V((32, 128), F32),
        V((8, 64, 384), BF), V((8, 64, 384), BF), V((640, 384), F32), V((640, 128), BF),
        V((128, 640), BF), V((128, 640), BF), V((640, 128), BF), V((640, 128), BF),
        V((8, 512, 256), BF), V((8, 64, 256), BF), V((9, 512, 640), BF),
        V((8, 512, 256), BF), V((8, 512, 256), BF), V((8, 64, 256), BF), V((8, 64, 256), BF),
        V((128, 640), F32), V((8, 640), F32), V((640, 384), BF),
        V((8, 64, 384), BF), V((8, 64, 384), BF), V((8, 384, 384), BF), V((8, 384, 384), BF),
        V((8, 256, 384), BF), V((8, 256, 384), BF), V((8, 256, 384), BF), V((8, 256, 384), BF),
        V((256, 128), F32), V((256, 128), F32), V((8, 256), F32), V((8, 8, 256), F32),
        V((64, 384), F32), V((32, 384), F32), V((32, 128), F32), V((8, 32, 128), F32),
        V((384, 384), F32), V((192, 384), F32), V((384, 384), F32), V((192, 384), F32),
        V((512, 256), F32),
    ] + [
        pltpu.SemaphoreType.DMA(shape)
        for shape in (
            [(6,), (3,), (8, 3), (8, 3), (8, 3), (7,), (7,)] + [(8,)] * 18 + [(2, 8)] * 2
            + [(8,)] * 4
        )
    ]


def on_device(
    img_tokens, txt_tokens, img_weight, txt_weight, img_modulation, txt_modulation, qk_gains,
    timestep, valid_text, img_cotangent, txt_cotangent,
):
    features = time_features(timestep, img_modulation.shape[0])
    feat = jnp.broadcast_to(features, (16, features.shape[1]))
    gains = jnp.concatenate([qk_gains.reshape(4, HD), jnp.zeros((4, HD), F32)], 0)
    live = jnp.broadcast_to(
        (jnp.arange(512, dtype=jnp.int32) < valid_text[0]).astype(F32)[:, None], (512, 128))
    anys = pl.BlockSpec(memory_space=pl.ANY)
    vm = pl.BlockSpec(memory_space=pltpu.VMEM)
    dw_img, dw_txt, dx_img, dx_txt = pl.pallas_call(
        kernel,
        out_shape=(
            jax.ShapeDtypeStruct((3, 192, 256), F32),
            jax.ShapeDtypeStruct((3, 192, 256), F32),
            jax.ShapeDtypeStruct((256, 384), BF),
            jax.ShapeDtypeStruct((32, 384), BF),
        ),
        in_specs=[anys] * 6 + [vm] * 3 + [anys] * 2,
        out_specs=[vm] * 4,
        scratch_shapes=scratch(),
        compiler_params=pltpu.CompilerParams(
            collective_id=0, has_side_effects=True, vmem_limit_bytes=62 * 2 ** 20),
        name="joint_block",
    )(
        img_tokens, txt_tokens, jnp.transpose(img_weight, (1, 0, 2)),
        jnp.transpose(txt_weight, (1, 0, 2)), img_modulation, txt_modulation, feat, gains, live,
        img_cotangent, txt_cotangent,
    )
    return (
        jnp.transpose(dw_img, (1, 0, 2)), jnp.transpose(dw_txt, (1, 0, 2)), dx_img, dx_txt
    )


def solution(mesh):
    return jax.shard_map(
        on_device,
        mesh=mesh,
        in_specs=(
            P("seq", None),
            P("seq", None),
            P("fsdp", None, None),
            P("fsdp", None, None),
            P(),
            P(),
            P(),
            P(),
            P(),
            P("seq", "fsdp"),
            P("seq", "fsdp"),
        ),
        out_specs=(
            P("seq", None, "fsdp"),
            P("seq", None, "fsdp"),
            P("seq", "fsdp"),
            P("seq", "fsdp"),
        ),
        check_vma=False,
    )
```

```python
import functools
import math

import jax
import jax.numpy as jnp
from jax import lax
from jax.experimental import pallas as pl
from jax.experimental.pallas import tpu as pltpu
from jax.sharding import PartitionSpec as P

HD = 128
BF = jnp.bfloat16
F32 = jnp.float32
MESH = pl.DeviceIdType.MESH
SCALE = HD ** (-0.5)
EXP2 = SCALE / math.log(2.0)
EPS = 1e-06


def time_features(timestep, freq_dim):
    half_freq = freq_dim // 2
    frequency = jnp.exp(-math.log(10000.0) * jnp.arange(half_freq, dtype=jnp.float32) / half_freq)
    angles = timestep.astype(jnp.float32)[:, None] * frequency[None, :]
    features = jnp.concatenate([jnp.cos(angles), jnp.sin(angles)], axis=1)
    return jax.nn.silu(features).astype(jnp.bfloat16)


def dot(a, b):
    return jnp.dot(a, b, preferred_element_type=F32)


def dot_nt(a, b):
    return lax.dot_general(a, b, (((1,), (1,)), ((), ())), preferred_element_type=F32)


def dot_tn(a, b):
    return lax.dot_general(a, b, (((0,), (0,)), ((), ())), preferred_element_type=F32)


def norm_back(x, gain, grad):
    r = lax.rsqrt(jnp.mean(x * x, axis=-1, keepdims=True) + EPS)
    gd = gain * grad
    return r * gd - x * (r * r * r * jnp.mean(x * gd, axis=-1, keepdims=True))


def kernel(
    x_img, x_txt, w_img, w_txt, mod_img, mod_txt, feat, gains, valid, cot_img, cot_txt,
    dw_img, dw_txt, dx_img, dx_txt,
    xi, xt, mods, mixed, sc, W, wt, hid, hidt, htg, nimg, ntxt, invi, invt,
    tps, tpr, qkvp, dO, qr, qT, dOT, q2, dO2, kv, kvt, ets, etx, dkvs, dkvr, dkvts, dkvtr,
    oT, stx, stxr, dqf, dqr, gq, gtf, gts, dws, dwr, pxs, pxr, phs, phr, s1v, s2v, sts, str_,
    thx, thr, tsts, tstr, wx, wxr, wxt, wxtr, wsum, wcs, wcr,
    lsem, wl_sem, wtl_sem, w_ss, w_rs, p_ss, p_rs, x_ss, x_rs, t_ss, t_rs, h_ss, h_rs,
    kv_ss, kv_rs, kt_ss, kt_rs, dk_ss, dk_rs, dt_ss, dt_rs, gf_ss, gf_rs, gs_ss, gs_rs,
    dq_ss, dq_rs, dw_ss, dw_rs, ph_ss, ph_rs, st_ss, st_rs, ts_ss, ts_rs,
):
    s = lax.axis_index("seq")
    f = lax.axis_index("fsdp")
    chip, c = s // 2, s % 2
    xlo, z = chip // 4, chip % 4
    y, xhi = f // 2, f % 2
    o = 1 - c

    def f_at(r, sign):
        return ((y + sign * (r % 4) + 4) % 4) * 2 + (xhi + r // 4) % 2

    def chip_at(r, sign):
        return ((xlo + r // 4) % 2) * 4 + (z + sign * (r % 4) + 4) % 4

    def fdev(r, sign):
        return (s, f_at(r, sign))

    def sdev(r, sign):
        return (chip_at(r, sign) * 2 + c, f)

    pdev = (chip * 2 + o, f)
    xdev = sdev(4, 1)
    xo = 1 - xlo

    def remote(src, dst, ss, rs, dev):
        return pltpu.make_async_remote_copy(
            src_ref=src, dst_ref=dst, send_sem=ss, recv_sem=rs, device_id=dev, device_id_type=MESH
        )

    def loop(lo, hi, body):
        def step(i, carry):
            body(i)
            return carry

        lax.fori_loop(lo, hi, step, 0)

    def m128(v):
        return pl.multiple_of(v, 128)

    loc = [
        pltpu.make_async_copy(x_img, xi, lsem.at[0]),
        pltpu.make_async_copy(x_txt, xt, lsem.at[1]),
        pltpu.make_async_copy(mod_img, mods.at[1], lsem.at[2]),
        pltpu.make_async_copy(mod_txt, mods.at[0], lsem.at[3]),
        pltpu.make_async_copy(
            cot_img.at[:, pl.ds(m128(c * 128), 128)],
            dO.at[pl.ds(pl.multiple_of(128 + xlo * 512 + c * 256, 128), 256)], lsem.at[4]),
        pltpu.make_async_copy(
            cot_txt.at[:, pl.ds(m128(c * 128), 128)],
            dO.at[pl.ds(pl.multiple_of(xlo * 64 + c * 32, 32), 32)], lsem.at[5]),
    ]
    for cp in loc:
        cp.start()

    barrier = pltpu.get_barrier_semaphore()

    def hello(r):
        pl.semaphore_signal(barrier, inc=1, device_id=fdev(r, 1), device_id_type=MESH)
        pl.semaphore_signal(barrier, inc=1, device_id=sdev(r, 1), device_id_type=MESH)

    loop(1, 8, hello)
    pl.semaphore_signal(barrier, inc=1, device_id=pdev, device_id_type=MESH)

    def w_cols(ref, j, fp):
        return ref.at[j, :, pl.ds(m128((2 * fp + c) * 128), 128)]

    def wl_copy(j):
        return pltpu.make_async_copy(
            w_cols(w_img, j, f), W.at[0, :, pl.ds(j * 128, 128)], wl_sem.at[j])

    def wt_copy(r, j):
        return pltpu.make_async_copy(
            w_cols(w_txt, j, f_at(r, 1)), wt.at[r, :, pl.ds(j * 128, 128)], wtl_sem.at[r, j])

    for j in range(3):
        wl_copy(j).start()

    pl.semaphore_wait(barrier, 15)

    def w_copy(r, j):
        return remote(
            w_cols(w_img, j, f_at(r, 1)), W.at[r, :, pl.ds(j * 128, 128)],
            w_ss.at[r, j], w_rs.at[r, j], fdev(r, 1))

    def send_w(r):
        for j in range(3):
            w_copy(r, j).start()

    loop(1, 8, send_w)

    def start_wt(r):
        for j in range(3):
            wt_copy(r, j).start()

    loop(0, 8, start_wt)

    img_rows = pl.ds(pl.multiple_of(128 + c * 256, 128), 256)
    txt_rows = pl.ds(pl.multiple_of(c * 32, 32), 32)
    half_rows = pl.ds(pl.multiple_of(c * 256, 256), 256)
    cp_coti = remote(cot_img.at[:, pl.ds(m128(o * 128), 128)],
                     dO.at[pl.ds(pl.multiple_of(128 + xlo * 512 + c * 256, 128), 256)],
                     p_ss.at[0], p_rs.at[0], pdev)
    cp_cott = remote(cot_txt.at[:, pl.ds(m128(o * 128), 128)],
                     dO.at[pl.ds(pl.multiple_of(xlo * 64 + c * 32, 32), 32)],
                     p_ss.at[1], p_rs.at[1], pdev)
    cp_coti.start()
    cp_cott.start()

    for which in (0, 1):
        loc[3 - which].wait()
        row = jnp.broadcast_to(feat[...].astype(F32), (16, 256)).astype(BF)
        mixed[which] = dot(row, mods[which])[:8]
        for b in range(8):
            sc[which, b] = 1.0 + mixed[which, :, 3072 + b * 384:3072 + (b + 1) * 384]

    def prepare(which, src, nrm, inv, put):
        rows = 16

        def body(i):
            at = pl.multiple_of(i * rows, rows)
            v = src[pl.ds(at, rows), :].astype(F32)
            cen = v - jnp.mean(v, axis=-1, keepdims=True)
            iv = lax.rsqrt(jnp.mean(cen * cen, axis=-1, keepdims=True) + EPS)
            n = cen * iv
            inv[pl.ds(at, rows), :] = jnp.broadcast_to(iv, (rows, 128))
            h = (n * (1.0 + mixed[which, 0:1, 3072:]) + mixed[which, 0:1, :3072]).astype(BF)
            for b in range(8):
                nrm[b, pl.ds(at, rows), :] = n[:, b * 384:(b + 1) * 384]
                put(b, at, rows, h[:, b * 384:(b + 1) * 384])

        loop(0, src.shape[0] // rows, body)

    def put_txt(b, at, rows, h):
        hidt[b, pl.ds(pl.multiple_of(c * 32 + at, 16), rows), :] = h

    def put_img(b, at, rows, h):
        hid[b, pl.ds(pl.multiple_of(c * 256 + at, 16), rows), :] = h

    loc[1].wait()
    prepare(0, xt, ntxt, invt, put_txt)
    cp_ht = remote(hidt.at[:, txt_rows], hidt.at[:, txt_rows], p_ss.at[2], p_rs.at[2], pdev)
    cp_ht.start()
    loc[0].wait()
    prepare(1, xi, nimg, invi, put_img)
    cp_hi = remote(hid.at[:, half_rows], hid.at[:, half_rows], p_ss.at[3], p_rs.at[3], pdev)
    cp_hi.start()

    cp_ht.wait_recv()

    def t_copy(r):
        return remote(tps.at[r], tpr.at[r], t_ss.at[r], t_rs.at[r], fdev(r, 1))

    def h_copy(r):
        return remote(hidt.at[chip_at(r, 1)], htg.at[r], h_ss.at[r], h_rs.at[r], sdev(r, 1))

    def txt_partial(i):
        r = (i + 1) % 8
        for j in range(3):
            wt_copy(r, j).wait()
        tps[r] = dot(hidt[f], wt[r]).astype(BF)

        @pl.when(r != 0)
        def _():
            t_copy(r).start()

    loop(0, 8, txt_partial)
    htg[0] = hidt[chip]
    loop(1, 8, lambda r: h_copy(r).start())

    own_t = pl.ds(pl.multiple_of(xlo * 64, 64), 64)
    own_i = pl.ds(pl.multiple_of(128 + xlo * 512, 128), 512)
    loc[4].wait()
    loc[5].wait()
    cp_coti.wait_recv()
    cp_cott.wait_recv()
    cp_xot = remote(dO.at[own_t], dO.at[own_t], x_ss.at[0], x_rs.at[0], xdev)
    cp_xoi = remote(dO.at[own_i], dO.at[own_i], x_ss.at[1], x_rs.at[1], xdev)
    cp_xot.start()
    cp_xoi.start()

    cp_hi.wait_recv()
    for j in range(3):
        wl_copy(j).wait()
    qkvp[128:, :] = dot(hid[f], W[0])

    def img_proj(r):
        for j in range(3):
            w_copy(r, j).wait_recv()
        qkvp[128:, :] += dot(hid[f_at(r, -1)], W[r])

    loop(1, 8, img_proj)

    qkvp[0:64, :] = tps[0].astype(F32)
    qkvp[64:128, :] = jnp.zeros((64, 384), F32)

    def txt_add(r):
        t_copy(r).wait_recv()
        qkvp[0:64, :] += tpr[r].astype(F32)

    loop(1, 8, txt_add)

    def normed_head(lo, hi, col, g):
        a = qkvp[lo:hi, col:col + 128]
        return (a * lax.rsqrt(jnp.mean(a * a, axis=-1, keepdims=True) + EPS)
                * gains[g:g + 1, :]).astype(BF)

    def kv_copy(r):
        return remote(kv.at[0], kv.at[r], kv_ss.at[r], kv_rs.at[r], sdev(r, 1))

    def kt_copy(r):
        return remote(kvt.at[0], kvt.at[r], kt_ss.at[r], kt_rs.at[r], sdev(r, 1))

    kv[0, :, 0:128] = normed_head(128, 640, 128, 3)
    kv[0, :, 128:256] = qkvp[128:, 256:384].astype(BF)
    loop(1, 4, lambda r: kv_copy(r).start())
    kvt[0, :, 0:128] = normed_head(0, 64, 128, 1)
    kvt[0, :, 128:256] = qkvp[0:64, 256:384].astype(BF)
    loop(1, 4, lambda r: kt_copy(r).start())
    qr[own_i, :] = normed_head(128, 640, 0, 2)
    qr[own_t, :] = normed_head(0, 64, 0, 0)
    cp_xqt = remote(qr.at[own_t], qr.at[own_t], x_ss.at[2], x_rs.at[2], xdev)
    cp_xqi = remote(qr.at[own_i], qr.at[own_i], x_ss.at[3], x_rs.at[3], xdev)
    cp_xqi.start()
    cp_xqt.start()
    cp_xot.wait_recv()
    cp_xoi.wait_recv()
    dOT[...] = dO[...].astype(F32).T.astype(BF)
    cp_xqi.wait_recv()
    cp_xqt.wait_recv()
    qT[...] = qr[...].astype(F32).T.astype(BF)

    oT[...] = jnp.zeros_like(oT)
    stx[...] = jnp.zeros_like(stx)

    def half_of(i):
        return pl.ds(pl.multiple_of((i % 2) * 256, 256), 256)

    def forward(i):
        r = i // 2

        @pl.when((i % 2 == 0) & (r != 0))
        def _():
            kv_copy(r).wait_recv()

        e = jnp.exp2(dot(kv[r, half_of(i), 0:128], qT[...]) * EXP2)
        stx[0:1, :] += jnp.sum(e, axis=0, keepdims=True)
        eb = e.astype(BF)
        ets[i] = eb
        oT[...] += dot_tn(kv[r, half_of(i), 128:256], eb)

    loop(0, 8, forward)
    loop(1, 4, lambda r: kt_copy(r).wait_recv())

    def forward_text(r):
        e = jnp.exp2(dot(kvt[r, :, 0:128], qT[...]) * EXP2)
        index = chip_at(r, -1) * 64 + lax.broadcasted_iota(jnp.int32, (64, 1152), 0)
        e = jnp.where(index < valid[0], e, 0.0)
        stx[0:1, :] += jnp.sum(e, axis=0, keepdims=True)
        etx[pl.ds(pl.multiple_of(r * 64, 64), 64), :] = e.astype(BF)

    loop(0, 4, forward_text)
    vt = kvt[:, :, 128:256].reshape(256, 128)
    kt_all = kvt[:, :, 0:128].reshape(256, 128)
    oT[...] += dot_tn(vt, etx[...])

    stx[1:2, :] = jnp.sum(dOT[...].astype(F32) * oT[...], axis=0, keepdims=True)
    cp_st = remote(stx, stxr, x_ss.at[4], x_rs.at[4], xdev)
    cp_st.start()
    oT[...] = jnp.zeros_like(oT)
    cp_st.wait_recv()
    rcp = 1.0 / (stx[0:1, :] + stxr[0:1, :])
    delta = (stx[1:2, :] + stxr[1:2, :]) * rcp
    stxr[2:3, :] = rcp
    stxr[3:4, :] = delta
    q2[...] = (qT[...].astype(F32) * rcp).T.astype(BF)
    dO2[...] = (dOT[...].astype(F32) * rcp).T.astype(BF)

    def back(k, v, eb):
        dp = dot(v, dOT[...])
        ds = (eb.astype(F32) * (dp - stxr[3:4, :])).astype(BF)
        oT[...] += dot_tn(k, ds)
        return (dot(ds, q2[...]) * SCALE).astype(BF), dot(eb, dO2[...]).astype(BF)

    def dk_copy(r):
        return remote(dkvs.at[r], dkvr.at[r], dk_ss.at[r], dk_rs.at[r], sdev(r, -1))

    def dt_copy(r):
        return remote(dkvts.at[r], dkvtr.at[r], dt_ss.at[r], dt_rs.at[r], sdev(r, -1))

    def backward(i):
        r = (i // 2 + 1) % 4
        rows = half_of(i)
        gk, gv = back(kv[r, rows, 0:128], kv[r, rows, 128:256], ets[r * 2 + i % 2])
        dkvs[r, rows, 0:128] = gk
        dkvs[r, rows, 128:256] = gv

        @pl.when((i % 2 == 1) & (r != 0))
        def _():
            dk_copy(r).start()

    loop(0, 6, backward)
    gk, gv = back(kt_all, vt, etx[...])
    dkvts[:, :, 0:128] = gk.reshape(4, 64, 128)
    dkvts[:, :, 128:256] = gv.reshape(4, 64, 128)
    loop(1, 4, lambda r: dt_copy(r).start())
    loop(6, 8, backward)

    dq = (oT[...] * (stxr[2:3, :] * SCALE)).T
    dO2[...] = dq.astype(BF)
    qkvp[64:128, 0:128] = dq[0:64]
    qkvp[64:128, 128:256] = dq[64:128]
    dqf[0:512, :] = dq[128:640]
    dqf[512:1024, :] = dq[640:1152]
    their_t = pl.ds(pl.multiple_of(xo * 64, 64), 64)
    their_i = pl.ds(pl.multiple_of(128 + xo * 512, 128), 512)
    cp_dqi = remote(dO2.at[their_i], dqr.at[pl.ds(64, 512)], x_ss.at[5], x_rs.at[5], xdev)
    cp_dqt = remote(dO2.at[their_t], dqr.at[pl.ds(0, 64)], x_ss.at[6], x_rs.at[6], xdev)
    cp_dqi.start()
    cp_dqt.start()
    cp_dqi.wait_recv()
    dqi = dqf[pl.ds(pl.multiple_of(xlo * 512, 512), 512), :] + dqr[64:576, :].astype(F32)
    gq[128:, 0:128] = norm_back(qkvp[128:, 0:128], gains[2:3, :], dqi).astype(BF)

    def dw_copy(r, part):
        cols = pl.ds(0, 128) if part == 0 else pl.ds(128, 256)
        ss, rs = (dq_ss, dq_rs) if part == 0 else (dw_ss, dw_rs)
        return remote(dws.at[r, :, cols], dwr.at[r, :, cols], ss.at[r], rs.at[r], sdev(r % 4, 1))

    def weight_part(i, part):
        r = ((i // 4 + 1) % 2) * 4 + (i + 1) % 4
        lo, hi = (0, 128) if part == 0 else (128, 384)
        dws[r, :, lo:hi] = dot_tn(hid[chip_at(r, 1)], gq[128:, lo:hi]).astype(BF)

        @pl.when(r % 4 != 0)
        def _():
            dw_copy(r, part).start()

    loop(0, 8, lambda i: weight_part(i, 0))
    cp_dqt.wait_recv()
    dqt = jnp.where(xlo == 0, qkvp[64:128, 0:128], qkvp[64:128, 128:256]) + dqr[0:64, :].astype(F32)
    gq[0:64, 0:128] = norm_back(qkvp[0:64, 0:128], gains[0:1, :], dqt).astype(BF)

    wsum[0:64, 0:256] = dkvts[0].astype(F32)

    def add_t(r):
        dt_copy(r).wait_recv()
        wsum[0:64, 0:256] += dkvtr[r].astype(F32)

    loop(1, 4, add_t)
    gq[0:64, 128:256] = norm_back(
        qkvp[0:64, 128:256], gains[1:2, :], wsum[0:64, 0:128]).astype(BF)
    gq[0:64, 256:384] = wsum[0:64, 128:256].astype(BF)

    def gf_copy(r):
        return remote(gtf.at[0], gtf.at[r], gf_ss.at[r], gf_rs.at[r], fdev(r, 1))

    def gs_copy(r):
        return remote(gts.at[0], gts.at[r], gs_ss.at[r], gs_rs.at[r], sdev(r, 1))

    gtf[0] = gq[0:64, :]
    gts[0] = gq[0:64, :]
    loop(1, 8, lambda r: gf_copy(r).start())
    loop(1, 8, lambda r: gs_copy(r).start())

    wsum[:, 0:256] = dkvs[0].astype(F32)

    def add_k(r):
        dk_copy(r).wait_recv()
        wsum[:, 0:256] += dkvr[r].astype(F32)

    loop(1, 4, add_k)
    gq[128:, 128:256] = norm_back(
        qkvp[128:, 128:256], gains[3:4, :], wsum[:, 0:128]).astype(BF)
    gq[128:, 256:384] = wsum[:, 128:256].astype(BF)

    other_rows = pl.ds(pl.multiple_of(128 + o * 256, 128), 256)

    def px_copy(r):
        return remote(pxs.at[r], pxr.at[r], ph_ss.at[0, r], ph_rs.at[0, r], pdev)

    def partner_part(r):
        pxs[r] = dot_nt(gq[other_rows, :], W[r]).astype(BF)
        px_copy(r).start()

    loop(0, 8, partner_part)

    def ph_copy(r):
        return remote(phs.at[r], phr.at[r], ph_ss.at[1, r], ph_rs.at[1, r], fdev(r, -1))

    s1v[...] = jnp.zeros_like(s1v)
    s2v[...] = jnp.zeros_like(s2v)

    def hidden_part(i):
        r = (i + 1) % 8
        b = f_at(r, -1)
        px_copy(r).wait_recv()
        p = (dot_nt(gq[img_rows, :], W[r]) + pxr[r].astype(F32)).astype(BF)
        phs[r] = p

        @pl.when(r != 0)
        def _():
            ph_copy(r).start()

        t = p.astype(F32) * sc[1, b, 0:1, :]
        u = t * nimg[b]
        s1v[...] += t[:, 0:128] + t[:, 128:256] + t[:, 256:384]
        s2v[...] += u[:, 0:128] + u[:, 128:256] + u[:, 256:384]

    def both(i):
        weight_part(i, 1)
        hidden_part(i)

    loop(0, 8, both)

    lane = lax.broadcasted_iota(jnp.int32, (256, 128), 1)
    s1 = jnp.sum(s1v[...], axis=-1, keepdims=True)
    s2 = jnp.sum(s2v[...], axis=-1, keepdims=True)
    sts[...] = jnp.where(lane == 0, s1, s2).T[0:8]

    def st_copy(r):
        return remote(sts, str_.at[r], st_ss.at[r], st_rs.at[r], fdev(r, 1))

    loop(1, 8, lambda r: st_copy(r).start())

    thx[...] = jnp.zeros_like(thx)

    def txt_hidden(r):
        @pl.when(r != 0)
        def _():
            gf_copy(r).wait_recv()

        thx[...] += dot_nt(gtf[r], wt[(r // 4) * 4 + (4 - r % 4) % 4])

    loop(0, 8, txt_hidden)
    their = pl.ds(pl.multiple_of(o * 32, 32), 32)
    cp_th = remote(thx.at[their], thr, p_ss.at[4], p_rs.at[4], pdev)
    cp_th.start()

    loop(1, 8, lambda r: gs_copy(r).wait_recv())
    loop(1, 8, lambda r: h_copy(r).wait_recv())
    wxt[...] = dot_tn(htg[...].reshape(512, 384), gts[...].reshape(512, 384))
    mine = pl.ds(pl.multiple_of(c * 192, 64), 192)
    theirs = pl.ds(pl.multiple_of(o * 192, 64), 192)
    cp_wt = remote(wxt.at[theirs], wxtr, p_ss.at[5], p_rs.at[5], pdev)
    cp_wt.start()

    cp_th.wait_recv()
    gh = thx[txt_rows, :] + thr[...]
    tsc = gh * sc[0, f, 0:1, :]
    tn = ntxt[f]
    t1 = jnp.sum(tsc, axis=-1, keepdims=True)
    t2 = jnp.sum(tsc * tn, axis=-1, keepdims=True)
    lane_t = lax.broadcasted_iota(jnp.int32, (32, 128), 1)
    tsts[...] = jnp.where(lane_t == 0, t1, t2)

    def ts_copy(r):
        return remote(tsts, tstr.at[r], ts_ss.at[r], ts_rs.at[r], fdev(r, 1))

    loop(1, 8, lambda r: ts_copy(r).start())
    thr[...] = tsc

    def place(out, part, head):
        for j in range(3):
            out[j, :, pl.ds(m128(head * 128), 128)] = part[:, j * 128:(j + 1) * 128]

    cp_wt.wait_recv()
    place(dw_txt, wxt[mine, :], c)
    place(dw_txt, wxtr[...], o)

    st = sts[...]
    for r in range(1, 8):
        st_copy(r).wait_recv()
        st = st + str_[r]
    stT = jnp.concatenate([st, jnp.zeros((120, 256), F32)], axis=0).T
    acc = phs[0].astype(F32)
    for r in range(1, 8):
        ph_copy(r).wait_recv()
        acc = acc + phr[r].astype(F32)
    scaled = acc * sc[1, f, 0:1, :]
    dx_img[...] = (invi[:, 0:1] * (
        scaled - stT[:, 0:1] * (1.0 / 3072) - nimg[f] * (stT[:, 1:2] * (1.0 / 3072))
    )).astype(BF)

    tt = tsts[...]
    for r in range(1, 8):
        ts_copy(r).wait_recv()
        tt = tt + tstr[r]
    dx_txt[...] = (invt[:, 0:1] * (
        thr[...] - tt[:, 0:1] * (1.0 / 3072) - ntxt[f] * (tt[:, 1:2] * (1.0 / 3072))
    )).astype(BF)

    def add_w(r):
        dw_copy(r, 0).wait_recv()
        dw_copy(r, 1).wait_recv()
        wx[...] += dwr[r].astype(F32)

    wx[...] = dws[4].astype(F32)
    loop(5, 8, add_w)
    wcs[...] = wx[...].astype(BF)
    cp_wc = remote(wcs, wcr, x_ss.at[7], x_rs.at[7], xdev)
    cp_wc.start()
    wx[...] = dws[0].astype(F32)
    loop(1, 4, add_w)
    cp_wc.wait_recv()
    wx[...] += wcr[...].astype(F32)
    cp_wi = remote(wx.at[theirs], wxr, p_ss.at[6], p_rs.at[6], pdev)
    cp_wi.start()
    place(dw_img, wx[mine, :], c)
    cp_wi.wait_recv()
    place(dw_img, wxr[...], o)

    def drain(r):
        for j in range(3):
            w_copy(r, j).wait_send()
        for cp in (t_copy, h_copy, gf_copy, gs_copy, ph_copy, st_copy, ts_copy):
            cp(r).wait_send()

        @pl.when(r % 4 != 0)
        def _():
            dw_copy(r, 0).wait_send()
            dw_copy(r, 1).wait_send()

    def drain_z(r):
        for cp in (kv_copy, kt_copy, dk_copy, dt_copy):
            cp(r).wait_send()

    loop(1, 8, drain)
    loop(1, 4, drain_z)
    loop(0, 8, lambda r: px_copy(r).wait_send())
    for cp in (cp_coti, cp_cott, cp_ht, cp_hi, cp_th, cp_wt, cp_wi, cp_xot, cp_xoi, cp_xqt,
               cp_xqi, cp_st, cp_dqi, cp_dqt, cp_wc):
        cp.wait_send()


def finish(a, b, c, d, oa, ob, oc, od):
    oa[...] = a[...]
    ob[...] = b[...]
    oc[...] = c[...]
    od[...] = d[...]


def scratch():
    V = pltpu.VMEM
    return [
        V((256, 3072), BF), V((32, 3072), BF), V((2, 256, 6144), BF), V((2, 8, 6144), F32),
        V((2, 8, 8, 384), F32), V((8, 384, 384), BF), V((8, 384, 384), BF),
        V((8, 512, 384), BF), V((8, 64, 384), BF), V((8, 64, 384), BF),
        V((8, 256, 384), F32), V((8, 32, 384), F32), V((256, 128), F32), V((32, 128), F32),
        V((8, 64, 384), BF), V((8, 64, 384), BF), V((640, 384), F32), V((1152, 128), BF),
        V((1152, 128), BF), V((128, 1152), BF), V((128, 1152), BF), V((1152, 128), BF),
        V((1152, 128), BF),
        V((4, 512, 256), BF), V((4, 64, 256), BF), V((8, 256, 1152), BF), V((256, 1152), BF),
        V((4, 512, 256), BF), V((4, 512, 256), BF), V((4, 64, 256), BF), V((4, 64, 256), BF),
        V((128, 1152), F32), V((8, 1152), F32), V((8, 1152), F32), V((1024, 128), F32),
        V((576, 128), BF), V((640, 384), BF),
        V((8, 64, 384), BF), V((8, 64, 384), BF), V((8, 384, 384), BF), V((8, 384, 384), BF),
        V((8, 256, 384), BF), V((8, 256, 384), BF), V((8, 256, 384), BF), V((8, 256, 384), BF),
        V((256, 128), F32), V((256, 128), F32), V((8, 256), F32), V((8, 8, 256), F32),
        V((64, 384), F32), V((32, 384), F32), V((32, 128), F32), V((8, 32, 128), F32),
        V((384, 384), F32), V((192, 384), F32), V((384, 384), F32), V((192, 384), F32),
        V((512, 256), F32), V((384, 384), BF), V((384, 384), BF),
    ] + [
        pltpu.SemaphoreType.DMA(shape)
        for shape in (
            [(6,), (3,), (8, 3), (8, 3), (8, 3), (7,), (7,), (8,), (8,)] + [(8,)] * 4
            + [(4,)] * 8 + [(8,)] * 8 + [(2, 8)] * 2 + [(8,)] * 4
        )
    ]


def on_device(
    img_tokens, txt_tokens, img_weight, txt_weight, img_modulation, txt_modulation, qk_gains,
    timestep, valid_text, img_cotangent, txt_cotangent,
):
    features = time_features(timestep, img_modulation.shape[0])
    anys = pl.BlockSpec(memory_space=pl.ANY)
    vm = pl.BlockSpec(memory_space=pltpu.VMEM)
    dw_img, dw_txt, dx_img, dx_txt = pl.pallas_call(
        kernel,
        out_shape=(
            jax.ShapeDtypeStruct((3, 192, 256), F32),
            jax.ShapeDtypeStruct((3, 192, 256), F32),
            jax.ShapeDtypeStruct((256, 384), BF),
            jax.ShapeDtypeStruct((32, 384), BF),
        ),
        in_specs=[anys] * 6 + [vm] * 2 + [pl.BlockSpec(memory_space=pltpu.SMEM)] + [anys] * 2,
        out_specs=[vm] * 4,
        scratch_shapes=scratch(),
        compiler_params=pltpu.CompilerParams(
            collective_id=0, has_side_effects=True, vmem_limit_bytes=62 * 2 ** 20),
        name="joint_block",
    )(
        img_tokens, txt_tokens, jnp.transpose(img_weight, (1, 0, 2)),
        jnp.transpose(txt_weight, (1, 0, 2)), img_modulation, txt_modulation, features,
        qk_gains.reshape(4, HD), valid_text, img_cotangent, txt_cotangent,
    )
    shapes = tuple(jax.ShapeDtypeStruct(v.shape, v.dtype) for v in (dw_img, dw_txt, dx_img, dx_txt))
    dw_img, dw_txt, dx_img, dx_txt = pl.pallas_call(
        finish, out_shape=shapes, in_specs=[vm] * 4, out_specs=[vm] * 4, name="results",
    )(dw_img, dw_txt, dx_img, dx_txt)
    return (
        jnp.transpose(dw_img, (1, 0, 2)), jnp.transpose(dw_txt, (1, 0, 2)), dx_img, dx_txt
    )


def solution(mesh):
    return jax.shard_map(
        on_device,
        mesh=mesh,
        in_specs=(
            P("seq", None),
            P("seq", None),
            P("fsdp", None, None),
            P("fsdp", None, None),
            P(),
            P(),
            P(),
            P(),
            P(),
            P("seq", "fsdp"),
            P("seq", "fsdp"),
        ),
        out_specs=(
            P("seq", None, "fsdp"),
            P("seq", None, "fsdp"),
            P("seq", "fsdp"),
            P("seq", "fsdp"),
        ),
        check_vma=False,
    )
```

```python
import functools
import math

import jax
import jax.numpy as jnp
from jax import lax
from jax.experimental import pallas as pl
from jax.experimental.pallas import tpu as pltpu
from jax.sharding import PartitionSpec as P

HD = 128
BF = jnp.bfloat16
F32 = jnp.float32
MESH = pl.DeviceIdType.MESH
SCALE = HD ** (-0.5)
EXP2 = SCALE / math.log(2.0)
EPS = 1e-06


def time_features(timestep, freq_dim):
    half_freq = freq_dim // 2
    frequency = jnp.exp(-math.log(10000.0) * jnp.arange(half_freq, dtype=jnp.float32) / half_freq)
    angles = timestep.astype(jnp.float32)[:, None] * frequency[None, :]
    features = jnp.concatenate([jnp.cos(angles), jnp.sin(angles)], axis=1)
    return jax.nn.silu(features).astype(jnp.bfloat16)


def dot(a, b):
    return jnp.dot(a, b, preferred_element_type=F32)


def dot_nt(a, b):
    return lax.dot_general(a, b, (((1,), (1,)), ((), ())), preferred_element_type=F32)


def dot_tn(a, b):
    return lax.dot_general(a, b, (((0,), (0,)), ((), ())), preferred_element_type=F32)


def norm_back(x, gain, grad):
    r = lax.rsqrt(jnp.mean(x * x, axis=-1, keepdims=True) + EPS)
    gd = gain * grad
    return r * gd - x * (r * r * r * jnp.mean(x * gd, axis=-1, keepdims=True))


def kernel(
    x_img, x_txt, w_img, w_txt, mod_img, mod_txt, feat, gains, valid, cot_img, cot_txt,
    dw_img, dw_txt, dx_img, dx_txt,
    xi, xt, mods, mixed, sc, W, wt, hid, hidt, htg, nimg, ntxt, invi, invt,
    tps, tpr, qkvp, dO, qr, qT, dOT, q2, dO2, kv, kvt, ets, etx, dkvs, dkvr, dkvts, dkvtr,
    oT, stx, stxr, dqf, dqr, gq, gtf, gts, dws, dwr, pxs, pxr, phs, phr, s1v, s2v, sts, str_,
    thx, thr, tsts, tstr, wx, wxr, wxt, wxtr, wsum, wcs, wcr,
    lsem, wl_sem, wtl_sem, w_ss, w_rs, z_ss, z_rs, p_ss, p_rs, x_ss, x_rs, t_ss, t_rs, h_ss, h_rs,
    kv_ss, kv_rs, kt_ss, kt_rs, dk_ss, dk_rs, dt_ss, dt_rs, gf_ss, gf_rs, gs_ss, gs_rs,
    dq_ss, dq_rs, dw_ss, dw_rs, ph_ss, ph_rs, st_ss, st_rs, ts_ss, ts_rs,
):
    s = lax.axis_index("seq")
    f = lax.axis_index("fsdp")
    chip, c = s // 2, s % 2
    xlo, z = chip // 4, chip % 4
    y, xhi = f // 2, f % 2
    o = 1 - c

    def f_at(r, sign):
        return ((y + sign * (r % 4) + 4) % 4) * 2 + (xhi + r // 4) % 2

    def chip_at(r, sign):
        return ((xlo + r // 4) % 2) * 4 + (z + sign * (r % 4) + 4) % 4

    def fdev(r, sign):
        return (s, f_at(r, sign))

    def sdev(r, sign):
        return (chip_at(r, sign) * 2 + c, f)

    pdev = (chip * 2 + o, f)
    xdev = sdev(4, 1)
    xo = 1 - xlo

    def remote(src, dst, ss, rs, dev):
        return pltpu.make_async_remote_copy(
            src_ref=src, dst_ref=dst, send_sem=ss, recv_sem=rs, device_id=dev, device_id_type=MESH
        )

    def loop(lo, hi, body):
        def step(i, carry):
            body(i)
            return carry

        lax.fori_loop(lo, hi, step, 0)

    def m128(v):
        return pl.multiple_of(v, 128)

    loc = [
        pltpu.make_async_copy(x_img, xi, lsem.at[0]),
        pltpu.make_async_copy(x_txt, xt, lsem.at[1]),
        pltpu.make_async_copy(mod_img, mods.at[1], lsem.at[2]),
        pltpu.make_async_copy(mod_txt, mods.at[0], lsem.at[3]),
        pltpu.make_async_copy(
            cot_img.at[:, pl.ds(m128(c * 128), 128)],
            dO.at[pl.ds(pl.multiple_of(128 + xlo * 512 + c * 256, 128), 256)], lsem.at[4]),
        pltpu.make_async_copy(
            cot_txt.at[:, pl.ds(m128(c * 128), 128)],
            dO.at[pl.ds(pl.multiple_of(xlo * 64 + c * 32, 32), 32)], lsem.at[5]),
    ]
    for cp in loc:
        cp.start()

    barrier = pltpu.get_barrier_semaphore()

    def hello(r):
        pl.semaphore_signal(barrier, inc=1, device_id=fdev(r, 1), device_id_type=MESH)
        pl.semaphore_signal(barrier, inc=1, device_id=sdev(r, 1), device_id_type=MESH)

    loop(1, 8, hello)
    pl.semaphore_signal(barrier, inc=1, device_id=pdev, device_id_type=MESH)

    def w_cols(ref, j, fp):
        return ref.at[j, :, pl.ds(m128((2 * fp + c) * 128), 128)]

    def wl_copy(j):
        return pltpu.make_async_copy(
            w_cols(w_img, j, f), W.at[0, :, pl.ds(j * 128, 128)], wl_sem.at[j])

    def wt_copy(r, j):
        return pltpu.make_async_copy(
            w_cols(w_txt, j, f_at(r, 1)), wt.at[r, :, pl.ds(j * 128, 128)], wtl_sem.at[r, j])

    for j in range(3):
        wl_copy(j).start()

    hz = z % 2
    my_half = pl.ds(pl.multiple_of(hz * 192, 64), 192)

    def w_copy(r, j):
        return remote(
            w_img.at[j, my_half, pl.ds(m128((2 * f_at(r, 1) + c) * 128), 128)],
            W.at[r, my_half, pl.ds(j * 128, 128)],
            w_ss.at[r, j], w_rs.at[r, 1], fdev(r, 1))

    def w_landed(r):
        ref = W.at[r, my_half, pl.ds(128, 256)]
        return remote(ref, ref, w_ss.at[r, 1], w_rs.at[r, 1], fdev(r, 1))

    def wq_copy(r):
        return remote(
            w_cols(w_img, 0, f_at(r, 1)), W.at[r, :, pl.ds(0, 128)],
            w_ss.at[r, 0], w_rs.at[r, 0], fdev(r, 1))

    def z_copy(d, r, half):
        ref = W.at[r, pl.ds(pl.multiple_of(half * 192 + d * 96, 32), 96), pl.ds(128, 256)]
        return remote(ref, ref, z_ss.at[d, r], z_rs.at[d, r], sdev(1, 1 - 2 * d))

    def send_w(r):
        for j in (1, 2):
            w_copy(r, j).start()

    def start_wt(r):
        for j in range(3):
            wt_copy(r, j).start()

    def pass_w(r):
        w_landed(r).wait_recv()
        for d in (0, 1):
            z_copy(d, r, hz).start()
        wq_copy(r).start()

    pl.semaphore_wait(barrier, 15)
    loop(1, 8, send_w)
    loop(0, 8, start_wt)

    img_rows = pl.ds(pl.multiple_of(128 + c * 256, 128), 256)
    txt_rows = pl.ds(pl.multiple_of(c * 32, 32), 32)
    half_rows = pl.ds(pl.multiple_of(c * 256, 256), 256)
    cp_coti = remote(cot_img.at[:, pl.ds(m128(o * 128), 128)],
                     dO.at[pl.ds(pl.multiple_of(128 + xlo * 512 + c * 256, 128), 256)],
                     p_ss.at[0], p_rs.at[0], pdev)
    cp_cott = remote(cot_txt.at[:, pl.ds(m128(o * 128), 128)],
                     dO.at[pl.ds(pl.multiple_of(xlo * 64 + c * 32, 32), 32)],
                     p_ss.at[1], p_rs.at[1], pdev)
    cp_coti.start()
    cp_cott.start()

    for which in (0, 1):
        loc[3 - which].wait()
        row = jnp.broadcast_to(feat[...].astype(F32), (16, 256)).astype(BF)
        mixed[which] = dot(row, mods[which])[:8]
        for b in range(8):
            sc[which, b] = 1.0 + mixed[which, :, 3072 + b * 384:3072 + (b + 1) * 384]

    def prepare(which, src, nrm, inv, put):
        rows = 16

        def body(i):
            at = pl.multiple_of(i * rows, rows)
            v = src[pl.ds(at, rows), :].astype(F32)
            cen = v - jnp.mean(v, axis=-1, keepdims=True)
            iv = lax.rsqrt(jnp.mean(cen * cen, axis=-1, keepdims=True) + EPS)
            n = cen * iv
            inv[pl.ds(at, rows), :] = jnp.broadcast_to(iv, (rows, 128))
            h = (n * (1.0 + mixed[which, 0:1, 3072:]) + mixed[which, 0:1, :3072]).astype(BF)
            for b in range(8):
                nrm[b, pl.ds(at, rows), :] = n[:, b * 384:(b + 1) * 384]
                put(b, at, rows, h[:, b * 384:(b + 1) * 384])
            if which == 1:
                pl.when((i > 4) & (i < 12))(lambda: pass_w(i - 4))

        loop(0, src.shape[0] // rows, body)

    def put_txt(b, at, rows, h):
        hidt[b, pl.ds(pl.multiple_of(c * 32 + at, 16), rows), :] = h

    def put_img(b, at, rows, h):
        hid[b, pl.ds(pl.multiple_of(c * 256 + at, 16), rows), :] = h

    loc[1].wait()
    prepare(0, xt, ntxt, invt, put_txt)
    cp_ht = remote(hidt.at[:, txt_rows], hidt.at[:, txt_rows], p_ss.at[2], p_rs.at[2], pdev)
    cp_ht.start()
    loc[0].wait()
    prepare(1, xi, nimg, invi, put_img)
    cp_hi = remote(hid.at[:, half_rows], hid.at[:, half_rows], p_ss.at[3], p_rs.at[3], pdev)
    cp_hi.start()

    cp_ht.wait_recv()

    def t_copy(r):
        return remote(tps.at[r], tpr.at[r], t_ss.at[r], t_rs.at[r], fdev(r, 1))

    def h_copy(r):
        return remote(hidt.at[chip_at(r, 1)], htg.at[r], h_ss.at[r], h_rs.at[r], sdev(r, 1))

    def txt_partial(i):
        r = (i + 1) % 8
        for j in range(3):
            wt_copy(r, j).wait()
        tps[r] = dot(hidt[f], wt[r]).astype(BF)

        @pl.when(r != 0)
        def _():
            t_copy(r).start()

    loop(0, 8, txt_partial)
    htg[0] = hidt[chip]
    loop(1, 8, lambda r: h_copy(r).start())

    own_t = pl.ds(pl.multiple_of(xlo * 64, 64), 64)
    own_i = pl.ds(pl.multiple_of(128 + xlo * 512, 128), 512)
    loc[4].wait()
    loc[5].wait()
    cp_coti.wait_recv()
    cp_cott.wait_recv()
    cp_xot = remote(dO.at[own_t], dO.at[own_t], x_ss.at[0], x_rs.at[0], xdev)
    cp_xoi = remote(dO.at[own_i], dO.at[own_i], x_ss.at[1], x_rs.at[1], xdev)
    cp_xot.start()
    cp_xoi.start()

    cp_hi.wait_recv()
    for j in range(3):
        wl_copy(j).wait()
    qkvp[128:, :] = dot(hid[f], W[0])

    def img_proj(r):
        for d in (0, 1):
            z_copy(d, r, 1 - hz).wait_recv()
        qkvp[128:, 128:384] += dot(hid[f_at(r, -1)], W[r, :, 128:384])

    loop(1, 8, img_proj)

    def normed_head(lo, hi, col, g):
        a = qkvp[lo:hi, col:col + 128]
        return (a * lax.rsqrt(jnp.mean(a * a, axis=-1, keepdims=True) + EPS)
                * gains[g:g + 1, :]).astype(BF)

    def kv_copy(r):
        return remote(kv.at[0], kv.at[r], kv_ss.at[r], kv_rs.at[r], sdev(r, 1))

    def kt_copy(r):
        return remote(kvt.at[0], kvt.at[r], kt_ss.at[r], kt_rs.at[r], sdev(r, 1))

    kv[0, :, 0:128] = normed_head(128, 640, 128, 3)
    kv[0, :, 128:256] = qkvp[128:, 256:384].astype(BF)
    loop(1, 4, lambda r: kv_copy(r).start())

    qkvp[0:64, :] = tps[0].astype(F32)

    def txt_add(r):
        t_copy(r).wait_recv()
        qkvp[0:64, :] += tpr[r].astype(F32)

    loop(1, 8, txt_add)
    kvt[0, :, 0:128] = normed_head(0, 64, 128, 1)
    kvt[0, :, 128:256] = qkvp[0:64, 256:384].astype(BF)
    loop(1, 4, lambda r: kt_copy(r).start())

    def img_query(r):
        wq_copy(r).wait_recv()
        qkvp[128:, 0:128] += dot(hid[f_at(r, -1)], W[r, :, 0:128])

    loop(1, 8, img_query)
    qr[own_i, :] = normed_head(128, 640, 0, 2)
    qr[own_t, :] = normed_head(0, 64, 0, 0)
    cp_xqt = remote(qr.at[own_t], qr.at[own_t], x_ss.at[2], x_rs.at[2], xdev)
    cp_xqi = remote(qr.at[own_i], qr.at[own_i], x_ss.at[3], x_rs.at[3], xdev)
    cp_xqi.start()
    cp_xqt.start()
    cp_xot.wait_recv()
    cp_xoi.wait_recv()
    dOT[...] = dO[...].astype(F32).T.astype(BF)
    cp_xqi.wait_recv()
    cp_xqt.wait_recv()
    qT[...] = qr[...].astype(F32).T.astype(BF)

    oT[...] = jnp.zeros_like(oT)
    stx[...] = jnp.zeros_like(stx)

    def half_of(i):
        return pl.ds(pl.multiple_of((i % 2) * 256, 256), 256)

    def forward(i):
        r = i // 2

        @pl.when((i % 2 == 0) & (r != 0))
        def _():
            kv_copy(r).wait_recv()

        e = jnp.exp2(dot(kv[r, half_of(i), 0:128], qT[...]) * EXP2)
        stx[0:1, :] += jnp.sum(e, axis=0, keepdims=True)
        eb = e.astype(BF)
        ets[i] = eb
        oT[...] += dot_tn(kv[r, half_of(i), 128:256], eb)

    loop(0, 8, forward)
    loop(1, 4, lambda r: kt_copy(r).wait_recv())

    def forward_text(r):
        e = jnp.exp2(dot(kvt[r, :, 0:128], qT[...]) * EXP2)
        index = chip_at(r, -1) * 64 + lax.broadcasted_iota(jnp.int32, (64, 1152), 0)
        e = jnp.where(index < valid[0], e, 0.0)
        stx[0:1, :] += jnp.sum(e, axis=0, keepdims=True)
        etx[pl.ds(pl.multiple_of(r * 64, 64), 64), :] = e.astype(BF)

    loop(0, 4, forward_text)
    vt = kvt[:, :, 128:256].reshape(256, 128)
    kt_all = kvt[:, :, 0:128].reshape(256, 128)
    oT[...] += dot_tn(vt, etx[...])

    stx[1:2, :] = jnp.sum(dOT[...].astype(F32) * oT[...], axis=0, keepdims=True)
    cp_st = remote(stx, stxr, x_ss.at[4], x_rs.at[4], xdev)
    cp_st.start()
    oT[...] = jnp.zeros_like(oT)
    cp_st.wait_recv()
    rcp = 1.0 / (stx[0:1, :] + stxr[0:1, :])
    delta = (stx[1:2, :] + stxr[1:2, :]) * rcp
    stxr[2:3, :] = rcp
    stxr[3:4, :] = delta
    q2[...] = (qT[...].astype(F32) * rcp).T.astype(BF)
    dO2[...] = (dOT[...].astype(F32) * rcp).T.astype(BF)

    def back(k, v, eb):
        dp = dot(v, dOT[...])
        ds = (eb.astype(F32) * (dp - stxr[3:4, :])).astype(BF)
        oT[...] += dot_tn(k, ds)
        return (dot(ds, q2[...]) * SCALE).astype(BF), dot(eb, dO2[...]).astype(BF)

    def dk_copy(r):
        return remote(dkvs.at[r], dkvr.at[r], dk_ss.at[r], dk_rs.at[r], sdev(r, -1))

    def dt_copy(r):
        return remote(dkvts.at[r], dkvtr.at[r], dt_ss.at[r], dt_rs.at[r], sdev(r, -1))

    def backward(i):
        r = (i // 2 + 1) % 4
        rows = half_of(i)
        gk, gv = back(kv[r, rows, 0:128], kv[r, rows, 128:256], ets[r * 2 + i % 2])
        dkvs[r, rows, 0:128] = gk
        dkvs[r, rows, 128:256] = gv

        @pl.when((i % 2 == 1) & (r != 0))
        def _():
            dk_copy(r).start()

    loop(0, 6, backward)
    gk, gv = back(kt_all, vt, etx[...])
    dkvts[:, :, 0:128] = gk.reshape(4, 64, 128)
    dkvts[:, :, 128:256] = gv.reshape(4, 64, 128)
    loop(1, 4, lambda r: dt_copy(r).start())
    loop(6, 8, backward)

    dq = (oT[...] * (stxr[2:3, :] * SCALE)).T
    dO2[...] = dq.astype(BF)
    qkvp[64:128, 0:128] = dq[0:64]
    qkvp[64:128, 128:256] = dq[64:128]
    dqf[0:512, :] = dq[128:640]
    dqf[512:1024, :] = dq[640:1152]
    their_t = pl.ds(pl.multiple_of(xo * 64, 64), 64)
    their_i = pl.ds(pl.multiple_of(128 + xo * 512, 128), 512)
    cp_dqi = remote(dO2.at[their_i], dqr.at[pl.ds(64, 512)], x_ss.at[5], x_rs.at[5], xdev)
    cp_dqt = remote(dO2.at[their_t], dqr.at[pl.ds(0, 64)], x_ss.at[6], x_rs.at[6], xdev)
    cp_dqi.start()
    cp_dqt.start()
    cp_dqi.wait_recv()
    dqi = dqf[pl.ds(pl.multiple_of(xlo * 512, 512), 512), :] + dqr[64:576, :].astype(F32)
    gq[128:, 0:128] = norm_back(qkvp[128:, 0:128], gains[2:3, :], dqi).astype(BF)

    def dw_copy(r, part):
        cols = pl.ds(0, 128) if part == 0 else pl.ds(128, 256)
        ss, rs = (dq_ss, dq_rs) if part == 0 else (dw_ss, dw_rs)
        return remote(dws.at[r, :, cols], dwr.at[r, :, cols], ss.at[r], rs.at[r], sdev(r % 4, 1))

    def weight_part(i, part):
        r = ((i // 4 + 1) % 2) * 4 + (i + 1) % 4
        lo, hi = (0, 128) if part == 0 else (128, 384)
        dws[r, :, lo:hi] = dot_tn(hid[chip_at(r, 1)], gq[128:, lo:hi]).astype(BF)

        @pl.when(r % 4 != 0)
        def _():
            dw_copy(r, part).start()

    loop(0, 8, lambda i: weight_part(i, 0))
    cp_dqt.wait_recv()
    dqt = jnp.where(xlo == 0, qkvp[64:128, 0:128], qkvp[64:128, 128:256]) + dqr[0:64, :].astype(F32)
    gq[0:64, 0:128] = norm_back(qkvp[0:64, 0:128], gains[0:1, :], dqt).astype(BF)

    wsum[0:64, 0:256] = dkvts[0].astype(F32)

    def add_t(r):
        dt_copy(r).wait_recv()
        wsum[0:64, 0:256] += dkvtr[r].astype(F32)

    loop(1, 4, add_t)
    gq[0:64, 128:256] = norm_back(
        qkvp[0:64, 128:256], gains[1:2, :], wsum[0:64, 0:128]).astype(BF)
    gq[0:64, 256:384] = wsum[0:64, 128:256].astype(BF)

    def gf_copy(r):
        return remote(gtf.at[0], gtf.at[r], gf_ss.at[r], gf_rs.at[r], fdev(r, 1))

    def gs_copy(r):
        return remote(gts.at[0], gts.at[r], gs_ss.at[r], gs_rs.at[r], sdev(r, 1))

    gtf[0] = gq[0:64, :]
    gts[0] = gq[0:64, :]
    loop(1, 8, lambda r: gf_copy(r).start())
    loop(1, 8, lambda r: gs_copy(r).start())

    wsum[:, 0:256] = dkvs[0].astype(F32)

    def add_k(r):
        dk_copy(r).wait_recv()
        wsum[:, 0:256] += dkvr[r].astype(F32)

    loop(1, 4, add_k)
    gq[128:, 128:256] = norm_back(
        qkvp[128:, 128:256], gains[3:4, :], wsum[:, 0:128]).astype(BF)
    gq[128:, 256:384] = wsum[:, 128:256].astype(BF)

    other_rows = pl.ds(pl.multiple_of(128 + o * 256, 128), 256)

    def px_copy(r):
        return remote(pxs.at[r], pxr.at[r], ph_ss.at[0, r], ph_rs.at[0, r], pdev)

    def partner_part(r):
        pxs[r] = dot_nt(gq[other_rows, :], W[r]).astype(BF)
        px_copy(r).start()

    loop(0, 8, partner_part)

    def ph_copy(r):
        return remote(phs.at[r], phr.at[r], ph_ss.at[1, r], ph_rs.at[1, r], fdev(r, -1))

    s1v[...] = jnp.zeros_like(s1v)
    s2v[...] = jnp.zeros_like(s2v)

    def hidden_part(i):
        r = (i + 1) % 8
        b = f_at(r, -1)
        px_copy(r).wait_recv()
        p = (dot_nt(gq[img_rows, :], W[r]) + pxr[r].astype(F32)).astype(BF)
        phs[r] = p

        @pl.when(r != 0)
        def _():
            ph_copy(r).start()

        t = p.astype(F32) * sc[1, b, 0:1, :]
        u = t * nimg[b]
        s1v[...] += t[:, 0:128] + t[:, 128:256] + t[:, 256:384]
        s2v[...] += u[:, 0:128] + u[:, 128:256] + u[:, 256:384]

    def both(i):
        weight_part(i, 1)
        hidden_part(i)

    loop(0, 8, both)

    def add_w(r):
        dw_copy(r, 0).wait_recv()
        dw_copy(r, 1).wait_recv()
        wx[...] += dwr[r].astype(F32)

    wx[...] = dws[4].astype(F32)
    loop(5, 8, add_w)
    wcs[...] = wx[...].astype(BF)
    cp_wc = remote(wcs, wcr, x_ss.at[7], x_rs.at[7], xdev)
    cp_wc.start()

    lane = lax.broadcasted_iota(jnp.int32, (256, 128), 1)
    s1 = jnp.sum(s1v[...], axis=-1, keepdims=True)
    s2 = jnp.sum(s2v[...], axis=-1, keepdims=True)
    sts[...] = jnp.where(lane == 0, s1, s2).T[0:8]

    def st_copy(r):
        return remote(sts, str_.at[r], st_ss.at[r], st_rs.at[r], fdev(r, 1))

    loop(1, 8, lambda r: st_copy(r).start())

    thx[...] = jnp.zeros_like(thx)

    def txt_hidden(r):
        @pl.when(r != 0)
        def _():
            gf_copy(r).wait_recv()

        thx[...] += dot_nt(gtf[r], wt[(r // 4) * 4 + (4 - r % 4) % 4])

    loop(0, 8, txt_hidden)
    their = pl.ds(pl.multiple_of(o * 32, 32), 32)
    cp_th = remote(thx.at[their], thr, p_ss.at[4], p_rs.at[4], pdev)
    cp_th.start()

    loop(1, 8, lambda r: gs_copy(r).wait_recv())
    loop(1, 8, lambda r: h_copy(r).wait_recv())
    wxt[...] = dot_tn(htg[...].reshape(512, 384), gts[...].reshape(512, 384))
    mine = pl.ds(pl.multiple_of(c * 192, 64), 192)
    theirs = pl.ds(pl.multiple_of(o * 192, 64), 192)
    cp_wt = remote(wxt.at[theirs], wxtr, p_ss.at[5], p_rs.at[5], pdev)
    cp_wt.start()

    cp_th.wait_recv()
    gh = thx[txt_rows, :] + thr[...]
    tsc = gh * sc[0, f, 0:1, :]
    tn = ntxt[f]
    t1 = jnp.sum(tsc, axis=-1, keepdims=True)
    t2 = jnp.sum(tsc * tn, axis=-1, keepdims=True)
    lane_t = lax.broadcasted_iota(jnp.int32, (32, 128), 1)
    tsts[...] = jnp.where(lane_t == 0, t1, t2)

    def ts_copy(r):
        return remote(tsts, tstr.at[r], ts_ss.at[r], ts_rs.at[r], fdev(r, 1))

    loop(1, 8, lambda r: ts_copy(r).start())
    thr[...] = tsc

    def place(out, part, head):
        for j in range(3):
            out[j, :, pl.ds(m128(head * 128), 128)] = part[:, j * 128:(j + 1) * 128]

    cp_wt.wait_recv()
    place(dw_txt, wxt[mine, :], c)
    place(dw_txt, wxtr[...], o)

    st = sts[...]
    for r in range(1, 8):
        st_copy(r).wait_recv()
        st = st + str_[r]
    stT = jnp.concatenate([st, jnp.zeros((120, 256), F32)], axis=0).T
    acc = phs[0].astype(F32)
    for r in range(1, 8):
        ph_copy(r).wait_recv()
        acc = acc + phr[r].astype(F32)
    scaled = acc * sc[1, f, 0:1, :]
    dx_img[...] = (invi[:, 0:1] * (
        scaled - stT[:, 0:1] * (1.0 / 3072) - nimg[f] * (stT[:, 1:2] * (1.0 / 3072))
    )).astype(BF)

    tt = tsts[...]
    for r in range(1, 8):
        ts_copy(r).wait_recv()
        tt = tt + tstr[r]
    dx_txt[...] = (invt[:, 0:1] * (
        thr[...] - tt[:, 0:1] * (1.0 / 3072) - ntxt[f] * (tt[:, 1:2] * (1.0 / 3072))
    )).astype(BF)

    wx[...] = dws[0].astype(F32)
    loop(1, 4, add_w)
    cp_wc.wait_recv()
    wx[...] += wcr[...].astype(F32)
    cp_wi = remote(wx.at[theirs], wxr, p_ss.at[6], p_rs.at[6], pdev)
    cp_wi.start()
    place(dw_img, wx[mine, :], c)
    cp_wi.wait_recv()
    place(dw_img, wxr[...], o)

    def drain(r):
        for j in (1, 2):
            w_copy(r, j).wait_send()
        wq_copy(r).wait_send()
        for d in (0, 1):
            z_copy(d, r, hz).wait_send()
        for cp in (t_copy, h_copy, gf_copy, gs_copy, ph_copy, st_copy, ts_copy):
            cp(r).wait_send()

        @pl.when(r % 4 != 0)
        def _():
            dw_copy(r, 0).wait_send()
            dw_copy(r, 1).wait_send()

    def drain_z(r):
        for cp in (kv_copy, kt_copy, dk_copy, dt_copy):
            cp(r).wait_send()

    loop(1, 8, drain)
    loop(1, 4, drain_z)
    loop(0, 8, lambda r: px_copy(r).wait_send())
    for cp in (cp_coti, cp_cott, cp_ht, cp_hi, cp_th, cp_wt, cp_wi, cp_xot, cp_xoi, cp_xqt,
               cp_xqi, cp_st, cp_dqi, cp_dqt, cp_wc):
        cp.wait_send()


def finish(a, b, c, d, oa, ob, oc, od):
    oa[...] = a[...]
    ob[...] = b[...]
    oc[...] = c[...]
    od[...] = d[...]


def scratch():
    V = pltpu.VMEM
    return [
        V((256, 3072), BF), V((32, 3072), BF), V((2, 256, 6144), BF), V((2, 8, 6144), F32),
        V((2, 8, 8, 384), F32), V((8, 384, 384), BF), V((8, 384, 384), BF),
        V((8, 512, 384), BF), V((8, 64, 384), BF), V((8, 64, 384), BF),
        V((8, 256, 384), F32), V((8, 32, 384), F32), V((256, 128), F32), V((32, 128), F32),
        V((8, 64, 384), BF), V((8, 64, 384), BF), V((640, 384), F32), V((1152, 128), BF),
        V((1152, 128), BF), V((128, 1152), BF), V((128, 1152), BF), V((1152, 128), BF),
        V((1152, 128), BF),
        V((4, 512, 256), BF), V((4, 64, 256), BF), V((8, 256, 1152), BF), V((256, 1152), BF),
        V((4, 512, 256), BF), V((4, 512, 256), BF), V((4, 64, 256), BF), V((4, 64, 256), BF),
        V((128, 1152), F32), V((8, 1152), F32), V((8, 1152), F32), V((1024, 128), F32),
        V((576, 128), BF), V((640, 384), BF),
        V((8, 64, 384), BF), V((8, 64, 384), BF), V((8, 384, 384), BF), V((8, 384, 384), BF),
        V((8, 256, 384), BF), V((8, 256, 384), BF), V((8, 256, 384), BF), V((8, 256, 384), BF),
        V((256, 128), F32), V((256, 128), F32), V((8, 256), F32), V((8, 8, 256), F32),
        V((64, 384), F32), V((32, 384), F32), V((32, 128), F32), V((8, 32, 128), F32),
        V((384, 384), F32), V((192, 384), F32), V((384, 384), F32), V((192, 384), F32),
        V((512, 256), F32), V((384, 384), BF), V((384, 384), BF),
    ] + [
        pltpu.SemaphoreType.DMA(shape)
        for shape in (
            [(6,), (3,), (8, 3), (8, 3), (8, 2), (2, 8), (2, 8), (7,), (7,), (8,), (8,)] + [(8,)] * 4
            + [(4,)] * 8 + [(8,)] * 8 + [(2, 8)] * 2 + [(8,)] * 4
        )
    ]


def on_device(
    img_tokens, txt_tokens, img_weight, txt_weight, img_modulation, txt_modulation, qk_gains,
    timestep, valid_text, img_cotangent, txt_cotangent,
):
    features = time_features(timestep, img_modulation.shape[0])
    anys = pl.BlockSpec(memory_space=pl.ANY)
    vm = pl.BlockSpec(memory_space=pltpu.VMEM)
    dw_img, dw_txt, dx_img, dx_txt = pl.pallas_call(
        kernel,
        out_shape=(
            jax.ShapeDtypeStruct((3, 192, 256), F32),
            jax.ShapeDtypeStruct((3, 192, 256), F32),
            jax.ShapeDtypeStruct((256, 384), BF),
            jax.ShapeDtypeStruct((32, 384), BF),
        ),
        in_specs=[anys] * 6 + [vm] * 2 + [pl.BlockSpec(memory_space=pltpu.SMEM)] + [anys] * 2,
        out_specs=[vm] * 4,
        scratch_shapes=scratch(),
        compiler_params=pltpu.CompilerParams(
            collective_id=0, has_side_effects=True, vmem_limit_bytes=62 * 2 ** 20),
        name="joint_block",
    )(
        img_tokens, txt_tokens, jnp.transpose(img_weight, (1, 0, 2)),
        jnp.transpose(txt_weight, (1, 0, 2)), img_modulation, txt_modulation, features,
        qk_gains.reshape(4, HD), valid_text, img_cotangent, txt_cotangent,
    )
    shapes = tuple(jax.ShapeDtypeStruct(v.shape, v.dtype) for v in (dw_img, dw_txt, dx_img, dx_txt))
    dw_img, dw_txt, dx_img, dx_txt = pl.pallas_call(
        finish, out_shape=shapes, in_specs=[vm] * 4, out_specs=[vm] * 4, name="results",
    )(dw_img, dw_txt, dx_img, dx_txt)
    return (
        jnp.transpose(dw_img, (1, 0, 2)), jnp.transpose(dw_txt, (1, 0, 2)), dx_img, dx_txt
    )


def solution(mesh):
    return jax.shard_map(
        on_device,
        mesh=mesh,
        in_specs=(
            P("seq", None),
            P("seq", None),
            P("fsdp", None, None),
            P("fsdp", None, None),
            P(),
            P(),
            P(),
            P(),
            P(),
            P("seq", "fsdp"),
            P("seq", "fsdp"),
        ),
        out_specs=(
            P("seq", None, "fsdp"),
            P("seq", None, "fsdp"),
            P("seq", "fsdp"),
            P("seq", "fsdp"),
        ),
        check_vma=False,
    )
```

```python
import functools
import math

import jax
import jax.numpy as jnp
from jax import lax
from jax.experimental import pallas as pl
from jax.experimental.pallas import tpu as pltpu
from jax.sharding import PartitionSpec as P

HD = 128
BF = jnp.bfloat16
F32 = jnp.float32
MESH = pl.DeviceIdType.MESH
SCALE = HD ** (-0.5)
EXP2 = SCALE / math.log(2.0)
EPS = 1e-06


def time_features(timestep, freq_dim):
    half_freq = freq_dim // 2
    frequency = jnp.exp(-math.log(10000.0) * jnp.arange(half_freq, dtype=jnp.float32) / half_freq)
    angles = timestep.astype(jnp.float32)[:, None] * frequency[None, :]
    features = jnp.concatenate([jnp.cos(angles), jnp.sin(angles)], axis=1)
    return jax.nn.silu(features).astype(jnp.bfloat16)


def dot(a, b):
    return jnp.dot(a, b, preferred_element_type=F32)


def dot_nt(a, b):
    return lax.dot_general(a, b, (((1,), (1,)), ((), ())), preferred_element_type=F32)


def dot_tn(a, b):
    return lax.dot_general(a, b, (((0,), (0,)), ((), ())), preferred_element_type=F32)


def norm_back(x, gain, grad):
    r = lax.rsqrt(jnp.mean(x * x, axis=-1, keepdims=True) + EPS)
    gd = gain * grad
    return r * gd - x * (r * r * r * jnp.mean(x * gd, axis=-1, keepdims=True))


def kernel(
    x_img, x_txt, w_img, w_txt, mod_img, mod_txt, feat, gains, valid, cot_img, cot_txt,
    dw_img, dw_txt, dx_img, dx_txt,
    xi, xt, mods, mixed, sc, W, wt, hid, hidt, htg, nimg, ntxt, invi, invt,
    tps, tpr, qkvp, dO, qr, qT, dOT, q2, dO2, kv, ets, acc, dks, dkr,
    dqT, stx, stxr, stf, dqs, dqr, dqts, dqtr, gq, gtf, gts, dws, dwr, rl, pxs, pxr, phs, phr,
    hcs, hcr, s1v, s2v, sts, str_,
    thx, thr, tsts, tstr, wx, wxr, wxt, wxtr, wcs, wcr,
    lsem, wl_sem, wtl_sem, w_ss, w_rs, z_ss, z_rs, p_ss, p_rs, x_ss, x_rs, t_ss, t_rs, h_ss, h_rs,
    do_ss, do_rs, q_ss, q_rs, dq_ss, dq_rs, sx_ss, sx_rs, rl_ss, rl_rs,
    gf_ss, gf_rs, gs_ss, gs_rs, dw_ss, dw_rs, ph_ss, ph_rs, st_ss, st_rs, ts_ss, ts_rs,
):
    s = lax.axis_index("seq")
    f = lax.axis_index("fsdp")
    chip, c = s // 2, s % 2
    xlo, z = chip // 4, chip % 4
    y, xhi = f // 2, f % 2
    o = 1 - c

    def f_at(r, sign):
        return ((y + sign * (r % 4) + 4) % 4) * 2 + (xhi + r // 4) % 2

    def chip_at(r, sign):
        return ((xlo + r // 4) % 2) * 4 + (z + sign * (r % 4) + 4) % 4

    def fdev(r, sign):
        return (s, f_at(r, sign))

    def sdev(r, sign):
        return (chip_at(r, sign) * 2 + c, f)

    pdev = (chip * 2 + o, f)
    xdev = sdev(4, 1)
    xo = 1 - xlo
    xodev = ((xo * 4 + z) * 2 + o, f)

    def remote(src, dst, ss, rs, dev):
        return pltpu.make_async_remote_copy(
            src_ref=src, dst_ref=dst, send_sem=ss, recv_sem=rs, device_id=dev, device_id_type=MESH
        )

    def loop(lo, hi, body):
        def step(i, carry):
            body(i)
            return carry

        lax.fori_loop(lo, hi, step, 0)

    def m128(v):
        return pl.multiple_of(v, 128)

    loc = [
        pltpu.make_async_copy(x_img, xi, lsem.at[0]),
        pltpu.make_async_copy(x_txt, xt, lsem.at[1]),
        pltpu.make_async_copy(mod_img, mods.at[1], lsem.at[2]),
        pltpu.make_async_copy(mod_txt, mods.at[0], lsem.at[3]),
        pltpu.make_async_copy(
            cot_img.at[:, pl.ds(m128(c * 128), 128)],
            dO.at[pl.ds(pl.multiple_of(z * 512 + c * 256, 256), 256)], lsem.at[4]),
        pltpu.make_async_copy(
            cot_txt.at[:, pl.ds(m128(c * 128), 128)],
            dO.at[pl.ds(pl.multiple_of(2048 + z * 64 + c * 32, 32), 32)], lsem.at[5]),
    ]
    for cp in loc:
        cp.start()

    barrier = pltpu.get_barrier_semaphore()

    def hello(r):
        pl.semaphore_signal(barrier, inc=1, device_id=fdev(r, 1), device_id_type=MESH)
        pl.semaphore_signal(barrier, inc=1, device_id=sdev(r, 1), device_id_type=MESH)

    loop(1, 8, hello)
    pl.semaphore_signal(barrier, inc=1, device_id=pdev, device_id_type=MESH)
    pl.semaphore_signal(barrier, inc=1, device_id=xodev, device_id_type=MESH)

    def w_cols(ref, j, fp):
        return ref.at[j, :, pl.ds(m128((2 * fp + c) * 128), 128)]

    def wl_copy(j):
        return pltpu.make_async_copy(
            w_cols(w_img, j, f), W.at[0, :, pl.ds(j * 128, 128)], wl_sem.at[j])

    def wt_copy(r, j):
        return pltpu.make_async_copy(
            w_cols(w_txt, j, f_at(r, 1)), wt.at[r, :, pl.ds(j * 128, 128)], wtl_sem.at[r, j])

    for j in range(3):
        wl_copy(j).start()

    hz = z % 2
    my_half = pl.ds(pl.multiple_of(hz * 192, 64), 192)

    def w_copy(r, j):
        return remote(
            w_img.at[j, my_half, pl.ds(m128((2 * f_at(r, 1) + c) * 128), 128)],
            W.at[r, my_half, pl.ds(j * 128, 128)],
            w_ss.at[r, j], w_rs.at[r, j], fdev(r, 1))

    def wv_copy(r):
        return remote(
            w_cols(w_img, 2, f_at(r, 1)), W.at[r, :, pl.ds(256, 128)],
            w_ss.at[r, 2], w_rs.at[r, 2], fdev(r, 1))

    def z_copy(j, d, r, half):
        ref = W.at[r, pl.ds(pl.multiple_of(half * 192 + d * 96, 32), 96), pl.ds(j * 128, 128)]
        return remote(ref, ref, z_ss.at[j, d, r], z_rs.at[j, d, r], sdev(1, 1 - 2 * d))

    def start_wt(r):
        for j in range(3):
            wt_copy(r, j).start()

    def pass_w(j):
        def one(r):
            w_copy(r, j).wait_recv()
            for d in (0, 1):
                z_copy(j, d, r, hz).start()

        loop(1, 8, one)

    def start_keys():
        loop(1, 8, lambda r: w_copy(r, 0).wait_send())
        loop(1, 8, lambda r: w_copy(r, 1).start())

    pl.semaphore_wait(barrier, 16)
    loop(1, 8, lambda r: w_copy(r, 0).start())
    loop(0, 8, start_wt)

    img_rows = pl.ds(pl.multiple_of(128 + c * 256, 128), 256)
    txt_rows = pl.ds(pl.multiple_of(c * 32, 32), 32)
    half_rows = pl.ds(pl.multiple_of(c * 256, 256), 256)
    cp_coti = remote(cot_img.at[:, pl.ds(m128(o * 128), 128)],
                     dO.at[pl.ds(pl.multiple_of(z * 512 + c * 256, 256), 256)],
                     p_ss.at[0], p_rs.at[0], pdev)
    cp_cott = remote(cot_txt.at[:, pl.ds(m128(o * 128), 128)],
                     dO.at[pl.ds(pl.multiple_of(2048 + z * 64 + c * 32, 32), 32)],
                     p_ss.at[1], p_rs.at[1], pdev)
    cp_coti.start()
    cp_cott.start()

    for which in (0, 1):
        loc[3 - which].wait()
        row = jnp.broadcast_to(feat[...].astype(F32), (16, 256)).astype(BF)
        mixed[which] = dot(row, mods[which])[:8]
        for b in range(8):
            sc[which, b] = 1.0 + mixed[which, :, 3072 + b * 384:3072 + (b + 1) * 384]

    def z_rows(part, zz):
        if part == 0:
            return pl.ds(pl.multiple_of(zz * 512, 512), 512)
        return pl.ds(pl.multiple_of(2048 + zz * 64, 64), 64)

    def ring_copy(ref, ss, rs, part, b, zz):
        rows = ref.at[z_rows(part, zz)]
        return remote(rows, rows, ss.at[part, b], rs.at[part, b], sdev(b, 1))

    def z_back(b):
        return (z + 4 - b) % 4

    loc[4].wait()
    loc[5].wait()
    cp_coti.wait_recv()
    cp_cott.wait_recv()

    def send_do(b):
        for part in (0, 1):
            ring_copy(dO, do_ss, do_rs, part, b, z).start()

    loop(1, 4, send_do)

    def prepare(which, src, nrm, inv, put):
        rows = 16

        def body(i):
            at = pl.multiple_of(i * rows, rows)
            v = src[pl.ds(at, rows), :].astype(F32)
            cen = v - jnp.mean(v, axis=-1, keepdims=True)
            iv = lax.rsqrt(jnp.mean(cen * cen, axis=-1, keepdims=True) + EPS)
            n = cen * iv
            inv[pl.ds(at, rows), :] = jnp.broadcast_to(iv, (rows, 128))
            h = (n * (1.0 + mixed[which, 0:1, 3072:]) + mixed[which, 0:1, :3072]).astype(BF)
            for b in range(8):
                nrm[b, pl.ds(at, rows), :] = n[:, b * 384:(b + 1) * 384]
                put(b, at, rows, h[:, b * 384:(b + 1) * 384])
            if which == 1:
                pl.when(i == 8)(start_keys)

        loop(0, src.shape[0] // rows, body)

    def put_txt(b, at, rows, h):
        hidt[b, pl.ds(pl.multiple_of(c * 32 + at, 16), rows), :] = h

    def put_img(b, at, rows, h):
        hid[b, pl.ds(pl.multiple_of(c * 256 + at, 16), rows), :] = h

    loc[1].wait()
    prepare(0, xt, ntxt, invt, put_txt)
    cp_ht = remote(hidt.at[:, txt_rows], hidt.at[:, txt_rows], p_ss.at[2], p_rs.at[2], pdev)
    cp_ht.start()
    loc[0].wait()
    prepare(1, xi, nimg, invi, put_img)
    cp_hi = remote(hid.at[:, half_rows], hid.at[:, half_rows], p_ss.at[3], p_rs.at[3], pdev)
    cp_hi.start()

    pass_w(0)
    loop(1, 8, lambda r: w_copy(r, 1).wait_send())
    loop(1, 8, lambda r: wv_copy(r).start())

    cp_ht.wait_recv()

    def t_copy(r):
        return remote(tps.at[r], tpr.at[r], t_ss.at[r], t_rs.at[r], fdev(r, 1))

    def h_copy(r):
        return remote(hidt.at[chip_at(r, 1)], htg.at[r], h_ss.at[r], h_rs.at[r], sdev(r, 1))

    def txt_partial(i):
        r = (i + 1) % 8
        for j in range(3):
            wt_copy(r, j).wait()
        tps[r] = dot(hidt[f], wt[r]).astype(BF)

        @pl.when(r != 0)
        def _():
            t_copy(r).start()

    loop(0, 8, txt_partial)
    pass_w(1)

    def normed_head(lo, hi, col, g):
        a = qkvp[lo:hi, col:col + 128]
        return (a * lax.rsqrt(jnp.mean(a * a, axis=-1, keepdims=True) + EPS)
                * gains[g:g + 1, :]).astype(BF)

    def kv_copy(lo, n, col, wide, at):
        cols = pl.ds(col, wide)
        return remote(kv.at[pl.ds(lo, n), cols], kv.at[pl.ds(lo + 576, n), cols],
                      x_ss.at[at], x_rs.at[at], xdev)

    cp_kvk = kv_copy(0, 512, 0, 128, 0)
    cp_kvv = kv_copy(0, 512, 128, 128, 5)
    cp_kvt = kv_copy(512, 64, 0, 256, 1)

    def send_q(part):
        loop(1, 4, lambda b: ring_copy(qr, q_ss, q_rs, part, b, z).start())

    def project(j):
        lo, hi = j * 128, j * 128 + 128

        def one(r):
            if j == 2:
                wv_copy(r).wait_recv()
            else:
                for d in (0, 1):
                    z_copy(j, d, r, 1 - hz).wait_recv()
            qkvp[128:, lo:hi] += dot(hid[f_at(r, -1)], W[r, :, lo:hi])

        loop(1, 8, one)

    cp_hi.wait_recv()
    for j in range(3):
        wl_copy(j).wait()
    qkvp[128:, :] = dot(hid[f], W[0])
    project(0)
    qr[z_rows(0, z), :] = normed_head(128, 640, 0, 2)
    send_q(0)
    project(1)
    kv[0:512, 0:128] = normed_head(128, 640, 128, 3)
    cp_kvk.start()

    qkvp[0:64, :] = tps[0].astype(F32)

    def txt_add(r):
        t_copy(r).wait_recv()
        qkvp[0:64, :] += tpr[r].astype(F32)

    loop(1, 8, txt_add)
    kv[512:576, 0:128] = normed_head(0, 64, 128, 1)
    kv[512:576, 128:256] = qkvp[0:64, 256:384].astype(BF)
    cp_kvt.start()
    qr[z_rows(1, z), :] = normed_head(0, 64, 0, 0)
    send_q(1)
    project(2)
    kv[0:512, 128:256] = qkvp[128:, 256:384].astype(BF)
    cp_kvv.start()

    def wait_do(b):
        for part in (0, 1):
            ring_copy(dO, do_ss, do_rs, part, b, z_back(b)).wait_recv()

    loop(1, 4, wait_do)
    dOT[...] = dO[...].astype(F32).T.astype(BF)

    def cols_at(i):
        return pl.ds(pl.multiple_of(i * 256, 256), 256)

    def chunk_at(i):
        return ((z + i // 2) % 4) * 2 + i % 2

    def forward(idx):
        cols = cols_at(idx)
        tot = jnp.zeros((1, 256), F32)
        for a in (0, 1):
            e = jnp.exp2(dot(kv[a * 576:a * 576 + 576, 0:128], qT[:, cols]) * EXP2)
            index = chip_at(a * 4, 1) * 64 + lax.broadcasted_iota(jnp.int32, (64, 256), 0)
            et = jnp.where(index < valid[0], e[512:576], 0.0)
            tot += jnp.sum(e[0:512], axis=0, keepdims=True) + jnp.sum(et, axis=0, keepdims=True)
            ets[idx, a * 576:a * 576 + 512, :] = e[0:512].astype(BF)
            ets[idx, a * 576 + 512:a * 576 + 576, :] = et.astype(BF)
        part = dot_tn(kv[:, 128:256], ets[idx])
        stx[0:1, cols] = tot
        stx[1:2, cols] = jnp.sum(dOT[:, cols].astype(F32) * part, axis=0, keepdims=True)

    cp_kvk.wait_recv()
    cp_kvt.wait_recv()
    cp_kvv.wait_recv()

    def forward_img(k):
        b = (4 - k) % 4

        @pl.when(b != 0)
        def _():
            ring_copy(qr, q_ss, q_rs, 0, b, z_back(b)).wait_recv()

        zz = z_back(b)
        rows = z_rows(0, zz)
        qT[:, rows] = qr[rows, :].astype(F32).T.astype(BF)
        loop(0, 2, lambda h: forward(zz * 2 + h))

    loop(0, 4, forward_img)
    loop(1, 4, lambda b: ring_copy(qr, q_ss, q_rs, 1, b, z_back(b)).wait_recv())
    qT[:, 2048:2304] = qr[2048:2304, :].astype(F32).T.astype(BF)
    forward(8)

    def sx_copy(b):
        return remote(stx, stxr.at[b], sx_ss.at[b], sx_rs.at[b], sdev(b, 1))

    loop(1, 4, lambda b: sx_copy(b).start())
    loop(1, 4, lambda b: sx_copy(b).wait_recv())
    sums = stx[...] + stxr[1] + stxr[2] + stxr[3]
    rcp = 1.0 / sums[0:1]
    stf[0:1, :] = rcp
    stf[1:2, :] = sums[1:2] * rcp
    q2[...] = (qT[...].astype(F32) * rcp).T.astype(BF)
    dO2[...] = (dOT[...].astype(F32) * rcp).T.astype(BF)
    htg[0] = hidt[chip]
    loop(1, 8, lambda r: h_copy(r).start())

    def back(a, idx):
        cols = cols_at(idx)
        keys = slice(a * 576, a * 576 + 576)
        dp = dot(kv[keys, 128:256], dOT[:, cols])
        eb = ets[idx, keys, :]
        ds = (eb.astype(F32) * (dp - stf[1:2, cols])).astype(BF)
        part = dot_tn(kv[keys, 0:128], ds)
        if a == 1:
            dqT[:, cols] = part
        else:
            dqT[:, cols] += part
        acc[:, 0:128] += dot(ds, q2[cols, :])
        acc[:, 128:256] += dot(eb, dO2[cols, :])

    acc[...] = jnp.zeros_like(acc)
    loop(0, 9, lambda i: back(1, i))
    dks[:, 0:128] = (acc[:, 0:128] * SCALE).astype(BF)
    dks[:, 128:256] = acc[:, 128:256].astype(BF)
    cp_dk = remote(dks, dkr, x_ss.at[2], x_rs.at[2], xdev)
    cp_dk.start()
    acc[...] = jnp.zeros_like(acc)

    def dq_rows(cols):
        return (dqT[:, cols] * (stf[0:1, cols] * SCALE)).T

    def dq_copy(b):
        return remote(dqs.at[b], dqr.at[b], dq_ss.at[0, b], dq_rs.at[0, b], sdev(b, 1))

    def dqt_copy(b):
        mine = pl.ds(pl.multiple_of(((z + b) % 4) * 64, 64), 64)
        return remote(dqts.at[mine], dqtr.at[b], dq_ss.at[1, b], dq_rs.at[1, b], sdev(b, 1))

    def back_peer(b):
        zz = (z + b) % 4
        loop(0, 2, lambda h: back(0, zz * 2 + h))
        dqs[b] = dq_rows(z_rows(0, zz)).astype(BF)
        dq_copy(b).start()

    loop(1, 4, back_peer)
    back(0, 8)
    dqts[...] = dq_rows(slice(2048, 2304)).astype(BF)
    loop(1, 4, lambda b: dqt_copy(b).start())
    loop(0, 2, lambda h: back(0, z * 2 + h))

    cp_dk.wait_recv()
    acc[:, 0:128] = acc[:, 0:128] * SCALE + dkr[:, 0:128].astype(F32)
    acc[:, 128:256] += dkr[:, 128:256].astype(F32)
    gq[128:, 128:256] = norm_back(
        qkvp[128:, 128:256], gains[3:4, :], acc[0:512, 0:128]).astype(BF)
    gq[128:, 256:384] = acc[0:512, 128:256].astype(BF)
    gq[0:64, 128:256] = norm_back(
        qkvp[0:64, 128:256], gains[1:2, :], acc[512:576, 0:128]).astype(BF)
    gq[0:64, 256:384] = acc[512:576, 128:256].astype(BF)

    dqi = dq_rows(z_rows(0, z))
    own_text = pl.ds(pl.multiple_of(z * 64, 64), 64)
    for b in (1, 2, 3):
        dqt_copy(b).wait_recv()
    dqt = dqts[own_text, :].astype(F32)
    for b in (1, 2, 3):
        dqt = dqt + dqtr[b].astype(F32)
    gq[0:64, 0:128] = norm_back(qkvp[0:64, 0:128], gains[0:1, :], dqt).astype(BF)
    for b in (1, 2, 3):
        dq_copy(b).wait_recv()
        dqi = dqi + dqr[b].astype(F32)
    gq[128:, 0:128] = norm_back(qkvp[128:, 0:128], gains[2:3, :], dqi).astype(BF)

    def gf_copy(r):
        return remote(gtf.at[0], gtf.at[r], gf_ss.at[r], gf_rs.at[r], fdev(r, 1))

    def gs_copy(r):
        return remote(gts.at[0], gts.at[r], gs_ss.at[r], gs_rs.at[r], sdev(r, 1))

    gtf[0] = gq[0:64, :]
    gts[0] = gq[0:64, :]
    loop(1, 8, lambda r: gf_copy(r).start())

    def dw_block(a, b):
        return dot_tn(hid[chip_at(a * 4 + b, 1)], gq[128:, :])

    def rl_copy(a, d):
        rows = pl.ds(d * 192, 192)
        return remote(dws.at[a * 4 + 2, rows], rl.at[a, rows], rl_ss.at[a, d], rl_rs.at[a, d],
                      sdev(1 + 2 * d, 1))

    def dw_copy(r):
        return remote(dws.at[r], dwr.at[r], dw_ss.at[r], dw_rs.at[r], sdev(r % 4, 1))

    dws[6] = dw_block(1, 2).astype(BF)
    for d in (0, 1):
        rl_copy(1, d).start()
    dws[2] = dw_block(0, 2).astype(BF)

    other_rows = pl.ds(pl.multiple_of(128 + o * 256, 128), 256)

    def px_copy(r):
        return remote(pxs.at[r], pxr.at[r], ph_ss.at[0, r], ph_rs.at[0, r], pdev)

    def partner_part(i):
        r = (7 - i) % 8
        pxs[r] = dot_nt(gq[other_rows, :], W[r]).astype(BF)
        px_copy(r).start()

    loop(0, 8, partner_part)
    for d in (0, 1):
        rl_copy(1, d).wait_send()
    for d in (0, 1):
        rl_copy(0, d).start()

    def ph_copy(r):
        return remote(phs.at[r], phr.at[r], ph_ss.at[1, r], ph_rs.at[1, r], fdev(r % 4, -1))

    s1v[...] = jnp.zeros_like(s1v)
    s2v[...] = jnp.zeros_like(s2v)

    def hidden_part(i):
        r = (7 - i) % 8
        b = f_at(r, -1)
        px_copy(r).wait_recv()
        p = (dot_nt(gq[img_rows, :], W[r]) + pxr[r].astype(F32)).astype(BF)
        phs[r] = p

        @pl.when(r % 4 != 0)
        def _():
            ph_copy(r).start()

        t = p.astype(F32) * sc[1, b, 0:1, :]
        u = t * nimg[b]
        s1v[...] += t[:, 0:128] + t[:, 128:256] + t[:, 256:384]
        s2v[...] += u[:, 0:128] + u[:, 128:256] + u[:, 256:384]

    def passed_on(a, d):
        rl_copy(a, d).wait_recv()
        r = a * 4 + 1 + 2 * d
        block = dw_block(a, 1 + 2 * d)
        lo, hi = d * 192, d * 192 + 192
        dws[r, 192 - lo:384 - lo, :] = block[192 - lo:384 - lo].astype(BF)
        dws[r, lo:hi, :] = (block[lo:hi] + rl[a, lo:hi, :].astype(F32)).astype(BF)

    loop(0, 2, hidden_part)
    for d in (0, 1):
        passed_on(1, d)
        dw_copy(5 + 2 * d).start()
    loop(2, 6, hidden_part)
    for d in (0, 1):
        passed_on(0, d)
    for d in (0, 1):
        dw_copy(5 + 2 * d).wait_send()
    for d in (0, 1):
        dw_copy(1 + 2 * d).start()
    loop(1, 8, lambda r: gs_copy(r).start())
    loop(6, 8, hidden_part)

    lane = lax.broadcasted_iota(jnp.int32, (256, 128), 1)
    s1 = jnp.sum(s1v[...], axis=-1, keepdims=True)
    s2 = jnp.sum(s2v[...], axis=-1, keepdims=True)
    sts[...] = jnp.where(lane == 0, s1, s2).T[0:8]

    def st_copy(r):
        return remote(sts, str_.at[r], st_ss.at[r], st_rs.at[r], fdev(r, 1))

    loop(1, 8, lambda r: st_copy(r).start())

    thx[...] = jnp.zeros_like(thx)

    def txt_hidden(r):
        @pl.when(r != 0)
        def _():
            gf_copy(r).wait_recv()

        thx[...] += dot_nt(gtf[r], wt[(r // 4) * 4 + (4 - r % 4) % 4])

    loop(0, 8, txt_hidden)
    their = pl.ds(pl.multiple_of(o * 32, 32), 32)
    cp_th = remote(thx.at[their], thr, p_ss.at[4], p_rs.at[4], pdev)
    cp_th.start()

    cp_th.wait_recv()
    gh = thx[txt_rows, :] + thr[...]
    tsc = gh * sc[0, f, 0:1, :]
    tn = ntxt[f]
    t1 = jnp.sum(tsc, axis=-1, keepdims=True)
    t2 = jnp.sum(tsc * tn, axis=-1, keepdims=True)
    lane_t = lax.broadcasted_iota(jnp.int32, (32, 128), 1)
    tsts[...] = jnp.where(lane_t == 0, t1, t2)

    def ts_copy(r):
        return remote(tsts, tstr.at[r], ts_ss.at[r], ts_rs.at[r], fdev(r, 1))

    loop(1, 8, lambda r: ts_copy(r).start())
    thr[...] = tsc

    mine = pl.ds(pl.multiple_of(c * 192, 64), 192)
    theirs = pl.ds(pl.multiple_of(o * 192, 64), 192)
    wx[...] = dw_block(1, 0)
    for r in (5, 7):
        dw_copy(r).wait_recv()
        wx[...] += dwr[r].astype(F32)
    wcs[...] = wx[...].astype(BF)
    cp_wc = remote(wcs.at[mine], wcr.at[0], x_ss.at[3], x_rs.at[3], xdev)
    cp_wo = remote(wcs.at[theirs], wcr.at[1], x_ss.at[6], x_rs.at[6], xodev)
    cp_wc.start()
    cp_wo.start()
    hsum = phs[4].astype(F32)
    for r in (5, 6, 7):
        ph_copy(r).wait_recv()
        hsum = hsum + phr[r].astype(F32)
    hcs[...] = hsum.astype(BF)
    cp_hc = remote(hcs, hcr, x_ss.at[4], x_rs.at[4], fdev(4, 1))
    cp_hc.start()
    wx[...] = dw_block(0, 0)

    loop(1, 8, lambda r: gs_copy(r).wait_recv())
    loop(1, 8, lambda r: h_copy(r).wait_recv())
    wxt[...] = dot_tn(htg[...].reshape(512, 384), gts[...].reshape(512, 384))
    cp_wt = remote(wxt.at[theirs], wxtr, p_ss.at[5], p_rs.at[5], pdev)
    cp_wt.start()

    def place(out, part, head):
        for j in range(3):
            out[j, :, pl.ds(m128(head * 128), 128)] = part[:, j * 128:(j + 1) * 128]

    for r in (1, 3):
        dw_copy(r).wait_recv()
        wx[...] += dwr[r].astype(F32)
    cp_wi = remote(wx.at[theirs], wxr, p_ss.at[6], p_rs.at[6], pdev)
    cp_wi.start()

    st = sts[...]
    for r in range(1, 8):
        st_copy(r).wait_recv()
        st = st + str_[r]
    stT = jnp.concatenate([st, jnp.zeros((120, 256), F32)], axis=0).T
    gsum = phs[0].astype(F32)
    for r in (1, 2, 3):
        ph_copy(r).wait_recv()
        gsum = gsum + phr[r].astype(F32)
    cp_hc.wait_recv()
    gsum = gsum + hcr[...].astype(F32)
    scaled = gsum * sc[1, f, 0:1, :]
    dx_img[...] = (invi[:, 0:1] * (
        scaled - stT[:, 0:1] * (1.0 / 3072) - nimg[f] * (stT[:, 1:2] * (1.0 / 3072))
    )).astype(BF)

    tt = tsts[...]
    for r in range(1, 8):
        ts_copy(r).wait_recv()
        tt = tt + tstr[r]
    dx_txt[...] = (invt[:, 0:1] * (
        thr[...] - tt[:, 0:1] * (1.0 / 3072) - ntxt[f] * (tt[:, 1:2] * (1.0 / 3072))
    )).astype(BF)

    cp_wt.wait_recv()
    place(dw_txt, wxt[mine, :], c)
    place(dw_txt, wxtr[...], o)
    cp_wc.wait_recv()
    place(dw_img, wx[mine, :] + wcr[0].astype(F32), c)
    cp_wi.wait_recv()
    cp_wo.wait_recv()
    place(dw_img, wxr[...] + wcr[1].astype(F32), o)

    def drain(r):
        wv_copy(r).wait_send()
        for j in (0, 1):
            for d in (0, 1):
                z_copy(j, d, r, hz).wait_send()
        for cp in (t_copy, h_copy, gf_copy, gs_copy, st_copy, ts_copy):
            cp(r).wait_send()

        @pl.when(r % 4 != 0)
        def _():
            ph_copy(r).wait_send()

    def drain_z(b):
        for part in (0, 1):
            ring_copy(dO, do_ss, do_rs, part, b, z).wait_send()
            ring_copy(qr, q_ss, q_rs, part, b, z).wait_send()
        for cp in (sx_copy, dq_copy, dqt_copy):
            cp(b).wait_send()

    loop(1, 8, drain)
    loop(1, 4, drain_z)
    loop(0, 8, lambda r: px_copy(r).wait_send())
    for d in (0, 1):
        rl_copy(0, d).wait_send()
        dw_copy(1 + 2 * d).wait_send()
    for cp in (cp_coti, cp_cott, cp_ht, cp_hi, cp_th, cp_wt, cp_wi, cp_kvk, cp_kvv, cp_kvt,
               cp_dk, cp_wc, cp_wo, cp_hc):
        cp.wait_send()


def finish(a, b, c, d, oa, ob, oc, od):
    oa[...] = a[...]
    ob[...] = b[...]
    oc[...] = c[...]
    od[...] = d[...]


def scratch():
    V = pltpu.VMEM
    return [
        V((256, 3072), BF), V((32, 3072), BF), V((2, 256, 6144), BF), V((2, 8, 6144), F32),
        V((2, 8, 8, 384), F32), V((8, 384, 384), BF), V((8, 384, 384), BF),
        V((8, 512, 384), BF), V((8, 64, 384), BF), V((8, 64, 384), BF),
        V((8, 256, 384), F32), V((8, 32, 384), F32), V((256, 128), F32), V((32, 128), F32),
        V((8, 64, 384), BF), V((8, 64, 384), BF), V((640, 384), F32), V((2304, 128), BF),
        V((2304, 128), BF), V((128, 2304), BF), V((128, 2304), BF), V((2304, 128), BF),
        V((2304, 128), BF),
        V((1152, 256), BF), V((9, 1152, 256), BF), V((576, 256), F32), V((576, 256), BF),
        V((576, 256), BF),
        V((128, 2304), F32), V((2, 2304), F32), V((4, 2, 2304), F32), V((2, 2304), F32),
        V((4, 512, 128), BF), V((4, 512, 128), BF), V((256, 128), BF), V((4, 64, 128), BF),
        V((640, 384), BF),
        V((8, 64, 384), BF), V((8, 64, 384), BF), V((8, 384, 384), BF), V((8, 384, 384), BF),
        V((2, 384, 384), BF),
        V((8, 256, 384), BF), V((8, 256, 384), BF), V((8, 256, 384), BF), V((8, 256, 384), BF),
        V((256, 384), BF), V((256, 384), BF),
        V((256, 128), F32), V((256, 128), F32), V((8, 256), F32), V((8, 8, 256), F32),
        V((64, 384), F32), V((32, 384), F32), V((32, 128), F32), V((8, 32, 128), F32),
        V((384, 384), F32), V((192, 384), F32), V((384, 384), F32), V((192, 384), F32),
        V((384, 384), BF), V((2, 192, 384), BF),
    ] + [
        pltpu.SemaphoreType.DMA(shape)
        for shape in (
            [(6,), (3,), (8, 3), (8, 3), (8, 3), (2, 2, 8), (2, 2, 8), (7,), (7,), (7,), (7,)]
            + [(8,)] * 4 + [(2, 4)] * 6 + [(4,)] * 2 + [(2, 2)] * 2 + [(8,)] * 6
            + [(2, 8)] * 2 + [(8,)] * 4
        )
    ]


def on_device(
    img_tokens, txt_tokens, img_weight, txt_weight, img_modulation, txt_modulation, qk_gains,
    timestep, valid_text, img_cotangent, txt_cotangent,
):
    features = time_features(timestep, img_modulation.shape[0])
    anys = pl.BlockSpec(memory_space=pl.ANY)
    vm = pl.BlockSpec(memory_space=pltpu.VMEM)
    dw_img, dw_txt, dx_img, dx_txt = pl.pallas_call(
        kernel,
        out_shape=(
            jax.ShapeDtypeStruct((3, 192, 256), F32),
            jax.ShapeDtypeStruct((3, 192, 256), F32),
            jax.ShapeDtypeStruct((256, 384), BF),
            jax.ShapeDtypeStruct((32, 384), BF),
        ),
        in_specs=[anys] * 6 + [vm] * 2 + [pl.BlockSpec(memory_space=pltpu.SMEM)] + [anys] * 2,
        out_specs=[vm] * 4,
        scratch_shapes=scratch(),
        compiler_params=pltpu.CompilerParams(
            collective_id=0, has_side_effects=True, vmem_limit_bytes=62 * 2 ** 20),
        name="joint_block",
    )(
        img_tokens, txt_tokens, jnp.transpose(img_weight, (1, 0, 2)),
        jnp.transpose(txt_weight, (1, 0, 2)), img_modulation, txt_modulation, features,
        qk_gains.reshape(4, HD), valid_text, img_cotangent, txt_cotangent,
    )
    shapes = tuple(jax.ShapeDtypeStruct(v.shape, v.dtype) for v in (dw_img, dw_txt, dx_img, dx_txt))
    dw_img, dw_txt, dx_img, dx_txt = pl.pallas_call(
        finish, out_shape=shapes, in_specs=[vm] * 4, out_specs=[vm] * 4, name="results",
    )(dw_img, dw_txt, dx_img, dx_txt)
    return (
        jnp.transpose(dw_img, (1, 0, 2)), jnp.transpose(dw_txt, (1, 0, 2)), dx_img, dx_txt
    )


def solution(mesh):
    return jax.shard_map(
        on_device,
        mesh=mesh,
        in_specs=(
            P("seq", None),
            P("seq", None),
            P("fsdp", None, None),
            P("fsdp", None, None),
            P(),
            P(),
            P(),
            P(),
            P(),
            P("seq", "fsdp"),
            P("seq", "fsdp"),
        ),
        out_specs=(
            P("seq", None, "fsdp"),
            P("seq", None, "fsdp"),
            P("seq", "fsdp"),
            P("seq", "fsdp"),
        ),
        check_vma=False,
    )
```

```python
import functools
import math

import jax
import jax.numpy as jnp
from jax import lax
from jax.experimental import pallas as pl
from jax.experimental.pallas import tpu as pltpu
from jax.sharding import PartitionSpec as P

HD = 128
BF = jnp.bfloat16
F32 = jnp.float32
MESH = pl.DeviceIdType.MESH
SCALE = HD ** (-0.5)
EXP2 = SCALE / math.log(2.0)
EPS = 1e-06


def time_features(timestep, freq_dim):
    half_freq = freq_dim // 2
    frequency = jnp.exp(-math.log(10000.0) * jnp.arange(half_freq, dtype=jnp.float32) / half_freq)
    angles = timestep.astype(jnp.float32)[:, None] * frequency[None, :]
    features = jnp.concatenate([jnp.cos(angles), jnp.sin(angles)], axis=1)
    return jax.nn.silu(features).astype(jnp.bfloat16)


def dot(a, b):
    return jnp.dot(a, b, preferred_element_type=F32)


def dot_nt(a, b):
    return lax.dot_general(a, b, (((1,), (1,)), ((), ())), preferred_element_type=F32)


def dot_tn(a, b):
    return lax.dot_general(a, b, (((0,), (0,)), ((), ())), preferred_element_type=F32)


def norm_back(x, gain, grad):
    r = lax.rsqrt(jnp.mean(x * x, axis=-1, keepdims=True) + EPS)
    gd = gain * grad
    return r * gd - x * (r * r * r * jnp.mean(x * gd, axis=-1, keepdims=True))


def kernel(
    x_img, x_txt, w_img, w_txt, mod_img, mod_txt, feat, gains, valid, cot_img, cot_txt,
    dw_img, dw_txt, dx_img, dx_txt,
    xi, xt, mods, mixed, sc, W, wt, hid, hidt, htg, nimg, ntxt, invi, invt,
    tps, tpr, qkvp, dO, qr, qT, dOT, q2, dO2, kv, ets, acc, dks, dkr,
    dqT, stx, stxr, stf, dqs, dqr, dqts, dqtr, gq, gtf, gts, dws, dwr, rl, pxs, pxr, phs, phr,
    hcs, hcr, s1v, s2v, sts, str_,
    thx, thr, tsts, tstr, wx, wxr, wxt, wxtr, wcs, wcr,
    lsem, wl_sem, wtl_sem, w_ss, w_rs, z_ss, z_rs, p_ss, p_rs, x_ss, x_rs, t_ss, t_rs, h_ss, h_rs,
    do_ss, do_rs, q_ss, q_rs, dq_ss, dq_rs, sx_ss, sx_rs, rl_ss, rl_rs,
    gf_ss, gf_rs, gs_ss, gs_rs, dw_ss, dw_rs, ph_ss, ph_rs, st_ss, st_rs, ts_ss, ts_rs,
):
    s = lax.axis_index("seq")
    f = lax.axis_index("fsdp")
    chip, c = s // 2, s % 2
    xlo, z = chip // 4, chip % 4
    y, xhi = f // 2, f % 2
    o = 1 - c

    def f_at(r, sign):
        return ((y + sign * (r % 4) + 4) % 4) * 2 + (xhi + r // 4) % 2

    def chip_at(r, sign):
        return ((xlo + r // 4) % 2) * 4 + (z + sign * (r % 4) + 4) % 4

    def fdev(r, sign):
        return (s, f_at(r, sign))

    def sdev(r, sign):
        return (chip_at(r, sign) * 2 + c, f)

    pdev = (chip * 2 + o, f)
    xdev = sdev(4, 1)
    xo = 1 - xlo
    xodev = ((xo * 4 + z) * 2 + o, f)

    def remote(src, dst, ss, rs, dev):
        return pltpu.make_async_remote_copy(
            src_ref=src, dst_ref=dst, send_sem=ss, recv_sem=rs, device_id=dev, device_id_type=MESH
        )

    def loop(lo, hi, body):
        def step(i, carry):
            body(i)
            return carry

        lax.fori_loop(lo, hi, step, 0)

    def m128(v):
        return pl.multiple_of(v, 128)

    loc = [
        pltpu.make_async_copy(x_img, xi, lsem.at[0]),
        pltpu.make_async_copy(x_txt, xt, lsem.at[1]),
        pltpu.make_async_copy(mod_img, mods.at[1], lsem.at[2]),
        pltpu.make_async_copy(mod_txt, mods.at[0], lsem.at[3]),
        pltpu.make_async_copy(
            cot_img.at[:, pl.ds(m128(c * 128), 128)],
            dO.at[pl.ds(pl.multiple_of(z * 512 + c * 256, 256), 256)], lsem.at[4]),
        pltpu.make_async_copy(
            cot_txt.at[:, pl.ds(m128(c * 128), 128)],
            dO.at[pl.ds(pl.multiple_of(2048 + z * 64 + c * 32, 32), 32)], lsem.at[5]),
    ]
    for cp in loc:
        cp.start()

    barrier = pltpu.get_barrier_semaphore()

    def hello(r):
        pl.semaphore_signal(barrier, inc=1, device_id=fdev(r, 1), device_id_type=MESH)
        pl.semaphore_signal(barrier, inc=1, device_id=sdev(r, 1), device_id_type=MESH)

    loop(1, 8, hello)
    pl.semaphore_signal(barrier, inc=1, device_id=pdev, device_id_type=MESH)
    pl.semaphore_signal(barrier, inc=1, device_id=xodev, device_id_type=MESH)

    def w_cols(ref, j, fp):
        return ref.at[j, :, pl.ds(m128((2 * fp + c) * 128), 128)]

    def wl_copy(j):
        return pltpu.make_async_copy(
            w_cols(w_img, j, f), W.at[0, :, pl.ds(j * 128, 128)], wl_sem.at[j])

    def wt_copy(r, j):
        return pltpu.make_async_copy(
            w_cols(w_txt, j, f_at(r, 1)), wt.at[r, :, pl.ds(j * 128, 128)], wtl_sem.at[r, j])

    for j in range(3):
        wl_copy(j).start()

    hz = z % 2
    my_half = pl.ds(pl.multiple_of(hz * 192, 64), 192)

    def w_copy(r, j):
        return remote(
            w_img.at[j, my_half, pl.ds(m128((2 * f_at(r, 1) + c) * 128), 128)],
            W.at[r, my_half, pl.ds(j * 128, 128)],
            w_ss.at[r, j], w_rs.at[r, j], fdev(r, 1))

    def wv_copy(r):
        return remote(
            w_cols(w_img, 2, f_at(r, 1)), W.at[r, :, pl.ds(256, 128)],
            w_ss.at[r, 2], w_rs.at[r, 2], fdev(r, 1))

    def z_copy(j, d, r, half):
        ref = W.at[r, pl.ds(pl.multiple_of(half * 192 + d * 96, 32), 96), pl.ds(j * 128, 128)]
        return remote(ref, ref, z_ss.at[j, d, r], z_rs.at[j, d, r], sdev(1, 1 - 2 * d))

    def start_wt(r):
        for j in range(3):
            wt_copy(r, j).start()

    def pass_w(j):
        def one(r):
            w_copy(r, j).wait_recv()
            for d in (0, 1):
                z_copy(j, d, r, hz).start()

        loop(1, 8, one)

    def start_keys():
        loop(1, 8, lambda r: w_copy(r, 0).wait_send())
        loop(1, 8, lambda r: w_copy(r, 1).start())

    pl.semaphore_wait(barrier, 16)
    loop(1, 8, lambda r: w_copy(r, 0).start())
    loop(0, 8, start_wt)

    img_rows = pl.ds(pl.multiple_of(128 + c * 256, 128), 256)
    txt_rows = pl.ds(pl.multiple_of(c * 32, 32), 32)
    half_rows = pl.ds(pl.multiple_of(c * 256, 256), 256)
    cp_coti = remote(cot_img.at[:, pl.ds(m128(o * 128), 128)],
                     dO.at[pl.ds(pl.multiple_of(z * 512 + c * 256, 256), 256)],
                     p_ss.at[0], p_rs.at[0], pdev)
    cp_cott = remote(cot_txt.at[:, pl.ds(m128(o * 128), 128)],
                     dO.at[pl.ds(pl.multiple_of(2048 + z * 64 + c * 32, 32), 32)],
                     p_ss.at[1], p_rs.at[1], pdev)
    cp_coti.start()
    cp_cott.start()

    for which in (0, 1):
        loc[3 - which].wait()
        row = jnp.broadcast_to(feat[...].astype(F32), (16, 256)).astype(BF)
        mixed[which] = dot(row, mods[which])[:8]
        for b in range(8):
            sc[which, b] = 1.0 + mixed[which, :, 3072 + b * 384:3072 + (b + 1) * 384]

    def z_rows(part, zz):
        if part == 0:
            return pl.ds(pl.multiple_of(zz * 512, 512), 512)
        return pl.ds(pl.multiple_of(2048 + zz * 64, 64), 64)

    def ring_copy(ref, ss, rs, part, b, zz):
        rows = ref.at[z_rows(part, zz)]
        return remote(rows, rows, ss.at[part, b], rs.at[part, b], sdev(b, 1))

    def z_back(b):
        return (z + 4 - b) % 4

    loc[4].wait()
    loc[5].wait()
    cp_coti.wait_recv()
    cp_cott.wait_recv()

    def send_do(b):
        for part in (0, 1):
            ring_copy(dO, do_ss, do_rs, part, b, z).start()

    loop(1, 4, send_do)

    def prepare(which, src, nrm, inv, put):
        rows = 16

        def body(i):
            at = pl.multiple_of(i * rows, rows)
            v = src[pl.ds(at, rows), :].astype(F32)
            cen = v - jnp.mean(v, axis=-1, keepdims=True)
            iv = lax.rsqrt(jnp.mean(cen * cen, axis=-1, keepdims=True) + EPS)
            n = cen * iv
            inv[pl.ds(at, rows), :] = jnp.broadcast_to(iv, (rows, 128))
            h = (n * (1.0 + mixed[which, 0:1, 3072:]) + mixed[which, 0:1, :3072]).astype(BF)
            for b in range(8):
                nrm[b, pl.ds(at, rows), :] = n[:, b * 384:(b + 1) * 384]
                put(b, at, rows, h[:, b * 384:(b + 1) * 384])
            if which == 1:
                pl.when(i == 8)(start_keys)

        loop(0, src.shape[0] // rows, body)

    def put_txt(b, at, rows, h):
        hidt[b, pl.ds(pl.multiple_of(c * 32 + at, 16), rows), :] = h

    def put_img(b, at, rows, h):
        hid[b, pl.ds(pl.multiple_of(c * 256 + at, 16), rows), :] = h

    loc[1].wait()
    prepare(0, xt, ntxt, invt, put_txt)
    cp_ht = remote(hidt.at[:, txt_rows], hidt.at[:, txt_rows], p_ss.at[2], p_rs.at[2], pdev)
    cp_ht.start()
    loc[0].wait()
    prepare(1, xi, nimg, invi, put_img)
    cp_hi = remote(hid.at[:, half_rows], hid.at[:, half_rows], p_ss.at[3], p_rs.at[3], pdev)
    cp_hi.start()

    pass_w(0)
    loop(1, 8, lambda r: w_copy(r, 1).wait_send())
    loop(1, 8, lambda r: wv_copy(r).start())

    cp_ht.wait_recv()

    def t_copy(r):
        return remote(tps.at[r], tpr.at[r], t_ss.at[r], t_rs.at[r], fdev(r, 1))

    def h_copy(r):
        return remote(hidt.at[chip_at(r, 1)], htg.at[r], h_ss.at[r], h_rs.at[r], sdev(r, 1))

    def txt_partial(i):
        r = (i + 1) % 8
        for j in range(3):
            wt_copy(r, j).wait()
        tps[r] = dot(hidt[f], wt[r]).astype(BF)

        @pl.when(r != 0)
        def _():
            t_copy(r).start()

    loop(0, 8, txt_partial)
    pass_w(1)

    def normed_head(lo, hi, col, g):
        a = qkvp[lo:hi, col:col + 128]
        return (a * lax.rsqrt(jnp.mean(a * a, axis=-1, keepdims=True) + EPS)
                * gains[g:g + 1, :]).astype(BF)

    def kv_copy(lo, n, col, wide, at):
        cols = pl.ds(col, wide)
        return remote(kv.at[pl.ds(lo, n), cols], kv.at[pl.ds(lo + 576, n), cols],
                      x_ss.at[at], x_rs.at[at], xdev)

    cp_kvk = kv_copy(0, 512, 0, 128, 0)
    cp_kvv = kv_copy(0, 512, 128, 128, 5)
    cp_kvt = kv_copy(512, 64, 0, 256, 1)

    def send_q(part):
        loop(1, 4, lambda b: ring_copy(qr, q_ss, q_rs, part, b, z).start())

    def project(j):
        lo, hi = j * 128, j * 128 + 128

        def one(r):
            if j == 2:
                wv_copy(r).wait_recv()
            else:
                for d in (0, 1):
                    z_copy(j, d, r, 1 - hz).wait_recv()
            qkvp[128:, lo:hi] += dot(hid[f_at(r, -1)], W[r, :, lo:hi])

        loop(1, 8, one)

    cp_hi.wait_recv()
    for j in range(3):
        wl_copy(j).wait()
    qkvp[128:, :] = dot(hid[f], W[0])
    project(0)
    qr[z_rows(0, z), :] = normed_head(128, 640, 0, 2)
    send_q(0)
    project(1)
    kv[0:512, 0:128] = normed_head(128, 640, 128, 3)
    cp_kvk.start()

    qkvp[0:64, :] = tps[0].astype(F32)

    def txt_add(r):
        t_copy(r).wait_recv()
        qkvp[0:64, :] += tpr[r].astype(F32)

    loop(1, 8, txt_add)
    kv[512:576, 0:128] = normed_head(0, 64, 128, 1)
    kv[512:576, 128:256] = qkvp[0:64, 256:384].astype(BF)
    cp_kvt.start()
    qr[z_rows(1, z), :] = normed_head(0, 64, 0, 0)
    send_q(1)
    project(2)
    kv[0:512, 128:256] = qkvp[128:, 256:384].astype(BF)
    cp_kvv.start()

    def wait_do(b):
        for part in (0, 1):
            ring_copy(dO, do_ss, do_rs, part, b, z_back(b)).wait_recv()

    loop(1, 4, wait_do)
    dOT[...] = dO[...].astype(F32).T.astype(BF)

    def cols_at(i):
        return pl.ds(pl.multiple_of(i * 256, 256), 256)

    def chunk_at(i):
        return ((z + i // 2) % 4) * 2 + i % 2

    def forward(idx):
        cols = cols_at(idx)
        tot = jnp.zeros((1, 256), F32)
        for a in (0, 1):
            e = jnp.exp2(dot(kv[a * 576:a * 576 + 576, 0:128], qT[:, cols]) * EXP2)
            index = chip_at(a * 4, 1) * 64 + lax.broadcasted_iota(jnp.int32, (64, 256), 0)
            et = jnp.where(index < valid[0], e[512:576], 0.0)
            tot += jnp.sum(e[0:512], axis=0, keepdims=True) + jnp.sum(et, axis=0, keepdims=True)
            ets[idx, a * 576:a * 576 + 512, :] = e[0:512].astype(BF)
            ets[idx, a * 576 + 512:a * 576 + 576, :] = et.astype(BF)
        part = dot_tn(kv[:, 128:256], ets[idx])
        stx[0:1, cols] = tot
        stx[1:2, cols] = jnp.sum(dOT[:, cols].astype(F32) * part, axis=0, keepdims=True)

    cp_kvk.wait_recv()
    cp_kvt.wait_recv()
    cp_kvv.wait_recv()

    def forward_img(k):
        b = (4 - k) % 4

        @pl.when(b != 0)
        def _():
            ring_copy(qr, q_ss, q_rs, 0, b, z_back(b)).wait_recv()

        zz = z_back(b)
        rows = z_rows(0, zz)
        qT[:, rows] = qr[rows, :].astype(F32).T.astype(BF)
        loop(0, 2, lambda h: forward(zz * 2 + h))

    loop(0, 4, forward_img)
    loop(1, 4, lambda b: ring_copy(qr, q_ss, q_rs, 1, b, z_back(b)).wait_recv())
    qT[:, 2048:2304] = qr[2048:2304, :].astype(F32).T.astype(BF)
    forward(8)

    def sx_copy(b):
        return remote(stx, stxr.at[b], sx_ss.at[b], sx_rs.at[b], sdev(b, 1))

    loop(1, 4, lambda b: sx_copy(b).start())
    loop(1, 4, lambda b: sx_copy(b).wait_recv())
    sums = stx[...] + stxr[1] + stxr[2] + stxr[3]
    rcp = 1.0 / sums[0:1]
    stf[0:1, :] = rcp
    stf[1:2, :] = sums[1:2] * rcp
    q2[...] = (qT[...].astype(F32) * rcp).T.astype(BF)
    dO2[...] = (dOT[...].astype(F32) * rcp).T.astype(BF)
    htg[0] = hidt[chip]
    loop(1, 8, lambda r: h_copy(r).start())

    def back(a, idx):
        cols = cols_at(idx)
        keys = slice(a * 576, a * 576 + 576)
        dp = dot(kv[keys, 128:256], dOT[:, cols])
        eb = ets[idx, keys, :]
        ds = (eb.astype(F32) * (dp - stf[1:2, cols])).astype(BF)
        part = dot_tn(kv[keys, 0:128], ds)
        if a == 1:
            dqT[:, cols] = part
        else:
            dqT[:, cols] += part
        acc[:, 0:128] += dot(ds, q2[cols, :])
        acc[:, 128:256] += dot(eb, dO2[cols, :])

    acc[...] = jnp.zeros_like(acc)
    loop(0, 9, lambda i: back(1, i))
    dks[:, 0:128] = (acc[:, 0:128] * SCALE).astype(BF)
    dks[:, 128:256] = acc[:, 128:256].astype(BF)
    cp_dk = remote(dks, dkr, x_ss.at[2], x_rs.at[2], xdev)
    cp_dk.start()
    acc[...] = jnp.zeros_like(acc)

    def dq_rows(cols):
        return (dqT[:, cols] * (stf[0:1, cols] * SCALE)).T

    def dq_copy(b):
        return remote(dqs.at[b], dqr.at[b], dq_ss.at[0, b], dq_rs.at[0, b], sdev(b, 1))

    def dqt_copy(b):
        mine = pl.ds(pl.multiple_of(((z + b) % 4) * 64, 64), 64)
        return remote(dqts.at[mine], dqtr.at[b], dq_ss.at[1, b], dq_rs.at[1, b], sdev(b, 1))

    def back_peer(b):
        zz = (z + b) % 4
        loop(0, 2, lambda h: back(0, zz * 2 + h))
        dqs[b] = dq_rows(z_rows(0, zz)).astype(BF)
        dq_copy(b).start()

    loop(1, 4, back_peer)
    back(0, 8)
    dqts[...] = dq_rows(slice(2048, 2304)).astype(BF)
    loop(1, 4, lambda b: dqt_copy(b).start())
    loop(0, 2, lambda h: back(0, z * 2 + h))

    cp_dk.wait_recv()
    acc[:, 0:128] = acc[:, 0:128] * SCALE + dkr[:, 0:128].astype(F32)
    acc[:, 128:256] += dkr[:, 128:256].astype(F32)
    gq[128:, 128:256] = norm_back(
        qkvp[128:, 128:256], gains[3:4, :], acc[0:512, 0:128]).astype(BF)
    gq[128:, 256:384] = acc[0:512, 128:256].astype(BF)
    gq[0:64, 128:256] = norm_back(
        qkvp[0:64, 128:256], gains[1:2, :], acc[512:576, 0:128]).astype(BF)
    gq[0:64, 256:384] = acc[512:576, 128:256].astype(BF)

    dqi = dq_rows(z_rows(0, z))
    own_text = pl.ds(pl.multiple_of(z * 64, 64), 64)
    for b in (1, 2, 3):
        dqt_copy(b).wait_recv()
    dqt = dqts[own_text, :].astype(F32)
    for b in (1, 2, 3):
        dqt = dqt + dqtr[b].astype(F32)
    gq[0:64, 0:128] = norm_back(qkvp[0:64, 0:128], gains[0:1, :], dqt).astype(BF)
    for b in (1, 2, 3):
        dq_copy(b).wait_recv()
        dqi = dqi + dqr[b].astype(F32)
    gq[128:, 0:128] = norm_back(qkvp[128:, 0:128], gains[2:3, :], dqi).astype(BF)

    def gf_copy(r):
        return remote(gtf.at[0], gtf.at[r], gf_ss.at[r], gf_rs.at[r], fdev(r, 1))

    def gs_copy(r):
        return remote(gts.at[0], gts.at[r], gs_ss.at[r], gs_rs.at[r], sdev(r, 1))

    gtf[0] = gq[0:64, :]
    gts[0] = gq[0:64, :]
    loop(1, 8, lambda r: gf_copy(r).start())

    def dw_block(a, b):
        return dot_tn(hid[chip_at(a * 4 + b, 1)], gq[128:, :])

    def rl_copy(d):
        rows = pl.ds(d * 192, 192)
        return remote(dws.at[2, rows], rl.at[0, rows], rl_ss.at[0, d], rl_rs.at[0, d],
                      sdev(1 + 2 * d, 1))

    def dw_copy(r):
        return remote(dws.at[r], dwr.at[r], dw_ss.at[r], dw_rs.at[r], sdev(r % 4, 1))

    dws[6] = dw_block(1, 2).astype(BF)
    cp_rx = remote(dws.at[6], rl.at[1], x_ss.at[7], x_rs.at[7], xdev)
    cp_rx.start()

    other_rows = pl.ds(pl.multiple_of(128 + o * 256, 128), 256)

    def px_copy(r):
        return remote(pxs.at[r], pxr.at[r], ph_ss.at[0, r], ph_rs.at[0, r], pdev)

    def partner_part(i):
        r = (7 - i) % 8
        pxs[r] = dot_nt(gq[other_rows, :], W[r]).astype(BF)
        px_copy(r).start()

    loop(0, 8, partner_part)
    for r in (5, 7):
        dws[r] = dw_block(1, r % 4).astype(BF)
        dw_copy(r).start()

    def ph_copy(r):
        return remote(phs.at[r], phr.at[r], ph_ss.at[1, r], ph_rs.at[1, r], fdev(r % 4, -1))

    s1v[...] = jnp.zeros_like(s1v)
    s2v[...] = jnp.zeros_like(s2v)

    def hidden_part(i):
        r = (7 - i) % 8
        b = f_at(r, -1)
        px_copy(r).wait_recv()
        p = (dot_nt(gq[img_rows, :], W[r]) + pxr[r].astype(F32)).astype(BF)
        phs[r] = p

        @pl.when(r % 4 != 0)
        def _():
            ph_copy(r).start()

        t = p.astype(F32) * sc[1, b, 0:1, :]
        u = t * nimg[b]
        s1v[...] += t[:, 0:128] + t[:, 128:256] + t[:, 256:384]
        s2v[...] += u[:, 0:128] + u[:, 128:256] + u[:, 256:384]

    loop(0, 4, hidden_part)

    thx[...] = jnp.zeros_like(thx)

    def txt_hidden(r):
        @pl.when(r != 0)
        def _():
            gf_copy(r).wait_recv()

        thx[...] += dot_nt(gtf[r], wt[(r // 4) * 4 + (4 - r % 4) % 4])

    loop(0, 8, txt_hidden)
    their = pl.ds(pl.multiple_of(o * 32, 32), 32)
    cp_th = remote(thx.at[their], thr, p_ss.at[4], p_rs.at[4], pdev)
    cp_th.start()

    wx[...] = dw_block(0, 2)
    cp_rx.wait_recv()
    dws[2] = (wx[...] + rl[1].astype(F32)).astype(BF)
    for d in (0, 1):
        rl_copy(d).start()
    loop(1, 8, lambda r: gs_copy(r).start())

    mine = pl.ds(pl.multiple_of(c * 192, 64), 192)
    theirs = pl.ds(pl.multiple_of(o * 192, 64), 192)
    wx[...] = dw_block(1, 0)
    for r in (5, 7):
        dw_copy(r).wait_recv()
        wx[...] += dwr[r].astype(F32)
    wcs[...] = wx[...].astype(BF)
    cp_wc = remote(wcs.at[mine], wcr.at[0], x_ss.at[3], x_rs.at[3], xdev)
    cp_wo = remote(wcs.at[theirs], wcr.at[1], x_ss.at[6], x_rs.at[6], xodev)
    cp_wc.start()
    cp_wo.start()

    cp_th.wait_recv()
    gh = thx[txt_rows, :] + thr[...]
    tsc = gh * sc[0, f, 0:1, :]
    tn = ntxt[f]
    t1 = jnp.sum(tsc, axis=-1, keepdims=True)
    t2 = jnp.sum(tsc * tn, axis=-1, keepdims=True)
    lane_t = lax.broadcasted_iota(jnp.int32, (32, 128), 1)
    tsts[...] = jnp.where(lane_t == 0, t1, t2)

    def ts_copy(r):
        return remote(tsts, tstr.at[r], ts_ss.at[r], ts_rs.at[r], fdev(r, 1))

    loop(1, 8, lambda r: ts_copy(r).start())
    thr[...] = tsc

    loop(5, 8, lambda r: ph_copy(r).wait_send())
    loop(4, 8, hidden_part)
    lane = lax.broadcasted_iota(jnp.int32, (256, 128), 1)
    s1 = jnp.sum(s1v[...], axis=-1, keepdims=True)
    s2 = jnp.sum(s2v[...], axis=-1, keepdims=True)
    sts[...] = jnp.where(lane == 0, s1, s2).T[0:8]

    def st_copy(r):
        return remote(sts, str_.at[r], st_ss.at[r], st_rs.at[r], fdev(r, 1))

    loop(1, 8, lambda r: st_copy(r).start())

    for d in (0, 1):
        r = 1 + 2 * d
        lo, hi = d * 192, d * 192 + 192
        wx[...] = dw_block(0, r)
        rl_copy(d).wait_recv()
        dws[r, 192 - lo:384 - lo, :] = wx[192 - lo:384 - lo, :].astype(BF)
        dws[r, lo:hi, :] = (wx[lo:hi, :] + rl[0, lo:hi, :].astype(F32)).astype(BF)
        dw_copy(r).start()

    hsum = phs[4].astype(F32)
    for r in (5, 6, 7):
        ph_copy(r).wait_recv()
        hsum = hsum + phr[r].astype(F32)
    hcs[...] = hsum.astype(BF)
    cp_hc = remote(hcs, hcr, x_ss.at[4], x_rs.at[4], fdev(4, 1))
    cp_hc.start()
    wx[...] = dw_block(0, 0)

    loop(1, 8, lambda r: gs_copy(r).wait_recv())
    loop(1, 8, lambda r: h_copy(r).wait_recv())
    wxt[...] = dot_tn(htg[...].reshape(512, 384), gts[...].reshape(512, 384))
    cp_wt = remote(wxt.at[theirs], wxtr, p_ss.at[5], p_rs.at[5], pdev)
    cp_wt.start()

    def place(out, part, head):
        for j in range(3):
            out[j, :, pl.ds(m128(head * 128), 128)] = part[:, j * 128:(j + 1) * 128]

    for r in (1, 3):
        dw_copy(r).wait_recv()
        wx[...] += dwr[r].astype(F32)
    cp_wi = remote(wx.at[theirs], wxr, p_ss.at[6], p_rs.at[6], pdev)
    cp_wi.start()

    st = sts[...]
    for r in range(1, 8):
        st_copy(r).wait_recv()
        st = st + str_[r]
    stT = jnp.concatenate([st, jnp.zeros((120, 256), F32)], axis=0).T
    gsum = phs[0].astype(F32)
    for r in (1, 2, 3):
        ph_copy(r).wait_recv()
        gsum = gsum + phr[r].astype(F32)
    cp_hc.wait_recv()
    gsum = gsum + hcr[...].astype(F32)
    scaled = gsum * sc[1, f, 0:1, :]
    dx_img[...] = (invi[:, 0:1] * (
        scaled - stT[:, 0:1] * (1.0 / 3072) - nimg[f] * (stT[:, 1:2] * (1.0 / 3072))
    )).astype(BF)

    tt = tsts[...]
    for r in range(1, 8):
        ts_copy(r).wait_recv()
        tt = tt + tstr[r]
    dx_txt[...] = (invt[:, 0:1] * (
        thr[...] - tt[:, 0:1] * (1.0 / 3072) - ntxt[f] * (tt[:, 1:2] * (1.0 / 3072))
    )).astype(BF)

    cp_wt.wait_recv()
    place(dw_txt, wxt[mine, :], c)
    place(dw_txt, wxtr[...], o)
    cp_wc.wait_recv()
    place(dw_img, wx[mine, :] + wcr[0].astype(F32), c)
    cp_wi.wait_recv()
    cp_wo.wait_recv()
    place(dw_img, wxr[...] + wcr[1].astype(F32), o)

    def drain(r):
        wv_copy(r).wait_send()
        for j in (0, 1):
            for d in (0, 1):
                z_copy(j, d, r, hz).wait_send()
        for cp in (t_copy, h_copy, gf_copy, gs_copy, st_copy, ts_copy):
            cp(r).wait_send()

    def drain_z(b):
        for part in (0, 1):
            ring_copy(dO, do_ss, do_rs, part, b, z).wait_send()
            ring_copy(qr, q_ss, q_rs, part, b, z).wait_send()
        for cp in (sx_copy, dq_copy, dqt_copy):
            cp(b).wait_send()

    loop(1, 8, drain)
    loop(1, 4, drain_z)
    loop(0, 8, lambda r: px_copy(r).wait_send())
    loop(1, 4, lambda r: ph_copy(r).wait_send())
    for d in (0, 1):
        rl_copy(d).wait_send()
    for r in (1, 3, 5, 7):
        dw_copy(r).wait_send()
    for cp in (cp_coti, cp_cott, cp_ht, cp_hi, cp_th, cp_wt, cp_wi, cp_kvk, cp_kvv, cp_kvt,
               cp_dk, cp_rx, cp_wc, cp_wo, cp_hc):
        cp.wait_send()


def finish(a, b, c, d, oa, ob, oc, od):
    oa[...] = a[...]
    ob[...] = b[...]
    oc[...] = c[...]
    od[...] = d[...]


def scratch():
    V = pltpu.VMEM
    return [
        V((256, 3072), BF), V((32, 3072), BF), V((2, 256, 6144), BF), V((2, 8, 6144), F32),
        V((2, 8, 8, 384), F32), V((8, 384, 384), BF), V((8, 384, 384), BF),
        V((8, 512, 384), BF), V((8, 64, 384), BF), V((8, 64, 384), BF),
        V((8, 256, 384), F32), V((8, 32, 384), F32), V((256, 128), F32), V((32, 128), F32),
        V((8, 64, 384), BF), V((8, 64, 384), BF), V((640, 384), F32), V((2304, 128), BF),
        V((2304, 128), BF), V((128, 2304), BF), V((128, 2304), BF), V((2304, 128), BF),
        V((2304, 128), BF),
        V((1152, 256), BF), V((9, 1152, 256), BF), V((576, 256), F32), V((576, 256), BF),
        V((576, 256), BF),
        V((128, 2304), F32), V((2, 2304), F32), V((4, 2, 2304), F32), V((2, 2304), F32),
        V((4, 512, 128), BF), V((4, 512, 128), BF), V((256, 128), BF), V((4, 64, 128), BF),
        V((640, 384), BF),
        V((8, 64, 384), BF), V((8, 64, 384), BF), V((8, 384, 384), BF), V((8, 384, 384), BF),
        V((2, 384, 384), BF),
        V((8, 256, 384), BF), V((8, 256, 384), BF), V((8, 256, 384), BF), V((8, 256, 384), BF),
        V((256, 384), BF), V((256, 384), BF),
        V((256, 128), F32), V((256, 128), F32), V((8, 256), F32), V((8, 8, 256), F32),
        V((64, 384), F32), V((32, 384), F32), V((32, 128), F32), V((8, 32, 128), F32),
        V((384, 384), F32), V((192, 384), F32), V((384, 384), F32), V((192, 384), F32),
        V((384, 384), BF), V((2, 192, 384), BF),
    ] + [
        pltpu.SemaphoreType.DMA(shape)
        for shape in (
            [(6,), (3,), (8, 3), (8, 3), (8, 3), (2, 2, 8), (2, 2, 8), (7,), (7,), (8,), (8,)]
            + [(8,)] * 4 + [(2, 4)] * 6 + [(4,)] * 2 + [(2, 2)] * 2 + [(8,)] * 6
            + [(2, 8)] * 2 + [(8,)] * 4
        )
    ]


def on_device(
    img_tokens, txt_tokens, img_weight, txt_weight, img_modulation, txt_modulation, qk_gains,
    timestep, valid_text, img_cotangent, txt_cotangent,
):
    features = time_features(timestep, img_modulation.shape[0])
    anys = pl.BlockSpec(memory_space=pl.ANY)
    vm = pl.BlockSpec(memory_space=pltpu.VMEM)
    dw_img, dw_txt, dx_img, dx_txt = pl.pallas_call(
        kernel,
        out_shape=(
            jax.ShapeDtypeStruct((3, 192, 256), F32),
            jax.ShapeDtypeStruct((3, 192, 256), F32),
            jax.ShapeDtypeStruct((256, 384), BF),
            jax.ShapeDtypeStruct((32, 384), BF),
        ),
        in_specs=[anys] * 6 + [vm] * 2 + [pl.BlockSpec(memory_space=pltpu.SMEM)] + [anys] * 2,
        out_specs=[vm] * 4,
        scratch_shapes=scratch(),
        compiler_params=pltpu.CompilerParams(
            collective_id=0, has_side_effects=True, vmem_limit_bytes=62 * 2 ** 20),
        name="joint_block",
    )(
        img_tokens, txt_tokens, jnp.transpose(img_weight, (1, 0, 2)),
        jnp.transpose(txt_weight, (1, 0, 2)), img_modulation, txt_modulation, features,
        qk_gains.reshape(4, HD), valid_text, img_cotangent, txt_cotangent,
    )
    shapes = tuple(jax.ShapeDtypeStruct(v.shape, v.dtype) for v in (dw_img, dw_txt, dx_img, dx_txt))
    dw_img, dw_txt, dx_img, dx_txt = pl.pallas_call(
        finish, out_shape=shapes, in_specs=[vm] * 4, out_specs=[vm] * 4, name="results",
    )(dw_img, dw_txt, dx_img, dx_txt)
    return (
        jnp.transpose(dw_img, (1, 0, 2)), jnp.transpose(dw_txt, (1, 0, 2)), dx_img, dx_txt
    )


def solution(mesh):
    return jax.shard_map(
        on_device,
        mesh=mesh,
        in_specs=(
            P("seq", None),
            P("seq", None),
            P("fsdp", None, None),
            P("fsdp", None, None),
            P(),
            P(),
            P(),
            P(),
            P(),
            P("seq", "fsdp"),
            P("seq", "fsdp"),
        ),
        out_specs=(
            P("seq", None, "fsdp"),
            P("seq", None, "fsdp"),
            P("seq", "fsdp"),
            P("seq", "fsdp"),
        ),
        check_vma=False,
    )
```

```python
import functools
import math

import jax
import jax.numpy as jnp
from jax import lax
from jax.experimental import pallas as pl
from jax.experimental.pallas import tpu as pltpu
from jax.sharding import PartitionSpec as P

HD = 128
BF = jnp.bfloat16
F32 = jnp.float32
MESH = pl.DeviceIdType.MESH
SCALE = HD ** (-0.5)
EXP2 = SCALE / math.log(2.0)
EPS = 1e-06


def time_features(timestep, freq_dim):
    half_freq = freq_dim // 2
    frequency = jnp.exp(-math.log(10000.0) * jnp.arange(half_freq, dtype=jnp.float32) / half_freq)
    angles = timestep.astype(jnp.float32)[:, None] * frequency[None, :]
    features = jnp.concatenate([jnp.cos(angles), jnp.sin(angles)], axis=1)
    return jax.nn.silu(features).astype(jnp.bfloat16)


def dot(a, b):
    return jnp.dot(a, b, preferred_element_type=F32)


def dot_nt(a, b):
    return lax.dot_general(a, b, (((1,), (1,)), ((), ())), preferred_element_type=F32)


def dot_tn(a, b):
    return lax.dot_general(a, b, (((0,), (0,)), ((), ())), preferred_element_type=F32)


def norm_back(x, gain, grad):
    r = lax.rsqrt(jnp.mean(x * x, axis=-1, keepdims=True) + EPS)
    gd = gain * grad
    return r * gd - x * (r * r * r * jnp.mean(x * gd, axis=-1, keepdims=True))


def kernel(
    x_img, x_txt, w_img, w_txt, mod_img, mod_txt, feat, gains, valid, cot_img, cot_txt,
    dw_img, dw_txt, dx_img, dx_txt,
    xi, xt, mods, mixed, sc, W, wt, hid, hidt, htg, nimg, ntxt, invi, invt,
    tps, tpr, qkvp, dO, qr, qT, dOT, q2, dO2, kv, ets, acc, dks, dkr,
    dqT, stx, stxr, stf, dqs, dqr, dqts, dqtr, gq, gtf, gts, dws, dwr, rl, pxs, pxr, phs, phr,
    hcs, hcr, s1v, s2v, sts, str_,
    thx, thr, tsts, tstr, wx, wxr, wxt, wxtr, wcs, wcr,
    lsem, wl_sem, wtl_sem, w_ss, w_rs, z_ss, z_rs, p_ss, p_rs, x_ss, x_rs, t_ss, t_rs, h_ss, h_rs,
    do_ss, do_rs, q_ss, q_rs, dq_ss, dq_rs, sx_ss, sx_rs, rl_ss, rl_rs,
    gf_ss, gf_rs, gs_ss, gs_rs, dw_ss, dw_rs, ph_ss, ph_rs, st_ss, st_rs, ts_ss, ts_rs,
):
    s = lax.axis_index("seq")
    f = lax.axis_index("fsdp")
    chip, c = s // 2, s % 2
    xlo, z = chip // 4, chip % 4
    y, xhi = f // 2, f % 2
    o = 1 - c

    def f_at(r, sign):
        return ((y + sign * (r % 4) + 4) % 4) * 2 + (xhi + r // 4) % 2

    def chip_at(r, sign):
        return ((xlo + r // 4) % 2) * 4 + (z + sign * (r % 4) + 4) % 4

    def fdev(r, sign):
        return (s, f_at(r, sign))

    def sdev(r, sign):
        return (chip_at(r, sign) * 2 + c, f)

    pdev = (chip * 2 + o, f)
    xdev = sdev(4, 1)
    xo = 1 - xlo
    xodev = ((xo * 4 + z) * 2 + o, f)

    def remote(src, dst, ss, rs, dev):
        return pltpu.make_async_remote_copy(
            src_ref=src, dst_ref=dst, send_sem=ss, recv_sem=rs, device_id=dev, device_id_type=MESH
        )

    def loop(lo, hi, body):
        def step(i, carry):
            body(i)
            return carry

        lax.fori_loop(lo, hi, step, 0)

    def m128(v):
        return pl.multiple_of(v, 128)

    loc = [
        pltpu.make_async_copy(x_img, xi, lsem.at[0]),
        pltpu.make_async_copy(x_txt, xt, lsem.at[1]),
        pltpu.make_async_copy(mod_img, mods.at[1], lsem.at[2]),
        pltpu.make_async_copy(mod_txt, mods.at[0], lsem.at[3]),
        pltpu.make_async_copy(
            cot_img.at[:, pl.ds(m128(c * 128), 128)],
            dO.at[pl.ds(pl.multiple_of(z * 512 + c * 256, 256), 256)], lsem.at[4]),
        pltpu.make_async_copy(
            cot_txt.at[:, pl.ds(m128(c * 128), 128)],
            dO.at[pl.ds(pl.multiple_of(2048 + z * 64 + c * 32, 32), 32)], lsem.at[5]),
    ]
    for cp in loc:
        cp.start()

    barrier = pltpu.get_barrier_semaphore()

    def hello(r):
        pl.semaphore_signal(barrier, inc=1, device_id=fdev(r, 1), device_id_type=MESH)
        pl.semaphore_signal(barrier, inc=1, device_id=sdev(r, 1), device_id_type=MESH)

    loop(1, 8, hello)
    pl.semaphore_signal(barrier, inc=1, device_id=pdev, device_id_type=MESH)
    pl.semaphore_signal(barrier, inc=1, device_id=xodev, device_id_type=MESH)

    def w_cols(ref, j, fp):
        return ref.at[j, :, pl.ds(m128((2 * fp + c) * 128), 128)]

    def wl_copy(j):
        return pltpu.make_async_copy(
            w_cols(w_img, j, f), W.at[0, :, pl.ds(j * 128, 128)], wl_sem.at[j])

    def wt_copy(r, j):
        return pltpu.make_async_copy(
            w_cols(w_txt, j, f_at(r, 1)), wt.at[r, :, pl.ds(j * 128, 128)], wtl_sem.at[r, j])

    for j in range(3):
        wl_copy(j).start()

    hz = z % 2
    my_half = pl.ds(pl.multiple_of(hz * 192, 64), 192)

    def w_copy(r, j):
        return remote(
            w_img.at[j, my_half, pl.ds(m128((2 * f_at(r, 1) + c) * 128), 128)],
            W.at[r, my_half, pl.ds(j * 128, 128)],
            w_ss.at[r, j], w_rs.at[r, j], fdev(r, 1))

    def wv_copy(r):
        return remote(
            w_cols(w_img, 2, f_at(r, 1)), W.at[r, :, pl.ds(256, 128)],
            w_ss.at[r, 2], w_rs.at[r, 2], fdev(r, 1))

    def z_copy(j, d, r, half):
        ref = W.at[r, pl.ds(pl.multiple_of(half * 192 + d * 96, 32), 96), pl.ds(j * 128, 128)]
        return remote(ref, ref, z_ss.at[j, d, r], z_rs.at[j, d, r], sdev(1, 1 - 2 * d))

    def start_wt(r):
        for j in range(3):
            wt_copy(r, j).start()

    def pass_w(j):
        def one(r):
            w_copy(r, j).wait_recv()
            for d in (0, 1):
                z_copy(j, d, r, hz).start()

        loop(1, 8, one)

    def start_keys():
        loop(1, 8, lambda r: w_copy(r, 1).start())

    def start_values():
        loop(1, 8, lambda r: wv_copy(r).start())

    pl.semaphore_wait(barrier, 16)
    loop(1, 8, lambda r: w_copy(r, 0).start())
    start_keys()
    loop(0, 8, start_wt)

    img_rows = pl.ds(pl.multiple_of(128 + c * 256, 128), 256)
    txt_rows = pl.ds(pl.multiple_of(c * 32, 32), 32)
    half_rows = pl.ds(pl.multiple_of(c * 256, 256), 256)
    cp_coti = remote(cot_img.at[:, pl.ds(m128(o * 128), 128)],
                     dO.at[pl.ds(pl.multiple_of(z * 512 + c * 256, 256), 256)],
                     p_ss.at[0], p_rs.at[0], pdev)
    cp_cott = remote(cot_txt.at[:, pl.ds(m128(o * 128), 128)],
                     dO.at[pl.ds(pl.multiple_of(2048 + z * 64 + c * 32, 32), 32)],
                     p_ss.at[1], p_rs.at[1], pdev)
    cp_coti.start()
    cp_cott.start()

    for which in (0, 1):
        loc[3 - which].wait()
        row = jnp.broadcast_to(feat[...].astype(F32), (16, 256)).astype(BF)
        mixed[which] = dot(row, mods[which])[:8]
        for b in range(8):
            sc[which, b] = 1.0 + mixed[which, :, 3072 + b * 384:3072 + (b + 1) * 384]

    def z_rows(part, zz):
        if part == 0:
            return pl.ds(pl.multiple_of(zz * 512, 512), 512)
        return pl.ds(pl.multiple_of(2048 + zz * 64, 64), 64)

    def ring_copy(ref, ss, rs, part, b, zz):
        rows = ref.at[z_rows(part, zz)]
        return remote(rows, rows, ss.at[part, b], rs.at[part, b], sdev(b, 1))

    def z_back(b):
        return (z + 4 - b) % 4

    loc[4].wait()
    loc[5].wait()
    cp_coti.wait_recv()
    cp_cott.wait_recv()

    def send_do(b):
        for part in (0, 1):
            ring_copy(dO, do_ss, do_rs, part, b, z).start()

    loop(1, 4, send_do)

    def prepare(which, src, nrm, inv, put):
        rows = 16

        def body(i):
            at = pl.multiple_of(i * rows, rows)
            v = src[pl.ds(at, rows), :].astype(F32)
            cen = v - jnp.mean(v, axis=-1, keepdims=True)
            iv = lax.rsqrt(jnp.mean(cen * cen, axis=-1, keepdims=True) + EPS)
            n = cen * iv
            inv[pl.ds(at, rows), :] = jnp.broadcast_to(iv, (rows, 128))
            h = (n * (1.0 + mixed[which, 0:1, 3072:]) + mixed[which, 0:1, :3072]).astype(BF)
            for b in range(8):
                nrm[b, pl.ds(at, rows), :] = n[:, b * 384:(b + 1) * 384]
                put(b, at, rows, h[:, b * 384:(b + 1) * 384])
            if which == 1:
                pl.when(i == 4)(start_values)

        loop(0, src.shape[0] // rows, body)

    def put_txt(b, at, rows, h):
        hidt[b, pl.ds(pl.multiple_of(c * 32 + at, 16), rows), :] = h

    def put_img(b, at, rows, h):
        hid[b, pl.ds(pl.multiple_of(c * 256 + at, 16), rows), :] = h

    loc[1].wait()
    prepare(0, xt, ntxt, invt, put_txt)
    cp_ht = remote(hidt.at[:, txt_rows], hidt.at[:, txt_rows], p_ss.at[2], p_rs.at[2], pdev)
    cp_ht.start()
    cp_ht.wait_recv()

    def t_copy(r):
        return remote(tps.at[r], tpr.at[r], t_ss.at[r], t_rs.at[r], fdev(r, 1))

    def h_copy(r):
        return remote(hidt.at[chip_at(r, 1)], htg.at[r], h_ss.at[r], h_rs.at[r], sdev(r, 1))

    def txt_partial(i):
        r = (i + 1) % 8
        for j in range(3):
            wt_copy(r, j).wait()
        tps[r] = dot(hidt[f], wt[r]).astype(BF)

        @pl.when(r != 0)
        def _():
            t_copy(r).start()

    loop(0, 8, txt_partial)
    loc[0].wait()
    prepare(1, xi, nimg, invi, put_img)
    cp_hi = remote(hid.at[:, half_rows], hid.at[:, half_rows], p_ss.at[3], p_rs.at[3], pdev)
    cp_hi.start()

    pass_w(0)

    pass_w(1)

    def normed_head(lo, hi, col, g):
        a = qkvp[lo:hi, col:col + 128]
        return (a * lax.rsqrt(jnp.mean(a * a, axis=-1, keepdims=True) + EPS)
                * gains[g:g + 1, :]).astype(BF)

    def kv_copy(lo, n, col, wide, at):
        cols = pl.ds(col, wide)
        return remote(kv.at[pl.ds(lo, n), cols], kv.at[pl.ds(lo + 576, n), cols],
                      x_ss.at[at], x_rs.at[at], xdev)

    cp_kvk = kv_copy(0, 512, 0, 128, 0)
    cp_kvv = kv_copy(0, 512, 128, 128, 5)
    cp_kvt = kv_copy(512, 64, 0, 256, 1)

    def send_q(part):
        loop(1, 4, lambda b: ring_copy(qr, q_ss, q_rs, part, b, z).start())

    def project(j):
        lo, hi = j * 128, j * 128 + 128

        def one(r):
            if j == 2:
                wv_copy(r).wait_recv()
            else:
                for d in (0, 1):
                    z_copy(j, d, r, 1 - hz).wait_recv()
            qkvp[128:, lo:hi] += dot(hid[f_at(r, -1)], W[r, :, lo:hi])

        loop(1, 8, one)

    cp_hi.wait_recv()
    for j in range(3):
        wl_copy(j).wait()
    qkvp[128:, :] = dot(hid[f], W[0])
    project(0)
    qr[z_rows(0, z), :] = normed_head(128, 640, 0, 2)
    send_q(0)
    project(1)
    kv[0:512, 0:128] = normed_head(128, 640, 128, 3)
    cp_kvk.start()

    qkvp[0:64, :] = tps[0].astype(F32)

    def txt_add(r):
        t_copy(r).wait_recv()
        qkvp[0:64, :] += tpr[r].astype(F32)

    loop(1, 8, txt_add)
    kv[512:576, 0:128] = normed_head(0, 64, 128, 1)
    kv[512:576, 128:256] = qkvp[0:64, 256:384].astype(BF)
    cp_kvt.start()
    qr[z_rows(1, z), :] = normed_head(0, 64, 0, 0)
    send_q(1)
    project(2)
    kv[0:512, 128:256] = qkvp[128:, 256:384].astype(BF)
    cp_kvv.start()

    def wait_do(b):
        for part in (0, 1):
            ring_copy(dO, do_ss, do_rs, part, b, z_back(b)).wait_recv()

    loop(1, 4, wait_do)
    dOT[...] = dO[...].astype(F32).T.astype(BF)

    def cols_at(i):
        return pl.ds(pl.multiple_of(i * 256, 256), 256)

    def chunk_at(i):
        return ((z + i // 2) % 4) * 2 + i % 2

    def forward(idx):
        cols = cols_at(idx)
        tot = jnp.zeros((1, 256), F32)
        for a in (0, 1):
            e = jnp.exp2(dot(kv[a * 576:a * 576 + 576, 0:128], qT[:, cols]) * EXP2)
            index = chip_at(a * 4, 1) * 64 + lax.broadcasted_iota(jnp.int32, (64, 256), 0)
            et = jnp.where(index < valid[0], e[512:576], 0.0)
            tot += jnp.sum(e[0:512], axis=0, keepdims=True) + jnp.sum(et, axis=0, keepdims=True)
            ets[idx, a * 576:a * 576 + 512, :] = e[0:512].astype(BF)
            ets[idx, a * 576 + 512:a * 576 + 576, :] = et.astype(BF)
        part = dot_tn(kv[:, 128:256], ets[idx])
        stx[0:1, cols] = tot
        stx[1:2, cols] = jnp.sum(dOT[:, cols].astype(F32) * part, axis=0, keepdims=True)

    cp_kvk.wait_recv()
    cp_kvt.wait_recv()
    cp_kvv.wait_recv()

    def forward_img(k):
        b = (4 - k) % 4

        @pl.when(b != 0)
        def _():
            ring_copy(qr, q_ss, q_rs, 0, b, z_back(b)).wait_recv()

        zz = z_back(b)
        rows = z_rows(0, zz)
        qT[:, rows] = qr[rows, :].astype(F32).T.astype(BF)
        loop(0, 2, lambda h: forward(zz * 2 + h))

    loop(0, 4, forward_img)
    loop(1, 4, lambda b: ring_copy(qr, q_ss, q_rs, 1, b, z_back(b)).wait_recv())
    qT[:, 2048:2304] = qr[2048:2304, :].astype(F32).T.astype(BF)
    forward(8)

    def sx_copy(b):
        return remote(stx, stxr.at[b], sx_ss.at[b], sx_rs.at[b], sdev(b, 1))

    loop(1, 4, lambda b: sx_copy(b).start())
    loop(1, 4, lambda b: sx_copy(b).wait_recv())
    sums = stx[...] + stxr[1] + stxr[2] + stxr[3]
    rcp = 1.0 / sums[0:1]
    stf[0:1, :] = rcp
    stf[1:2, :] = sums[1:2] * rcp
    q2[...] = (qT[...].astype(F32) * rcp).T.astype(BF)
    dO2[...] = (dOT[...].astype(F32) * rcp).T.astype(BF)
    htg[0] = hidt[chip]
    loop(1, 8, lambda r: h_copy(r).start())

    def back(a, idx):
        cols = cols_at(idx)
        keys = slice(a * 576, a * 576 + 576)
        dp = dot(kv[keys, 128:256], dOT[:, cols])
        eb = ets[idx, keys, :]
        ds = (eb.astype(F32) * (dp - stf[1:2, cols])).astype(BF)
        part = dot_tn(kv[keys, 0:128], ds)
        if a == 1:
            dqT[:, cols] = part
        else:
            dqT[:, cols] += part
        acc[:, 0:128] += dot(ds, q2[cols, :])
        acc[:, 128:256] += dot(eb, dO2[cols, :])

    acc[...] = jnp.zeros_like(acc)
    loop(0, 9, lambda i: back(1, i))
    dks[:, 0:128] = (acc[:, 0:128] * SCALE).astype(BF)
    dks[:, 128:256] = acc[:, 128:256].astype(BF)
    cp_dk = remote(dks, dkr, x_ss.at[2], x_rs.at[2], xdev)
    cp_dk.start()
    acc[...] = jnp.zeros_like(acc)

    def dq_rows(cols):
        return (dqT[:, cols] * (stf[0:1, cols] * SCALE)).T

    def dq_copy(b):
        return remote(dqs.at[b], dqr.at[b], dq_ss.at[0, b], dq_rs.at[0, b], sdev(b, 1))

    def dqt_copy(b):
        mine = pl.ds(pl.multiple_of(((z + b) % 4) * 64, 64), 64)
        return remote(dqts.at[mine], dqtr.at[b], dq_ss.at[1, b], dq_rs.at[1, b], sdev(b, 1))

    def back_peer(b):
        zz = (z + b) % 4
        loop(0, 2, lambda h: back(0, zz * 2 + h))
        dqs[b] = dq_rows(z_rows(0, zz)).astype(BF)
        dq_copy(b).start()

    loop(1, 4, back_peer)
    back(0, 8)
    dqts[...] = dq_rows(slice(2048, 2304)).astype(BF)
    loop(1, 4, lambda b: dqt_copy(b).start())
    loop(0, 2, lambda h: back(0, z * 2 + h))

    cp_dk.wait_recv()
    acc[:, 0:128] = acc[:, 0:128] * SCALE + dkr[:, 0:128].astype(F32)
    acc[:, 128:256] += dkr[:, 128:256].astype(F32)
    gq[128:, 128:256] = norm_back(
        qkvp[128:, 128:256], gains[3:4, :], acc[0:512, 0:128]).astype(BF)
    gq[128:, 256:384] = acc[0:512, 128:256].astype(BF)
    gq[0:64, 128:256] = norm_back(
        qkvp[0:64, 128:256], gains[1:2, :], acc[512:576, 0:128]).astype(BF)
    gq[0:64, 256:384] = acc[512:576, 128:256].astype(BF)

    dqi = dq_rows(z_rows(0, z))
    own_text = pl.ds(pl.multiple_of(z * 64, 64), 64)
    for b in (1, 2, 3):
        dqt_copy(b).wait_recv()
    dqt = dqts[own_text, :].astype(F32)
    for b in (1, 2, 3):
        dqt = dqt + dqtr[b].astype(F32)
    gq[0:64, 0:128] = norm_back(qkvp[0:64, 0:128], gains[0:1, :], dqt).astype(BF)
    for b in (1, 2, 3):
        dq_copy(b).wait_recv()
        dqi = dqi + dqr[b].astype(F32)
    gq[128:, 0:128] = norm_back(qkvp[128:, 0:128], gains[2:3, :], dqi).astype(BF)

    def gf_copy(r):
        return remote(gtf.at[0], gtf.at[r], gf_ss.at[r], gf_rs.at[r], fdev(r, 1))

    def gs_copy(r):
        return remote(gts.at[0], gts.at[r], gs_ss.at[r], gs_rs.at[r], sdev(r, 1))

    gtf[0] = gq[0:64, :]
    gts[0] = gq[0:64, :]
    loop(1, 8, lambda r: gf_copy(r).start())

    def dw_block(a, b):
        return dot_tn(hid[chip_at(a * 4 + b, 1)], gq[128:, :])

    def rl_copy(d):
        rows = pl.ds(d * 192, 192)
        return remote(dws.at[2, rows], rl.at[0, rows], rl_ss.at[0, d], rl_rs.at[0, d],
                      sdev(1 + 2 * d, 1))

    def dw_copy(r):
        return remote(dws.at[r], dwr.at[r], dw_ss.at[r], dw_rs.at[r], sdev(r % 4, 1))

    dws[6] = dw_block(1, 2).astype(BF)
    cp_rx = remote(dws.at[6], rl.at[1], x_ss.at[7], x_rs.at[7], xdev)
    cp_rx.start()

    other_rows = pl.ds(pl.multiple_of(128 + o * 256, 128), 256)

    def px_copy(r):
        return remote(pxs.at[r], pxr.at[r], ph_ss.at[0, r], ph_rs.at[0, r], pdev)

    def partner_part(i):
        r = (7 - i) % 8
        pxs[r] = dot_nt(gq[other_rows, :], W[r]).astype(BF)
        px_copy(r).start()

    loop(0, 8, partner_part)
    for r in (5, 7):
        dws[r] = dw_block(1, r % 4).astype(BF)
        dw_copy(r).start()

    def ph_copy(r):
        return remote(phs.at[r], phr.at[r], ph_ss.at[1, r], ph_rs.at[1, r], fdev(r % 4, -1))

    s1v[...] = jnp.zeros_like(s1v)
    s2v[...] = jnp.zeros_like(s2v)

    def hidden_part(i):
        r = (7 - i) % 8
        b = f_at(r, -1)
        px_copy(r).wait_recv()
        p = (dot_nt(gq[img_rows, :], W[r]) + pxr[r].astype(F32)).astype(BF)
        phs[r] = p

        @pl.when(r % 4 != 0)
        def _():
            ph_copy(r).start()

        t = p.astype(F32) * sc[1, b, 0:1, :]
        u = t * nimg[b]
        s1v[...] += t[:, 0:128] + t[:, 128:256] + t[:, 256:384]
        s2v[...] += u[:, 0:128] + u[:, 128:256] + u[:, 256:384]

    loop(0, 4, hidden_part)

    thx[...] = jnp.zeros_like(thx)

    def txt_hidden(r):
        @pl.when(r != 0)
        def _():
            gf_copy(r).wait_recv()

        thx[...] += dot_nt(gtf[r], wt[(r // 4) * 4 + (4 - r % 4) % 4])

    loop(0, 8, txt_hidden)
    their = pl.ds(pl.multiple_of(o * 32, 32), 32)
    cp_th = remote(thx.at[their], thr, p_ss.at[4], p_rs.at[4], pdev)
    cp_th.start()

    wx[...] = dw_block(0, 2)
    cp_rx.wait_recv()
    dws[2] = (wx[...] + rl[1].astype(F32)).astype(BF)
    for d in (0, 1):
        rl_copy(d).start()
    loop(1, 8, lambda r: gs_copy(r).start())

    mine = pl.ds(pl.multiple_of(c * 192, 64), 192)
    theirs = pl.ds(pl.multiple_of(o * 192, 64), 192)
    wx[...] = dw_block(1, 0)
    for r in (5, 7):
        dw_copy(r).wait_recv()
        wx[...] += dwr[r].astype(F32)
    wcs[...] = wx[...].astype(BF)
    cp_wc = remote(wcs.at[mine], wcr.at[0], x_ss.at[3], x_rs.at[3], xdev)
    cp_wo = remote(wcs.at[theirs], wcr.at[1], x_ss.at[6], x_rs.at[6], xodev)
    cp_wc.start()
    cp_wo.start()

    cp_th.wait_recv()
    gh = thx[txt_rows, :] + thr[...]
    tsc = gh * sc[0, f, 0:1, :]
    tn = ntxt[f]
    t1 = jnp.sum(tsc, axis=-1, keepdims=True)
    t2 = jnp.sum(tsc * tn, axis=-1, keepdims=True)
    lane_t = lax.broadcasted_iota(jnp.int32, (32, 128), 1)
    tsts[...] = jnp.where(lane_t == 0, t1, t2)

    def ts_copy(r):
        return remote(tsts, tstr.at[r], ts_ss.at[r], ts_rs.at[r], fdev(r, 1))

    loop(1, 8, lambda r: ts_copy(r).start())
    thr[...] = tsc

    loop(5, 8, lambda r: ph_copy(r).wait_send())
    loop(4, 8, hidden_part)
    lane = lax.broadcasted_iota(jnp.int32, (256, 128), 1)
    s1 = jnp.sum(s1v[...], axis=-1, keepdims=True)
    s2 = jnp.sum(s2v[...], axis=-1, keepdims=True)
    sts[...] = jnp.where(lane == 0, s1, s2).T[0:8]

    def st_copy(r):
        return remote(sts, str_.at[r], st_ss.at[r], st_rs.at[r], fdev(r, 1))

    loop(1, 8, lambda r: st_copy(r).start())

    for d in (0, 1):
        r = 1 + 2 * d
        lo, hi = d * 192, d * 192 + 192
        wx[...] = dw_block(0, r)
        rl_copy(d).wait_recv()
        dws[r, 192 - lo:384 - lo, :] = wx[192 - lo:384 - lo, :].astype(BF)
        dws[r, lo:hi, :] = (wx[lo:hi, :] + rl[0, lo:hi, :].astype(F32)).astype(BF)
        dw_copy(r).start()

    hsum = phs[4].astype(F32)
    for r in (5, 6, 7):
        ph_copy(r).wait_recv()
        hsum = hsum + phr[r].astype(F32)
    hcs[...] = hsum.astype(BF)
    cp_hc = remote(hcs, hcr, x_ss.at[4], x_rs.at[4], fdev(4, 1))
    cp_hc.start()
    wx[...] = dw_block(0, 0)

    loop(1, 8, lambda r: gs_copy(r).wait_recv())
    loop(1, 8, lambda r: h_copy(r).wait_recv())
    wxt[...] = dot_tn(htg[...].reshape(512, 384), gts[...].reshape(512, 384))
    cp_wt = remote(wxt.at[theirs], wxtr, p_ss.at[5], p_rs.at[5], pdev)
    cp_wt.start()

    def place(out, part, head):
        for j in range(3):
            out[j, :, pl.ds(m128(head * 128), 128)] = part[:, j * 128:(j + 1) * 128]

    for r in (1, 3):
        dw_copy(r).wait_recv()
        wx[...] += dwr[r].astype(F32)
    cp_wi = remote(wx.at[theirs], wxr, p_ss.at[6], p_rs.at[6], pdev)
    cp_wi.start()

    st = sts[...]
    for r in range(1, 8):
        st_copy(r).wait_recv()
        st = st + str_[r]
    stT = jnp.concatenate([st, jnp.zeros((120, 256), F32)], axis=0).T
    gsum = phs[0].astype(F32)
    for r in (1, 2, 3):
        ph_copy(r).wait_recv()
        gsum = gsum + phr[r].astype(F32)
    cp_hc.wait_recv()
    gsum = gsum + hcr[...].astype(F32)
    scaled = gsum * sc[1, f, 0:1, :]
    dx_img[...] = (invi[:, 0:1] * (
        scaled - stT[:, 0:1] * (1.0 / 3072) - nimg[f] * (stT[:, 1:2] * (1.0 / 3072))
    )).astype(BF)

    tt = tsts[...]
    for r in range(1, 8):
        ts_copy(r).wait_recv()
        tt = tt + tstr[r]
    dx_txt[...] = (invt[:, 0:1] * (
        thr[...] - tt[:, 0:1] * (1.0 / 3072) - ntxt[f] * (tt[:, 1:2] * (1.0 / 3072))
    )).astype(BF)

    cp_wt.wait_recv()
    place(dw_txt, wxt[mine, :], c)
    place(dw_txt, wxtr[...], o)
    cp_wc.wait_recv()
    place(dw_img, wx[mine, :] + wcr[0].astype(F32), c)
    cp_wi.wait_recv()
    cp_wo.wait_recv()
    place(dw_img, wxr[...] + wcr[1].astype(F32), o)

    def drain(r):
        wv_copy(r).wait_send()
        w_copy(r, 0).wait_send()
        w_copy(r, 1).wait_send()
        for j in (0, 1):
            for d in (0, 1):
                z_copy(j, d, r, hz).wait_send()
        for cp in (t_copy, h_copy, gf_copy, gs_copy, st_copy, ts_copy):
            cp(r).wait_send()

    def drain_z(b):
        for part in (0, 1):
            ring_copy(dO, do_ss, do_rs, part, b, z).wait_send()
            ring_copy(qr, q_ss, q_rs, part, b, z).wait_send()
        for cp in (sx_copy, dq_copy, dqt_copy):
            cp(b).wait_send()

    loop(1, 8, drain)
    loop(1, 4, drain_z)
    loop(0, 8, lambda r: px_copy(r).wait_send())
    loop(1, 4, lambda r: ph_copy(r).wait_send())
    for d in (0, 1):
        rl_copy(d).wait_send()
    for r in (1, 3, 5, 7):
        dw_copy(r).wait_send()
    for cp in (cp_coti, cp_cott, cp_ht, cp_hi, cp_th, cp_wt, cp_wi, cp_kvk, cp_kvv, cp_kvt,
               cp_dk, cp_rx, cp_wc, cp_wo, cp_hc):
        cp.wait_send()


def finish(*refs):
    ins, outs, bufs, isem, osem = refs[0:4], refs[4:8], refs[8:12], refs[12], refs[13]
    fetch = [pltpu.make_async_copy(ins[i], bufs[i], isem.at[i]) for i in range(4)]
    store = [pltpu.make_async_copy(bufs[i], outs[i], osem.at[i]) for i in range(4)]
    for cp in fetch:
        cp.start()
    for i in range(4):
        fetch[i].wait()
        store[i].start()
    for cp in store:
        cp.wait()


def scratch():
    V = pltpu.VMEM
    return [
        V((256, 3072), BF), V((32, 3072), BF), V((2, 256, 6144), BF), V((2, 8, 6144), F32),
        V((2, 8, 8, 384), F32), V((8, 384, 384), BF), V((8, 384, 384), BF),
        V((8, 512, 384), BF), V((8, 64, 384), BF), V((8, 64, 384), BF),
        V((8, 256, 384), F32), V((8, 32, 384), F32), V((256, 128), F32), V((32, 128), F32),
        V((8, 64, 384), BF), V((8, 64, 384), BF), V((640, 384), F32), V((2304, 128), BF),
        V((2304, 128), BF), V((128, 2304), BF), V((128, 2304), BF), V((2304, 128), BF),
        V((2304, 128), BF),
        V((1152, 256), BF), V((9, 1152, 256), BF), V((576, 256), F32), V((576, 256), BF),
        V((576, 256), BF),
        V((128, 2304), F32), V((2, 2304), F32), V((4, 2, 2304), F32), V((2, 2304), F32),
        V((4, 512, 128), BF), V((4, 512, 128), BF), V((256, 128), BF), V((4, 64, 128), BF),
        V((640, 384), BF),
        V((8, 64, 384), BF), V((8, 64, 384), BF), V((8, 384, 384), BF), V((8, 384, 384), BF),
        V((2, 384, 384), BF),
        V((8, 256, 384), BF), V((8, 256, 384), BF), V((8, 256, 384), BF), V((8, 256, 384), BF),
        V((256, 384), BF), V((256, 384), BF),
        V((256, 128), F32), V((256, 128), F32), V((8, 256), F32), V((8, 8, 256), F32),
        V((64, 384), F32), V((32, 384), F32), V((32, 128), F32), V((8, 32, 128), F32),
        V((384, 384), F32), V((192, 384), F32), V((384, 384), F32), V((192, 384), F32),
        V((384, 384), BF), V((2, 192, 384), BF),
    ] + [
        pltpu.SemaphoreType.DMA(shape)
        for shape in (
            [(6,), (3,), (8, 3), (8, 3), (8, 3), (2, 2, 8), (2, 2, 8), (7,), (7,), (8,), (8,)]
            + [(8,)] * 4 + [(2, 4)] * 6 + [(4,)] * 2 + [(2, 2)] * 2 + [(8,)] * 6
            + [(2, 8)] * 2 + [(8,)] * 4
        )
    ]


def on_device(
    img_tokens, txt_tokens, img_weight, txt_weight, img_modulation, txt_modulation, qk_gains,
    timestep, valid_text, img_cotangent, txt_cotangent,
):
    features = time_features(timestep, img_modulation.shape[0])
    anys = pl.BlockSpec(memory_space=pl.ANY)
    vm = pl.BlockSpec(memory_space=pltpu.VMEM)
    dw_img, dw_txt, dx_img, dx_txt = pl.pallas_call(
        kernel,
        out_shape=(
            jax.ShapeDtypeStruct((3, 192, 256), F32),
            jax.ShapeDtypeStruct((3, 192, 256), F32),
            jax.ShapeDtypeStruct((256, 384), BF),
            jax.ShapeDtypeStruct((32, 384), BF),
        ),
        in_specs=[anys] * 6 + [vm] * 2 + [pl.BlockSpec(memory_space=pltpu.SMEM)] + [anys] * 2,
        out_specs=[vm] * 4,
        scratch_shapes=scratch(),
        compiler_params=pltpu.CompilerParams(
            collective_id=0, has_side_effects=True, vmem_limit_bytes=62 * 2 ** 20),
        name="joint_block",
    )(
        img_tokens, txt_tokens, jnp.transpose(img_weight, (1, 0, 2)),
        jnp.transpose(txt_weight, (1, 0, 2)), img_modulation, txt_modulation, features,
        qk_gains.reshape(4, HD), valid_text, img_cotangent, txt_cotangent,
    )
    shapes = tuple(jax.ShapeDtypeStruct(v.shape, v.dtype) for v in (dw_img, dw_txt, dx_img, dx_txt))
    dw_img, dw_txt, dx_img, dx_txt = pl.pallas_call(
        finish, out_shape=shapes, in_specs=[anys] * 4, out_specs=[anys] * 4, name="results",
        scratch_shapes=[pltpu.VMEM(v.shape, v.dtype) for v in shapes]
        + [pltpu.SemaphoreType.DMA((4,))] * 2,
    )(dw_img, dw_txt, dx_img, dx_txt)
    return (
        jnp.transpose(dw_img, (1, 0, 2)), jnp.transpose(dw_txt, (1, 0, 2)), dx_img, dx_txt
    )


def solution(mesh):
    return jax.shard_map(
        on_device,
        mesh=mesh,
        in_specs=(
            P("seq", None),
            P("seq", None),
            P("fsdp", None, None),
            P("fsdp", None, None),
            P(),
            P(),
            P(),
            P(),
            P(),
            P("seq", "fsdp"),
            P("seq", "fsdp"),
        ),
        out_specs=(
            P("seq", None, "fsdp"),
            P("seq", None, "fsdp"),
            P("seq", "fsdp"),
            P("seq", "fsdp"),
        ),
        check_vma=False,
    )
```
